32 devices in a mesh: frame: 8 (over z, core), row: 4 (over y, x).
Axes of the slice: x: 2, y: 2, z: 4, core: 2. Of those that a mesh axis runs over, the one named last changes fastest.
Arguments:
- tokens: bfloat16 [16, 8, 16, 16, 1024], P('frame', None, 'row'), may hold values from -6 to 6
- cotangent: bfloat16 [16, 8, 16, 16, 1024], P('frame', None, 'row'), may hold values from -6 to 6
- noise_levels: int32 [16, 8], P('frame'), may hold values from 0 to 1023
- frame_times: int32 [16, 8], P('frame'), may hold values from 0 to 23, as said below
- step_count: int32 [1], replicated, may hold values from 1 to 20
- qkv_master: float32 [1024, 3072], P(None, ('frame', 'row')), may hold values from -0.25 to 0.25
- qkv_momentum: float32 [1024, 3072], P(None, ('frame', 'row')), may hold values from -0.0012207031 to 0.0012207031
- out_master: float32 [1024, 1024], P(('frame', 'row')), may hold values from -1.25 to 1.25
- out_momentum: float32 [1024, 1024], P(('frame', 'row')), may hold values from -0.0012207031 to 0.0012207031
- up_master: float32 [1024, 4096], P(None, ('frame', 'row')), may hold values from -0.253125 to 0.253125
- up_momentum: float32 [1024, 4096], P(None, ('frame', 'row')), may hold values from -0.0012207031 to 0.0012207031
- down_master: float32 [4096, 1024], P(('frame', 'row')), may hold values from -0.09375 to 0.09375
- down_momentum: float32 [4096, 1024], P(('frame', 'row')), may hold values from -0.0012207031 to 0.0012207031
- ada_master: float32 [1024, 6144], P(None, ('frame', 'row')), may hold values from -0.1875 to 0.1875
- ada_first: float32 [1024, 6144], P(None, ('frame', 'row')), may hold values from -0.00015258789 to 0.00015258789
- ada_second: float32 [1024, 6144], P(None, ('frame', 'row')), may hold values from 1.5053373e-09 to 2.0071164e-08
- table_master: float32 [1024, 1024], P(('frame', 'row')), may hold values from -5 to 5
- table_first: float32 [1024, 1024], P(('frame', 'row')), may hold values from -0.00015258789 to 0.00015258789
- table_second: float32 [1024, 1024], P(('frame', 'row')), may hold values from 1.5053373e-09 to 2.0071164e-08
- bias_master: float32 [6144], P(('frame', 'row')), may hold values from -3 to 3
- bias_first: float32 [6144], P(('frame', 'row')), may hold values from -0.00015258789 to 0.00015258789
- bias_second: float32 [6144], P(('frame', 'row')), may hold values from 1.5053373e-09 to 2.0071164e-08
Outputs:
- block_out: bfloat16 [16, 8, 16, 16, 1024], P('frame', None, 'row')
- input_grad: float32 [16, 8, 16, 16, 1024], P('frame', None, 'row')
- grad_norm: float32 [1], replicated
- qkv_momentum_new: float32 [1024, 3072], P(None, ('frame', 'row'))
- qkv_master_new: float32 [1024, 3072], P(None, ('frame', 'row'))
- out_momentum_new: float32 [1024, 1024], P(('frame', 'row'))
- out_master_new: float32 [1024, 1024], P(('frame', 'row'))
- up_momentum_new: float32 [1024, 4096], P(None, ('frame', 'row'))
- up_master_new: float32 [1024, 4096], P(None, ('frame', 'row'))
- down_momentum_new: float32 [4096, 1024], P(('frame', 'row'))
- down_master_new: float32 [4096, 1024], P(('frame', 'row'))
- ada_first_new: float32 [1024, 6144], P(None, ('frame', 'row'))
- ada_second_new: float32 [1024, 6144], P(None, ('frame', 'row'))
- ada_master_new: float32 [1024, 6144], P(None, ('frame', 'row'))
- table_first_new: float32 [1024, 1024], P(('frame', 'row'))
- table_clipped: float32 [1024, 1024], P(('frame', 'row'))
- table_master_new: float32 [1024, 1024], P(('frame', 'row'))
- bias_first_new: float32 [6144], P(('frame', 'row'))
- bias_second_new: float32 [6144], P(('frame', 'row'))
- bias_master_new: float32 [6144], P(('frame', 'row'))
The draws below stay inside these ranges and needn't reach their ends.
Inputs may be any that keep to these rules, and one draw needn't show every extreme that they name: `frame_times`: within each clip the times rise strictly; the first frame has time 0 and the last 23.
All inputs are finite; a program needn't handle non-finite values.
Results may differ from the reference program's by a relative error of at most 0.02.
The reference program's roundings to bfloat16 on the way count: a program that leaves them out, or rounds other values in their place, can miss the bound.
Values may be sent and summed in bfloat16 or wider, within the bound.
A program may use at most 384 MiB of HBM per device.

```python
import math
from functools import partial
import jax
import jax.numpy as jnp
from jax import lax

D = 1024
HEADS = 16
HD = 64
FF = 4096
LEVELS = 1024
PH = 16
PW = 16
CLIP_FRAMES = 8
CLIPS = 2
CLIP_TOTAL = 16
SEQ = 2048
PARAMS = 19929088
N_FRAME = 8


def draw_frame_times(key, part):

    def one_clip(clip_key):
        order = jax.random.permutation(clip_key, 3 * CLIP_FRAMES - 2)
        chosen = jnp.sort(order[:CLIP_FRAMES - 2] + 1).astype(jnp.int32)
        first_time = jnp.zeros((1,), jnp.int32)
        last_time = jnp.full((1,), 3 * CLIP_FRAMES - 1, jnp.int32)
        return jnp.concatenate([first_time, chosen, last_time])
    clip_keys = jax.random.split(jax.random.fold_in(key, 7), CLIPS * N_FRAME)
    return jax.vmap(one_clip)(clip_keys)


def draw_up_master(key, part):
    key = jax.random.fold_in(key, 11)
    base_key, column_key = jax.random.split(key)
    spread = D ** (-0.5)
    base = jnp.clip(jax.random.normal(base_key, (D, FF), jnp.float32), -6.0, 6.0) * spread
    column = jnp.clip(jax.random.normal(column_key, (FF,), jnp.float32), -3.0, 3.0) * (0.7 * spread)
    return (base + column[None, :]).astype(jnp.float32)


def set_ends(array, own_key, low, top_value):
    place = [jax.random.randint(jax.random.fold_in(own_key, axis), (), 0, length) for axis, length in enumerate(array.shape)]
    longest = array.shape.index(max(array.shape))
    beside = place[:longest] + [(place[longest] + 1) % array.shape[longest]] + place[longest + 1:]
    return array.at[tuple(place)].set(low).at[tuple(beside)].set(top_value)


def shard_levels(rng, extent, cuts, smallest, largest):
    def one(axis_at, parts):
        steps = jax.random.uniform(jax.random.fold_in(jax.random.fold_in(rng, 6), axis_at), (parts,), jnp.float32, smallest / len(cuts), largest / len(cuts))
        return jnp.repeat(jnp.exp(steps), extent[axis_at] // parts).reshape((-1,) + (1,) * (len(extent) - axis_at - 1))

    level = one(*cuts[0])
    for cut in cuts[1:]:
        level = level * one(*cut)
    return level


def scatter_about(stream_key, shape, scale, bound, cuts=(), kind=jnp.bfloat16):
    entries = scale * jax.random.normal(stream_key, shape, jnp.float32)
    if cuts:
        entries = entries * shard_levels(stream_key, shape, cuts, -0.22, 0.18)
    return jnp.clip(entries, -bound, bound).astype(kind)


def setup_inputs(seed: int = 0) -> dict:
    arg_keys = jax.random.split(jax.random.key(seed), 23)
    return {
        "tokens": scatter_about(arg_keys[0], (CLIP_TOTAL, CLIP_FRAMES, PH, PW, D), 1.0, 6.0, ((0, 8), (2, 4))),
        "cotangent": scatter_about(arg_keys[1], (CLIP_TOTAL, CLIP_FRAMES, PH, PW, D), 1.0, 6.0, ((0, 8), (2, 4))),
        "noise_levels": set_ends(jax.random.randint(arg_keys[2], (CLIP_TOTAL, CLIP_FRAMES), 0, LEVELS), jax.random.fold_in(arg_keys[2], 1), 0, LEVELS - 1).astype(jnp.int32),
        "frame_times": draw_frame_times(jax.random.fold_in(arg_keys[22], 71), 0),
        "step_count": jax.random.randint(arg_keys[4], (1,), 1, 21).astype(jnp.int32),
        "qkv_master": scatter_about(arg_keys[5], (D, 3 * D), (D // 2) ** -0.5, 0.25, ((1, 32),), jnp.float32),
        "qkv_momentum": scatter_about(arg_keys[6], (D, 3 * D), (PARAMS ** -0.5), 0.0012207031, ((1, 32),), jnp.float32),
        "out_master": scatter_about(arg_keys[7], (D, D), (max(1, 55 * D // SEQ)) ** -0.5, 1.25, ((0, 32),), jnp.float32),
        "out_momentum": scatter_about(arg_keys[8], (D, D), (PARAMS ** -0.5), 0.0012207031, ((0, 32),), jnp.float32),
        "up_master": draw_up_master(jax.random.fold_in(arg_keys[22], 71), 0),
        "up_momentum": scatter_about(arg_keys[10], (D, FF), (PARAMS ** -0.5), 0.0012207031, ((1, 32),), jnp.float32),
        "down_master": scatter_about(arg_keys[11], (FF, D), FF ** -0.5, 0.09375, ((0, 32),), jnp.float32),
        "down_momentum": scatter_about(arg_keys[12], (FF, D), (PARAMS ** -0.5), 0.0012207031, ((0, 32),), jnp.float32),
        "ada_master": scatter_about(arg_keys[13], (D, 6 * D), D ** -0.5, 0.1875, ((1, 32),), jnp.float32),
        "ada_first": scatter_about(arg_keys[14], (D, 6 * D), (0.11 * PARAMS ** -0.5), 0.00015258789, ((1, 32),), jnp.float32),
        "ada_second": jnp.clip(jnp.exp(math.log(2.0071164286150633e-08) - 2.5902672 * jax.random.uniform(arg_keys[15], (D, 6 * D), jnp.float32) ** shard_levels(arg_keys[15], (D, 6 * D), ((1, 32),), -0.2, 0.2)), 1.505337299256837e-09, 2.0071164286150633e-08),
        "table_master": scatter_about(arg_keys[16], (LEVELS, D), 1.0, 5.0, ((0, 32),), jnp.float32),
        "table_first": scatter_about(arg_keys[17], (LEVELS, D), (0.11 * PARAMS ** -0.5), 0.00015258789, ((0, 32),), jnp.float32),
        "table_second": jnp.clip(jnp.exp(math.log(2.0071164286150633e-08) - 2.5902672 * jax.random.uniform(arg_keys[18], (LEVELS, D), jnp.float32) ** shard_levels(arg_keys[18], (LEVELS, D), ((0, 32),), -0.2, 0.2)), 1.505337299256837e-09, 2.0071164286150633e-08),
        "bias_master": scatter_about(arg_keys[19], (6 * D,), 0.5, 3.0, ((0, 32),), jnp.float32),
        "bias_first": scatter_about(arg_keys[20], (6 * D,), (0.11 * PARAMS ** -0.5), 0.00015258789, ((0, 32),), jnp.float32),
        "bias_second": jnp.clip(jnp.exp(math.log(2.0071164286150633e-08) - 2.5902672 * jax.random.uniform(arg_keys[21], (6 * D,), jnp.float32) ** shard_levels(arg_keys[21], (6 * D,), ((0, 32),), -0.2, 0.2)), 1.505337299256837e-09, 2.0071164286150633e-08),
    }


@jax.custom_vjp
def low(v):
    return lax.optimization_barrier(v.astype(jnp.bfloat16)).astype(jnp.float32)

@jax.custom_vjp
def low_back(v):
    return v

def low_keep(v):
    return (low(v), None)

def low_pass(kept, grad):
    return (grad,)

def back_keep(v):
    return (v, None)

def back_low(kept, grad):
    return (low(grad),)
low.defvjp(low_keep, low_pass)
low_back.defvjp(back_keep, back_low)
highest = lax.Precision.HIGHEST
newton_one = 3.4445
newton_two = -4.775
newton_three = 2.0315
momentum_decay = 0.95
muon_rate = 1.5
weight_decay = 0.01
beta_first = 0.9
beta_second = 0.95
adam_floor = 1e-08
norm_floor = 1e-06
clip_limit = 1.0
rotary_base = 10000.0

def layer_norm(values):
    centered = values - lax.optimization_barrier(jnp.mean(values, axis=-1, keepdims=True))
    return centered * lax.rsqrt(lax.optimization_barrier(jnp.mean(centered * centered, axis=-1, keepdims=True)) + norm_floor)

def modulate(values, shift_part, scaling):
    return layer_norm(values) * (1.0 + scaling) + shift_part

def gelu_tanh(values):
    return jax.nn.gelu(values, approximate=True)

def rotary_angles(time_grid, row_grid, column_grid):
    quarter_pairs = HD // 4
    eighth_pairs = HD // 8
    time_rates = rotary_base ** (-jnp.arange(quarter_pairs, dtype=jnp.float32) / quarter_pairs)
    space_rates = rotary_base ** (-jnp.arange(eighth_pairs, dtype=jnp.float32) / eighth_pairs)
    return jnp.concatenate([time_grid[..., None] * time_rates, row_grid[..., None] * space_rates, column_grid[..., None] * space_rates], axis=-1)

def rotate(values, angles):
    paired = values.reshape(values.shape[:-1] + (values.shape[-1] // 2, 2))
    cosine = jnp.cos(angles)[..., None, :]
    sine = jnp.sin(angles)[..., None, :]
    first_part = paired[..., 0] * cosine - paired[..., 1] * sine
    second_part = paired[..., 0] * sine + paired[..., 1] * cosine
    return jnp.stack([first_part, second_part], axis=-1).reshape(values.shape)

def clip_forward(lowered, operands):
    w_qkv, w_out, w_up, w_down, w_ada, w_table, w_bias = lowered
    clip_tokens, clip_levels, clip_times = operands
    cond = low(jax.nn.silu(w_table[clip_levels]))
    modulation = low_back(jnp.dot(cond, w_ada, precision=highest) + w_bias).reshape(CLIP_FRAMES, 1, 1, 6 * D)
    pieces = [modulation[..., piece_index * D:(piece_index + 1) * D] for piece_index in range(6)]
    shift_one, scale_one, gate_one, shift_two, scale_two, gate_two = pieces
    grid_shape = (CLIP_FRAMES, PH, PW)
    time_grid = jnp.broadcast_to(clip_times.astype(jnp.float32)[:, None, None], grid_shape)
    row_grid = jnp.broadcast_to(jnp.arange(PH, dtype=jnp.int32).astype(jnp.float32)[None, :, None], grid_shape)
    column_grid = jnp.broadcast_to(jnp.arange(PW, dtype=jnp.int32).astype(jnp.float32)[None, None, :], grid_shape)
    angles = rotary_angles(time_grid, row_grid, column_grid).reshape(SEQ, HD // 2)
    hidden_one = low(modulate(clip_tokens, shift_one, scale_one)).reshape(SEQ, D)
    projected = low_back(jnp.dot(hidden_one, w_qkv, precision=highest)).reshape(SEQ, 3, HEADS, HD)
    queries = low_back(low(rotate(projected[:, 0], angles)))
    keys_rot = low_back(low(rotate(projected[:, 1], angles)))
    values_low = low_back(low(projected[:, 2]))
    scores = low_back(jnp.einsum('qhd,khd->hqk', queries, keys_rot, precision=highest) * (1.0 / math.sqrt(HD)))
    top_score = lax.optimization_barrier(jnp.max(scores, axis=-1, keepdims=True))
    raised = jnp.exp(scores - top_score)
    prob_full = raised / lax.optimization_barrier(jnp.sum(raised, axis=-1, keepdims=True))
    attended = low_back(low(jnp.einsum('hqk,khd->qhd', low(prob_full), values_low, precision=highest))).reshape(SEQ, D)
    branch_one = low_back(jnp.dot(attended, w_out, precision=highest)).reshape(CLIP_FRAMES, PH, PW, D)
    middle = clip_tokens + gate_one * branch_one
    hidden_two = low(modulate(middle, shift_two, scale_two)).reshape(SEQ, D)
    up_value = low_back(jnp.dot(hidden_two, w_up, precision=highest))
    activated = low(gelu_tanh(up_value))
    branch_two = low_back(jnp.dot(activated, w_down, precision=highest)).reshape(CLIP_FRAMES, PH, PW, D)
    return middle + gate_two * branch_two

def muon_update(grad_item, moment, master, clip_factor, flipped):
    clipped = clip_factor * grad_item
    moment_new = momentum_decay * moment + clipped
    update = clipped + momentum_decay * moment_new
    frob = jnp.sqrt(jnp.sum(update * update))
    tall = (update.T if flipped else update) / (frob + 1e-07)
    for newton_step in range(5):
        gram = jnp.dot(tall.T, tall, precision=highest)
        product = jnp.dot(tall, gram, precision=highest)
        tall = newton_one * tall + newton_two * product + newton_three * jnp.dot(product, gram, precision=highest)
    factor = math.sqrt(tall.shape[0] / tall.shape[1])
    ortho = tall.T if flipped else tall
    master_new = master * (1.0 - muon_rate * weight_decay) - muon_rate * factor * ortho
    return (moment_new, master_new)

def adam_update(grad_item, first, second, master, rate, clip_factor, step_value):
    clipped = clip_factor * grad_item
    first_new = beta_first * first + (1.0 - beta_first) * clipped
    second_new = beta_second * second + (1.0 - beta_second) * clipped * clipped
    first_fix = 1.0 - beta_first ** step_value
    second_fix = 1.0 - beta_second ** step_value
    master_new = master * (1.0 - rate * weight_decay) - rate * (first_new / first_fix) / (jnp.sqrt(second_new / second_fix) + adam_floor)
    return (first_new, second_new, master_new)

def reference(tokens, cotangent, noise_levels, frame_times, step_count, qkv_master, qkv_momentum, out_master, out_momentum, up_master, up_momentum, down_master, down_momentum, ada_master, ada_first, ada_second, table_master, table_first, table_second, bias_master, bias_first, bias_second):
    params = (qkv_master, out_master, up_master, down_master, ada_master, table_master, bias_master)

    def forward(inputs, weights):
        lowered = tuple((low(item) for item in weights))
        return lax.map(jax.checkpoint(partial(clip_forward, lowered)), (inputs, noise_levels, frame_times))
    block_out, pullback = jax.vjp(forward, tokens.astype(jnp.float32), params)
    input_grad, grads = pullback(cotangent.astype(jnp.float32))
    norm_value = jnp.sqrt(sum((jnp.sum(item * item) for item in grads)))
    clip_factor = jnp.minimum(1.0, clip_limit / (norm_value + 1e-06))
    qkv_momentum_new, qkv_master_new = muon_update(grads[0], qkv_momentum, qkv_master, clip_factor, True)
    out_momentum_new, out_master_new = muon_update(grads[1], out_momentum, out_master, clip_factor, False)
    up_momentum_new, up_master_new = muon_update(grads[2], up_momentum, up_master, clip_factor, True)
    down_momentum_new, down_master_new = muon_update(grads[3], down_momentum, down_master, clip_factor, False)
    step_value = step_count.astype(jnp.float32)[0]
    ada_first_new, ada_second_new, ada_master_new = adam_update(grads[4], ada_first, ada_second, ada_master, 0.03, clip_factor, step_value)
    table_clipped = clip_factor * grads[5]
    table_first_new, table_second_new, table_master_new = adam_update(grads[5], table_first, table_second, table_master, 0.5, clip_factor, step_value)
    bias_first_new, bias_second_new, bias_master_new = adam_update(grads[6], bias_first, bias_second, bias_master, 0.5, clip_factor, step_value)
    return (block_out.astype(jnp.bfloat16), input_grad, norm_value.reshape(1), qkv_momentum_new, qkv_master_new, out_momentum_new, out_master_new, up_momentum_new, up_master_new, down_momentum_new, down_master_new, ada_first_new, ada_second_new, ada_master_new, table_first_new, table_clipped, table_master_new, bias_first_new, bias_second_new, bias_master_new)
```

```python
import math

import jax
import jax.numpy as jnp
from jax import lax
from jax.experimental import pallas as pl
from jax.experimental.pallas import tpu as pltpu
from jax.sharding import PartitionSpec as P

D = 1024
HEADS = 16
HD = 64
FF = 4096


highest = lax.Precision.HIGHEST
newton_one = 3.4445
newton_two = -4.775
newton_three = 2.0315
momentum_decay = 0.95
muon_rate = 1.5
weight_decay = 0.01
beta_first = 0.9
beta_second = 0.95
adam_floor = 1e-08
norm_floor = 1e-06
clip_limit = 1.0
rotary_base = 10000.0
group_heads = 4


def layer_norm(values):
    centered = values - jnp.mean(values, axis=-1, keepdims=True)
    return centered * lax.rsqrt(jnp.mean(centered * centered, axis=-1, keepdims=True) + norm_floor)


def modulate(values, shift_part, scaling):
    return layer_norm(values) * (1.0 + scaling) + shift_part


def gelu_tanh(values):
    return jax.nn.gelu(values, approximate=True)


def rounded(values):
    return lax.optimization_barrier(values.astype(jnp.bfloat16)).astype(jnp.float32)


def rotary_angles(time_grid, row_grid, column_grid):
    quarter_pairs = HD // 4
    eighth_pairs = HD // 8
    time_rates = rotary_base ** (-jnp.arange(quarter_pairs, dtype=jnp.float32) / quarter_pairs)
    space_rates = rotary_base ** (-jnp.arange(eighth_pairs, dtype=jnp.float32) / eighth_pairs)
    return jnp.concatenate(
        [
            time_grid[..., None] * time_rates,
            row_grid[..., None] * space_rates,
            column_grid[..., None] * space_rates,
        ],
        axis=-1,
    )


def rotate(values, angles):
    paired = values.reshape(values.shape[:-1] + (values.shape[-1] // 2, 2))
    cosine = jnp.cos(angles)[..., None, :]
    sine = jnp.sin(angles)[..., None, :]
    first_part = paired[..., 0] * cosine - paired[..., 1] * sine
    second_part = paired[..., 0] * sine + paired[..., 1] * cosine
    return jnp.stack([first_part, second_part], axis=-1).reshape(values.shape)


def adam_update(grad_item, first, second, master, rate, clip_factor, step_value):
    clipped = clip_factor * grad_item
    first_new = beta_first * first + (1.0 - beta_first) * clipped
    second_new = beta_second * second + (1.0 - beta_second) * clipped * clipped
    first_fix = 1.0 - beta_first**step_value
    second_fix = 1.0 - beta_second**step_value
    master_new = master * (1.0 - rate * weight_decay) - rate * (first_new / first_fix) / (
        jnp.sqrt(second_new / second_fix) + adam_floor
    )
    return (first_new, second_new, master_new)


def halve(value, dim, axis, bit):
    mine = (lax.axis_index(axis) >> bit) & 1
    keep = lax.dynamic_index_in_dim(value, mine, dim, keepdims=False)
    send = lax.dynamic_index_in_dim(value, 1 - mine, dim, keepdims=False)
    size = lax.axis_size(axis)
    pairs = [(index, index ^ (1 << bit)) for index in range(size)]
    came = lax.ppermute(send.astype(jnp.bfloat16), axis, pairs)
    return keep.astype(jnp.float32) + came.astype(jnp.float32)


def halve_all(value, names, order):
    names = list(names)
    for name in order:
        dim = names.index(name)
        value = halve(value, dim, name[0], name[1])
        names.pop(dim)
    return value


def scatter_sum(value):
    frame_bits = lax.axis_size("frame").bit_length() - 1
    row_bits = lax.axis_size("row").bit_length() - 1
    names = [("frame", bit) for bit in reversed(range(frame_bits))]
    names += [("row", bit) for bit in reversed(range(row_bits))]
    value = value.reshape((2,) * (frame_bits + row_bits) + value.shape[1:])
    value = halve_all(value, names, [("frame", 0)])
    names.remove(("frame", 0))
    upward = [("row", bit) for bit in range(row_bits)]
    width = value.shape[-1] // 2
    left = halve_all(value[..., :width], names, upward)
    right = halve_all(value[..., width:], names, upward[::-1])
    names = names[: frame_bits - 1]
    value = jnp.concatenate([left, right], axis=-1)
    return halve_all(value, names, [("frame", bit) for bit in range(1, frame_bits)])


def split_two(value):
    high = value.astype(jnp.bfloat16)
    return high, (value - high.astype(jnp.float32)).astype(jnp.bfloat16)


def dot_low(left, right):
    return lax.dot_general(left, right, (((1,), (0,)), ((), ())), preferred_element_type=jnp.float32)


def newton_kernel(all_ref, mine_ref, out_ref, a_ref, q_ref, t_ref, ah, al, nh, nl, th, tl, qh, ql):
    width = a_ref.shape[0]
    rows = 256
    steps = width // rows
    depth = all_ref.shape[0]

    def block(index):
        return pl.ds(pl.multiple_of(index * rows, rows), rows)

    def gram(index, total):
        columns = block(index)

        def part(k, value):
            deep = pl.ds(pl.multiple_of(k * 1024, 1024), 1024)
            return value + lax.dot_general(
                all_ref[deep, columns],
                all_ref[deep, :],
                (((0,), (0,)), ((), ())),
                preferred_element_type=jnp.float32,
            )

        value = lax.fori_loop(0, depth // 1024, part, jnp.zeros((rows, width), jnp.float32))
        a_ref[columns, :] = value
        row_at = lax.broadcasted_iota(jnp.int32, (rows, width), 0) + index * rows
        column_at = lax.broadcasted_iota(jnp.int32, (rows, width), 1)
        return total + jnp.sum(jnp.where(row_at == column_at, value, 0.0))

    squares = 0.0
    for index in range(steps):
        squares = gram(index, squares)
    squares = jnp.full((1, 1), squares, jnp.float32)
    inverse = 1.0 / (jnp.sqrt(squares) + 1e-07)

    def first_split(index, carry):
        at = block(index)
        value = a_ref[at, :] * inverse * inverse
        a_ref[at, :] = value
        high, rest = split_two(value)
        ah[at, :] = high
        al[at, :] = rest
        return carry

    lax.fori_loop(0, steps, first_split, 0)

    def three(lh, ll, rh, rl):
        return dot_low(lh, rh) + dot_low(lh, rl) + dot_low(ll, rh)

    def one_step(number, exact, last):
        def make_n(index, carry):
            at = block(index)
            if exact:
                square = three(ah[at, :], al[at, :], ah[...], al[...])
            else:
                square = dot_low(ah[at, :], ah[...])
            value = newton_two * a_ref[at, :] + newton_three * square
            high, rest = split_two(value)
            nh[at, :] = high
            if exact:
                nl[at, :] = rest
            return carry

        lax.fori_loop(0, steps, make_n, 0)

        def make_q(index, carry):
            at = block(index)
            if number == 0:
                row_at = lax.broadcasted_iota(jnp.int32, (rows, width), 0) + index * rows
                column_at = lax.broadcasted_iota(jnp.int32, (rows, width), 1)
                value = nh[at, :].astype(jnp.float32) + jnp.where(row_at == column_at, newton_one, 0.0)
            elif exact:
                value = newton_one * q_ref[at, :] + three(qh[at, :], ql[at, :], nh[...], nl[...])
            else:
                value = newton_one * q_ref[at, :] + dot_low(qh[at, :], nh[...]) + dot_low(ql[at, :], nh[...])
            q_ref[at, :] = value
            high, rest = split_two(value)
            qh[at, :] = high
            ql[at, :] = rest
            return carry

        lax.fori_loop(0, steps, make_q, 0)
        if last:
            return

        def make_t(index, carry):
            at = block(index)
            if exact:
                value = newton_one * a_ref[at, :] + three(ah[at, :], al[at, :], nh[...], nl[...])
            else:
                value = newton_one * a_ref[at, :] + dot_low(ah[at, :], nh[...]) + dot_low(al[at, :], nh[...])
            t_ref[at, :] = value
            high, rest = split_two(value)
            th[at, :] = high
            tl[at, :] = rest
            return carry

        lax.fori_loop(0, steps, make_t, 0)

        def make_a(index, carry):
            at = block(index)
            if exact:
                value = newton_one * t_ref[at, :] + three(nh[at, :], nl[at, :], th[...], tl[...])
            else:
                value = newton_one * t_ref[at, :] + dot_low(nh[at, :], th[...]) + dot_low(nh[at, :], tl[...])
            a_ref[at, :] = value
            high, rest = split_two(value)
            ah[at, :] = high
            al[at, :] = rest
            return carry

        lax.fori_loop(0, steps, make_a, 0)

    for number in range(5):
        one_step(number, number >= 2, number == 4)

    mine = mine_ref[...]
    out_ref[...] = ((dot_low(mine, qh[...]) + dot_low(mine, ql[...])) * inverse).astype(out_ref.dtype)


def newton(everything, mine):
    width = everything.shape[1]
    full = pltpu.VMEM((width, width), jnp.float32)
    low = pltpu.VMEM((width, width), jnp.bfloat16)
    return pl.pallas_call(
        newton_kernel,
        out_shape=jax.ShapeDtypeStruct(mine.shape, jnp.bfloat16),
        in_specs=[pl.BlockSpec(memory_space=pltpu.VMEM)] * 2,
        out_specs=pl.BlockSpec(memory_space=pltpu.VMEM),
        scratch_shapes=[full] * 3 + [low] * 8,
        compiler_params=pltpu.CompilerParams(vmem_limit_bytes=52 * 1024 * 1024),
        cost_estimate=pl.CostEstimate(flops=110 * 10**9, bytes_accessed=12 * 10**6, transcendentals=0),
    )(everything, mine)


def per_device(
    tokens,
    cotangent,
    noise_levels,
    frame_times,
    step_count,
    qkv_master,
    qkv_momentum,
    out_master,
    out_momentum,
    up_master,
    up_momentum,
    down_master,
    down_momentum,
    ada_master,
    ada_first,
    ada_second,
    table_master,
    table_first,
    table_second,
    bias_master,
    bias_first,
    bias_second,
):
    low_type = jnp.bfloat16
    full_type = jnp.float32
    clip_count, frames, rows_dev, columns, model_width = tokens.shape
    seq_local = frames * rows_dev * columns
    row_devices = lax.axis_size("row")
    seq_full = seq_local * row_devices
    token_total = clip_count * seq_local
    frame_total = clip_count * frames
    attn_scale = 1.0 / math.sqrt(HD)
    shape_five = (clip_count, frames, rows_dev, columns, model_width)
    w_qkv, w_out, w_up, w_down, w_ada, w_table, w_bias = (
        lax.all_gather(qkv_master.astype(low_type), ("frame", "row"), axis=1, tiled=True),
        lax.all_gather(out_master.astype(low_type), ("frame", "row"), axis=0, tiled=True),
        lax.all_gather(up_master.astype(low_type), ("frame", "row"), axis=1, tiled=True),
        lax.all_gather(down_master.astype(low_type), ("frame", "row"), axis=0, tiled=True),
        lax.all_gather(ada_master.astype(low_type), ("frame", "row"), axis=1, tiled=True),
        lax.all_gather(table_master.astype(low_type), ("frame", "row"), axis=0, tiled=True),
        lax.all_gather(bias_master.astype(low_type), ("frame", "row"), axis=0, tiled=True),
    )
    level_flat = noise_levels.reshape(frame_total)
    level_hot = (
        level_flat[:, None] == jnp.arange(w_table.shape[0], dtype=jnp.int32)[None, :]
    ).astype(low_type)
    embedded = jnp.dot(level_hot, w_table, preferred_element_type=full_type)
    cond_low = jax.nn.silu(embedded).astype(low_type)
    modulation = jnp.dot(cond_low, w_ada, preferred_element_type=full_type) + w_bias.astype(
        full_type
    )
    mod_five = modulation.reshape(clip_count, frames, 1, 1, 6 * model_width)
    pieces = [
        mod_five[..., piece_index * model_width : (piece_index + 1) * model_width]
        for piece_index in range(6)
    ]
    shift_one, scale_one, gate_one, shift_two, scale_two, gate_two = pieces
    grid_shape = (clip_count, frames, rows_dev, columns)
    row_first = lax.axis_index("row") * rows_dev
    time_grid = jnp.broadcast_to(frame_times.astype(full_type)[:, :, None, None], grid_shape)
    row_grid = jnp.broadcast_to(
        (row_first + jnp.arange(rows_dev, dtype=jnp.int32)).astype(full_type)[None, None, :, None],
        grid_shape,
    )
    column_grid = jnp.broadcast_to(
        jnp.arange(columns, dtype=jnp.int32).astype(full_type)[None, None, None, :], grid_shape
    )
    angles = rotary_angles(time_grid, row_grid, column_grid).reshape(clip_count, seq_local, HD // 2)
    inputs_full = tokens.astype(full_type)
    hidden_one = (
        modulate(inputs_full, shift_one, scale_one)
        .astype(low_type)
        .reshape(token_total, model_width)
    )
    projected = jnp.dot(hidden_one, w_qkv, preferred_element_type=full_type).reshape(
        clip_count, seq_local, 3, HEADS, HD
    )
    queries = rotate(projected[:, :, 0], angles).astype(low_type)
    keys_rot = rotate(projected[:, :, 1], angles).astype(low_type)
    values_low = projected[:, :, 2].astype(low_type)
    keys_whole, values_whole = (
        lax.all_gather(keys_rot.reshape(shape_five), "row", axis=2, tiled=True),
        lax.all_gather(values_low.reshape(shape_five), "row", axis=2, tiled=True),
    )
    keys_seq = keys_whole.reshape(clip_count, seq_full, HEADS, HD)
    values_seq = values_whole.reshape(clip_count, seq_full, HEADS, HD)

    def attend_clip(operands):
        query_block, key_block, value_block = operands
        outputs = []
        log_totals = []
        for group_index in range(HEADS // group_heads):
            head_first = group_index * group_heads
            head_last = head_first + group_heads
            scores = (
                jnp.einsum(
                    "qhd,khd->hqk",
                    query_block[:, head_first:head_last],
                    key_block[:, head_first:head_last],
                    preferred_element_type=full_type,
                )
                * attn_scale
            )
            top_score = jnp.max(scores, axis=-1, keepdims=True)
            raised = jnp.exp(scores - top_score)
            total_weight = jnp.sum(raised, axis=-1, keepdims=True)
            prob_low = (raised / total_weight).astype(low_type)
            outputs.append(
                jnp.einsum(
                    "hqk,khd->qhd",
                    prob_low,
                    value_block[:, head_first:head_last],
                    preferred_element_type=full_type,
                )
            )
            log_totals.append((top_score + jnp.log(total_weight))[..., 0])
        return (jnp.concatenate(outputs, axis=1), jnp.concatenate(log_totals, axis=0))

    attended_full, log_total = lax.map(attend_clip, (queries, keys_seq, values_seq))
    attended = attended_full.astype(low_type).reshape(token_total, model_width)
    branch_one = jnp.dot(attended, w_out, preferred_element_type=full_type).reshape(shape_five)
    middle = inputs_full + gate_one * branch_one
    hidden_two = (
        modulate(middle, shift_two, scale_two).astype(low_type).reshape(token_total, model_width)
    )
    up_value = jnp.dot(hidden_two, w_up, preferred_element_type=full_type)
    activated = gelu_tanh(up_value).astype(low_type)
    branch_two = jnp.dot(activated, w_down, preferred_element_type=full_type).reshape(shape_five)
    block_out = (middle + gate_two * branch_two).astype(low_type)
    upstream = cotangent.astype(full_type)
    d_branch_two = (upstream * gate_two).astype(low_type).reshape(token_total, model_width)
    d_gate_two = jnp.sum(upstream * branch_two, axis=(2, 3))
    grad_down = jnp.einsum("tf,td->fd", activated, d_branch_two, preferred_element_type=full_type)
    d_activated = jnp.einsum("td,fd->tf", d_branch_two, w_down, preferred_element_type=full_type)
    d_up = jax.vjp(gelu_tanh, up_value)[1](d_activated)[0].astype(low_type)
    grad_up = jnp.einsum("tf,td->fd", d_up, hidden_two, preferred_element_type=full_type)
    d_hidden_two = jnp.einsum("tf,df->td", d_up, w_up, preferred_element_type=full_type).reshape(
        shape_five
    )
    d_middle_part, d_shift_two, d_scale_two = jax.vjp(modulate, middle, shift_two, scale_two)[1](
        d_hidden_two
    )
    d_middle = upstream + d_middle_part
    d_gate_one = jnp.sum(d_middle * branch_one, axis=(2, 3))
    d_branch_one = (d_middle * gate_one).astype(low_type).reshape(token_total, model_width)
    grad_out = jnp.einsum("td,te->de", attended, d_branch_one, preferred_element_type=full_type)
    d_attended = (
        jnp.einsum("te,de->td", d_branch_one, w_out, preferred_element_type=full_type)
        .astype(low_type)
        .reshape(clip_count, seq_local, HEADS, HD)
    )

    def attend_back(operands):
        query_block, key_block, value_block, log_block, grad_block = operands
        query_parts = []
        key_parts = []
        value_parts = []
        for group_index in range(HEADS // group_heads):
            head_first = group_index * group_heads
            head_last = head_first + group_heads
            query_group = query_block[:, head_first:head_last]
            key_group = key_block[:, head_first:head_last]
            value_group = value_block[:, head_first:head_last]
            grad_group = grad_block[:, head_first:head_last]
            scores = (
                jnp.einsum("qhd,khd->hqk", query_group, key_group, preferred_element_type=full_type)
                * attn_scale
            )
            prob_full = jnp.exp(scores - log_block[head_first:head_last][..., None])
            grad_prob = jnp.einsum(
                "qhd,khd->hqk", grad_group, value_group, preferred_element_type=full_type
            )
            inner_sum = jnp.sum(prob_full * grad_prob, axis=-1, keepdims=True)
            grad_scores = (prob_full * (grad_prob - inner_sum)).astype(low_type)
            query_parts.append(
                jnp.einsum("hqk,khd->qhd", grad_scores, key_group, preferred_element_type=full_type)
                * attn_scale
            )
            key_parts.append(
                jnp.einsum(
                    "hqk,qhd->khd", grad_scores, query_group, preferred_element_type=full_type
                )
                * attn_scale
            )
            value_parts.append(
                jnp.einsum(
                    "hqk,qhd->khd",
                    prob_full.astype(low_type),
                    grad_group,
                    preferred_element_type=full_type,
                )
            )
        return (
            jnp.concatenate(query_parts, axis=1),
            jnp.concatenate(key_parts, axis=1),
            jnp.concatenate(value_parts, axis=1),
        )

    grad_query, grad_key, grad_value = lax.map(
        attend_back, (queries, keys_seq, values_seq, log_total, d_attended)
    )
    gathered_shape = (clip_count, frames, rows_dev * row_devices, columns, model_width)
    key_sums, value_sums = (
        lax.psum_scatter(
            grad_key.reshape(gathered_shape).astype(jnp.bfloat16),
            "row",
            scatter_dimension=2,
            tiled=True,
        ).astype(jnp.float32),
        lax.psum_scatter(
            grad_value.reshape(gathered_shape).astype(jnp.bfloat16),
            "row",
            scatter_dimension=2,
            tiled=True,
        ).astype(jnp.float32),
    )
    d_queries = rounded(grad_query)
    d_keys = rounded(key_sums).reshape(clip_count, seq_local, HEADS, HD)
    d_values = rounded(value_sums).reshape(clip_count, seq_local, HEADS, HD)
    d_projected = (
        jnp.stack([rotate(d_queries, -angles), rotate(d_keys, -angles), d_values], axis=2)
        .astype(low_type)
        .reshape(token_total, 3 * model_width)
    )
    grad_qkv = jnp.einsum("te,td->ed", d_projected, hidden_one, preferred_element_type=full_type)
    d_hidden_one = jnp.einsum(
        "te,de->td", d_projected, w_qkv, preferred_element_type=full_type
    ).reshape(shape_five)
    d_input_part, d_shift_one, d_scale_one = jax.vjp(modulate, inputs_full, shift_one, scale_one)[
        1
    ](d_hidden_one)
    input_grad = d_middle + d_input_part
    frame_shape = (frame_total, model_width)
    d_modulation = jnp.concatenate(
        [
            d_shift_one.reshape(frame_shape),
            d_scale_one.reshape(frame_shape),
            d_gate_one.reshape(frame_shape),
            d_shift_two.reshape(frame_shape),
            d_scale_two.reshape(frame_shape),
            d_gate_two.reshape(frame_shape),
        ],
        axis=1,
    )
    frame_devices = lax.axis_size("frame")
    device_total = frame_devices * row_devices
    both = ("frame", "row")
    levels_all = lax.all_gather(level_flat, "frame", axis=0, tiled=True)
    embedded_all = lax.all_gather(embedded.astype(low_type), "frame", axis=0, tiled=True).astype(
        full_type
    )
    cond_all = jax.nn.silu(embedded_all).astype(low_type)
    ada_width = ada_master.shape[1]
    mod_parts = lax.all_to_all(
        jnp.moveaxis(d_modulation.reshape(frame_total, device_total, ada_width), 1, 0),
        both,
        split_axis=0,
        concat_axis=0,
        tiled=True,
    )
    mod_mine = (
        jnp.sum(mod_parts.reshape(frame_devices, row_devices, frame_total, ada_width), axis=1)
        .reshape(frame_devices * frame_total, ada_width)
        .astype(low_type)
    )
    g_ada = jnp.einsum("fd,fe->de", cond_all, mod_mine, preferred_element_type=full_type)
    g_bias = jnp.sum(mod_mine.astype(full_type), axis=0)
    d_cond = lax.psum(
        jnp.einsum("fe,de->fd", mod_mine, ada_master.astype(low_type), preferred_element_type=full_type),
        both,
    )
    d_embedded = jax.vjp(jax.nn.silu, embedded_all)[1](d_cond)[0]
    device_index = lax.axis_index("frame") * row_devices + lax.axis_index("row")
    level_rows = table_master.shape[0]
    hot_mine = (
        levels_all[None, :]
        == (device_index * level_rows + jnp.arange(level_rows, dtype=jnp.int32))[:, None]
    ).astype(full_type)
    g_table = jnp.dot(hot_mine, d_embedded, precision=highest)
    heights = (qkv_master.shape[1], out_master.shape[0], up_master.shape[1], down_master.shape[0])
    early = scatter_sum(
        jnp.concatenate(
            [
                grad_down.reshape(device_total, heights[3], model_width),
                grad_up.reshape(device_total, heights[2], model_width),
                grad_out.reshape(device_total, heights[1], model_width),
            ],
            axis=1,
        )
    )
    g_down = early[: heights[3]]
    g_up = early[heights[3] : heights[3] + heights[2]]
    g_out = early[heights[3] + heights[2] :]
    g_qkv = scatter_sum(grad_qkv.reshape(device_total, heights[0], model_width))
    muon_grads = (g_qkv, g_out, g_up, g_down)
    flipped = (True, False, True, False)

    def tall(value, member):
        return value.T if flipped[member] else value

    muon_moments = (qkv_momentum, out_momentum, up_momentum, down_momentum)
    muon_masters = (qkv_master, out_master, up_master, down_master)
    factors = (math.sqrt(3.0), 1.0, math.sqrt(FF / D), math.sqrt(FF / D))
    adam_local = jnp.sum(g_ada * g_ada) + jnp.sum(g_table * g_table) + jnp.sum(g_bias * g_bias)
    local_total = adam_local + sum((jnp.sum(item * item) for item in muon_grads))
    norm_value = jnp.sqrt(lax.psum(local_total, both))
    clip_factor = jnp.minimum(1.0, clip_limit / (norm_value + 1e-06))
    moments_new = []
    pieces = []
    slot = max(heights)
    for member in range(4):
        clipped = clip_factor * muon_grads[member]
        moment = momentum_decay * tall(muon_moments[member], member) + clipped
        update = (clipped + momentum_decay * moment).astype(low_type)
        moments_new.append(tall(moment, member))
        pieces.append(jnp.pad(update, ((0, slot - heights[member]), (0, 0))))
    slab = jnp.stack(pieces * (row_devices // 4))
    updates = lax.all_to_all(slab, "row", split_axis=0, concat_axis=0, tiled=True).reshape(
        row_devices * slot, model_width
    )
    everything = lax.all_gather(updates, "frame", axis=0, tiled=True)
    ortho_rows = newton(everything, updates).reshape(row_devices, slot, model_width)
    ortho_mine = lax.all_to_all(ortho_rows, "row", split_axis=0, concat_axis=0, tiled=True)
    blocks = [tall(ortho_mine[member, : heights[member]].astype(full_type), member) for member in range(4)]
    masters_new = []
    for member in range(4):
        ortho = blocks[member]
        masters_new.append(
            muon_masters[member] * (1.0 - muon_rate * weight_decay)
            - muon_rate * factors[member] * ortho
        )
    step_value = step_count.astype(full_type)[0]
    ada_first_new, ada_second_new, ada_master_new = adam_update(
        g_ada, ada_first, ada_second, ada_master, 0.03, clip_factor, step_value
    )
    table_clipped = clip_factor * g_table
    table_first_new, table_second_new, table_master_new = adam_update(
        g_table, table_first, table_second, table_master, 0.5, clip_factor, step_value
    )
    bias_first_new, bias_second_new, bias_master_new = adam_update(
        g_bias, bias_first, bias_second, bias_master, 0.5, clip_factor, step_value
    )
    return (
        block_out,
        input_grad,
        norm_value.reshape(1),
        moments_new[0],
        masters_new[0],
        moments_new[1],
        masters_new[1],
        moments_new[2],
        masters_new[2],
        moments_new[3],
        masters_new[3],
        ada_first_new,
        ada_second_new,
        ada_master_new,
        table_first_new,
        table_clipped,
        table_master_new,
        bias_first_new,
        bias_second_new,
        bias_master_new,
    )


def solution(mesh):
    return jax.shard_map(
        per_device,
        mesh=mesh,
        in_specs=(
            P("frame", None, "row", None, None),
            P("frame", None, "row", None, None),
            P("frame", None),
            P("frame", None),
            P(),
            P(None, ("frame", "row")),
            P(None, ("frame", "row")),
            P(("frame", "row"), None),
            P(("frame", "row"), None),
            P(None, ("frame", "row")),
            P(None, ("frame", "row")),
            P(("frame", "row"), None),
            P(("frame", "row"), None),
            P(None, ("frame", "row")),
            P(None, ("frame", "row")),
            P(None, ("frame", "row")),
            P(("frame", "row"), None),
            P(("frame", "row"), None),
            P(("frame", "row"), None),
            P(("frame", "row")),
            P(("frame", "row")),
            P(("frame", "row")),
        ),
        out_specs=(
            P("frame", None, "row", None, None),
            P("frame", None, "row", None, None),
            P(),
            P(None, ("frame", "row")),
            P(None, ("frame", "row")),
            P(("frame", "row"), None),
            P(("frame", "row"), None),
            P(None, ("frame", "row")),
            P(None, ("frame", "row")),
            P(("frame", "row"), None),
            P(("frame", "row"), None),
            P(None, ("frame", "row")),
            P(None, ("frame", "row")),
            P(None, ("frame", "row")),
            P(("frame", "row"), None),
            P(("frame", "row"), None),
            P(("frame", "row"), None),
            P(("frame", "row")),
            P(("frame", "row")),
            P(("frame", "row")),
        ),
        check_vma=False,
    )
```

```python
import functools
import math

import jax
import jax.numpy as jnp
from jax import lax
from jax.experimental import pallas as pl
from jax.experimental.pallas import tpu as pltpu
from jax.sharding import PartitionSpec as P

D = 1024
HEADS = 16
HD = 64
FF = 4096


highest = lax.Precision.HIGHEST
newton_one = 3.4445
newton_two = -4.775
newton_three = 2.0315
momentum_decay = 0.95
muon_rate = 1.5
weight_decay = 0.01
beta_first = 0.9
beta_second = 0.95
adam_floor = 1e-08
norm_floor = 1e-06
clip_limit = 1.0
rotary_base = 10000.0


def rotary_angles(time_grid, row_grid, column_grid):
    quarter_pairs = HD // 4
    eighth_pairs = HD // 8
    time_rates = rotary_base ** (-jnp.arange(quarter_pairs, dtype=jnp.float32) / quarter_pairs)
    space_rates = rotary_base ** (-jnp.arange(eighth_pairs, dtype=jnp.float32) / eighth_pairs)
    return jnp.concatenate(
        [
            time_grid[..., None] * time_rates,
            row_grid[..., None] * space_rates,
            column_grid[..., None] * space_rates,
        ],
        axis=-1,
    )


def adam_update(grad_item, first, second, master, rate, clip_factor, step_value):
    clipped = clip_factor * grad_item
    first_new = beta_first * first + (1.0 - beta_first) * clipped
    second_new = beta_second * second + (1.0 - beta_second) * clipped * clipped
    first_fix = 1.0 - beta_first**step_value
    second_fix = 1.0 - beta_second**step_value
    master_new = master * (1.0 - rate * weight_decay) - rate * (first_new / first_fix) / (
        jnp.sqrt(second_new / second_fix) + adam_floor
    )
    return (first_new, second_new, master_new)


def halve(value, dim, axis, bit):
    mine = (lax.axis_index(axis) >> bit) & 1
    keep = lax.dynamic_index_in_dim(value, mine, dim, keepdims=False)
    send = lax.dynamic_index_in_dim(value, 1 - mine, dim, keepdims=False)
    size = lax.axis_size(axis)
    pairs = [(index, index ^ (1 << bit)) for index in range(size)]
    came = lax.ppermute(send.astype(jnp.bfloat16), axis, pairs)
    return keep.astype(jnp.float32) + came.astype(jnp.float32)


def halve_all(value, names, order):
    names = list(names)
    for name in order:
        dim = names.index(name)
        value = halve(value, dim, name[0], name[1])
        names.pop(dim)
    return value


def scatter_sum(pairs, name):
    frame_bits = lax.axis_size("frame").bit_length() - 1
    row_bits = lax.axis_size("row").bit_length() - 1
    parity = (lax.axis_index("frame") & 1).astype(jnp.int32).reshape(1)
    send = weight_sums(1 - parity, pairs, jnp.bfloat16, name + "_send")
    size = lax.axis_size("frame")
    came = lax.ppermute(send, "frame", [(index, index ^ 1) for index in range(size)])
    keep = weight_sums(parity, pairs, jnp.float32, name + "_keep")
    value = keep + came.astype(jnp.float32)
    names = [("frame", bit) for bit in reversed(range(1, frame_bits))]
    names += [("row", bit) for bit in reversed(range(row_bits))]
    value = value.reshape((2,) * len(names) + value.shape[2:])
    upward = [("row", bit) for bit in range(row_bits)]
    width = value.shape[-1] // 2
    left = halve_all(value[..., :width], names, upward)
    right = halve_all(value[..., width:], names, upward[::-1])
    names = names[: frame_bits - 1]
    value = jnp.concatenate([left, right], axis=-1)
    return halve_all(value, names, [("frame", bit) for bit in range(1, frame_bits)])


def split_two(value):
    high = value.astype(jnp.bfloat16)
    return high, (value - high.astype(jnp.float32)).astype(jnp.bfloat16)


def dot_low(left, right):
    return lax.dot_general(left, right, (((1,), (0,)), ((), ())), preferred_element_type=jnp.float32)


def newton_kernel(all_ref, mine_ref, out_ref, a_ref, q_ref, t_ref, ah, al, nh, nl, th, tl, qh, ql):
    width = a_ref.shape[0]
    rows = 256
    steps = width // rows
    depth = all_ref.shape[0]

    def block(index):
        return pl.ds(pl.multiple_of(index * rows, rows), rows)

    def gram(index, total):
        columns = block(index)

        def part(k, value):
            deep = pl.ds(pl.multiple_of(k * 1024, 1024), 1024)
            return value + lax.dot_general(
                all_ref[deep, columns],
                all_ref[deep, :],
                (((0,), (0,)), ((), ())),
                preferred_element_type=jnp.float32,
            )

        value = lax.fori_loop(0, depth // 1024, part, jnp.zeros((rows, width), jnp.float32))
        a_ref[columns, :] = value
        row_at = lax.broadcasted_iota(jnp.int32, (rows, width), 0) + index * rows
        column_at = lax.broadcasted_iota(jnp.int32, (rows, width), 1)
        return total + jnp.sum(jnp.where(row_at == column_at, value, 0.0))

    squares = 0.0
    for index in range(steps):
        squares = gram(index, squares)
    squares = jnp.full((1, 1), squares, jnp.float32)
    inverse = 1.0 / (jnp.sqrt(squares) + 1e-07)

    def first_split(index, carry):
        at = block(index)
        value = a_ref[at, :] * inverse * inverse
        a_ref[at, :] = value
        high, rest = split_two(value)
        ah[at, :] = high
        al[at, :] = rest
        return carry

    lax.fori_loop(0, steps, first_split, 0)

    def three(lh, ll, rh, rl):
        return dot_low(lh, rh) + dot_low(lh, rl) + dot_low(ll, rh)

    def one_step(number, exact, last):
        def make_n(index, carry):
            at = block(index)
            if exact:
                square = three(ah[at, :], al[at, :], ah[...], al[...])
            else:
                square = dot_low(ah[at, :], ah[...])
            value = newton_two * a_ref[at, :] + newton_three * square
            high, rest = split_two(value)
            nh[at, :] = high
            if exact:
                nl[at, :] = rest
            return carry

        lax.fori_loop(0, steps, make_n, 0)

        def make_q(index, carry):
            at = block(index)
            if number == 0:
                row_at = lax.broadcasted_iota(jnp.int32, (rows, width), 0) + index * rows
                column_at = lax.broadcasted_iota(jnp.int32, (rows, width), 1)
                value = nh[at, :].astype(jnp.float32) + jnp.where(row_at == column_at, newton_one, 0.0)
            elif exact:
                value = newton_one * q_ref[at, :] + three(qh[at, :], ql[at, :], nh[...], nl[...])
            else:
                value = newton_one * q_ref[at, :] + dot_low(qh[at, :], nh[...]) + dot_low(ql[at, :], nh[...])
            q_ref[at, :] = value
            high, rest = split_two(value)
            qh[at, :] = high
            ql[at, :] = rest
            return carry

        lax.fori_loop(0, steps, make_q, 0)
        if last:
            return

        def make_t(index, carry):
            at = block(index)
            if exact:
                value = newton_one * a_ref[at, :] + three(ah[at, :], al[at, :], nh[...], nl[...])
            else:
                value = newton_one * a_ref[at, :] + dot_low(ah[at, :], nh[...]) + dot_low(al[at, :], nh[...])
            t_ref[at, :] = value
            high, rest = split_two(value)
            th[at, :] = high
            tl[at, :] = rest
            return carry

        lax.fori_loop(0, steps, make_t, 0)

        def make_a(index, carry):
            at = block(index)
            if exact:
                value = newton_one * t_ref[at, :] + three(nh[at, :], nl[at, :], th[...], tl[...])
            else:
                value = newton_one * t_ref[at, :] + dot_low(nh[at, :], th[...]) + dot_low(nh[at, :], tl[...])
            a_ref[at, :] = value
            high, rest = split_two(value)
            ah[at, :] = high
            al[at, :] = rest
            return carry

        lax.fori_loop(0, steps, make_a, 0)

    for number in range(5):
        one_step(number, number >= 2, number == 4)

    mine = mine_ref[...]
    out_ref[...] = ((dot_low(mine, qh[...]) + dot_low(mine, ql[...])) * inverse).astype(out_ref.dtype)


def newton(everything, mine):
    width = everything.shape[1]
    full = pltpu.VMEM((width, width), jnp.float32)
    low = pltpu.VMEM((width, width), jnp.bfloat16)
    return pl.pallas_call(
        newton_kernel,
        out_shape=jax.ShapeDtypeStruct(mine.shape, jnp.bfloat16),
        in_specs=[pl.BlockSpec(memory_space=pltpu.VMEM)] * 2,
        out_specs=pl.BlockSpec(memory_space=pltpu.VMEM),
        scratch_shapes=[full] * 3 + [low] * 8,
        compiler_params=pltpu.CompilerParams(vmem_limit_bytes=52 * 1024 * 1024),
        cost_estimate=pl.CostEstimate(flops=110 * 10**9, bytes_accessed=12 * 10**6, transcendentals=0),
    )(everything, mine)


def dot_nt(left, right):
    return lax.dot_general(left, right, (((1,), (1,)), ((), ())), preferred_element_type=jnp.float32)


def dot_tn(left, right):
    return lax.dot_general(left, right, (((0,), (0,)), ((), ())), preferred_element_type=jnp.float32)


MIB = 1024 * 1024


def vmem_params(mib, semantics=None):
    return pltpu.CompilerParams(vmem_limit_bytes=mib * MIB, dimension_semantics=semantics)


def whole_spec(array):
    zeros = (0,) * array.ndim
    return pl.BlockSpec(array.shape, lambda *_: zeros, pipeline_mode=pl.Buffered(1))


def turned(value, cosine, sine):
    even = lax.broadcasted_iota(jnp.int32, value.shape, 1) % 2 == 0
    width = value.shape[1]
    swapped = jnp.where(even, pltpu.roll(value, width - 1, 1), pltpu.roll(value, 1, 1))
    return value * cosine + swapped * sine


def framed(value, frames):
    rows, width = value.shape
    return value.reshape(frames, rows // frames, width)


def norm_parts(value):
    mean = jnp.mean(value, axis=-1, keepdims=True)
    centered = value - mean
    root = lax.rsqrt(jnp.mean(centered * centered, axis=-1, keepdims=True) + norm_floor)
    return centered * root, root


def project_kernel(slots, me_ref, x_ref, mod_ref, cos_ref, sin_ref, w_ref, hid_ref, *out_refs):
    frames = mod_ref.shape[1]
    group = D // slots
    normed, _ = norm_parts(x_ref[0].astype(jnp.float32))
    normed = framed(normed, frames)
    shift = mod_ref[0, :, 0:D][:, None, :]
    scaling = mod_ref[0, :, D : 2 * D][:, None, :]
    hidden = (normed * (1.0 + scaling) + shift).reshape(x_ref.shape[1], D).astype(jnp.bfloat16)
    hid_ref[0] = hidden
    cosine = cos_ref[...]
    sine = sin_ref[...]
    me = me_ref[0]
    for slot in range(slots):
        peer = me ^ slot
        for part in range(3):
            rows = pl.ds(pl.multiple_of(part * D + peer * group, group), group)
            value = dot_nt(hidden, w_ref[rows, :])
            if part == 2:
                out_refs[slot][part] = value.astype(jnp.bfloat16)
                continue
            for first in range(0, group, 128):
                piece = turned(value[:, first : first + 128], cosine, sine)
                if part == 0:
                    piece = piece * (1.0 / math.sqrt(HD))
                out_refs[slot][part, :, first : first + 128] = piece.astype(jnp.bfloat16)


def project(me, clip, tokens, mod, cosine, sine, w_qkv, slots):
    count, tall_rows, _ = tokens.shape
    tile = 256
    steps = tall_rows // tile
    group = D // slots
    out_shape = [jax.ShapeDtypeStruct((1, tall_rows, D), jnp.bfloat16)]
    out_shape += [jax.ShapeDtypeStruct((3, tall_rows, group), jnp.bfloat16)] * slots
    return pl.pallas_call(
        functools.partial(project_kernel, slots),
        grid=(steps,),
        in_specs=[
            pl.BlockSpec(memory_space=pltpu.SMEM),
            pl.BlockSpec((1, tile, D), lambda i: (clip, i, 0)),
            pl.BlockSpec((1, mod.shape[1], 6 * D), lambda i: (clip * steps + i, 0, 0)),
            pl.BlockSpec((tile, 128), lambda i: (clip * steps + i, 0)),
            pl.BlockSpec((tile, 128), lambda i: (clip * steps + i, 0)),
            whole_spec(w_qkv),
        ],
        out_specs=[pl.BlockSpec((1, tile, D), lambda i: (0, i, 0))]
        + [pl.BlockSpec((3, tile, group), lambda i: (0, i, 0))] * slots,
        out_shape=out_shape,
        compiler_params=vmem_params(48),
        cost_estimate=pl.CostEstimate(
            flops=6 * tall_rows * D * D, bytes_accessed=10 * MIB, transcendentals=0
        ),
        name="project",
    )(me, tokens, mod, cosine, sine, w_qkv)


def head_mask(shape, head, axis):
    return lax.broadcasted_iota(jnp.int32, shape, axis) // HD == head


def attend_kernel(slots, tile, *refs):
    ins, outs = refs[:slots], refs[slots : 2 * slots]
    full_ref, log_ref, qs, ks, vs = refs[2 * slots :]
    length = ins[0].shape[1]
    for slot in range(slots):
        rows = slice(slot * length, (slot + 1) * length)
        qs[rows, :] = ins[slot][0]
        ks[rows, :] = ins[slot][1]
        vs[rows, :] = ins[slot][2]

    def one(index, carry):
        rows = pl.ds(pl.multiple_of(index * tile, tile), tile)
        query = qs[rows, :]
        first = head_mask((tile, 128), 0, 1)
        parts = []
        logs = []
        for head in range(2):
            masked = jnp.where(first if head == 0 else ~first, query, jnp.zeros_like(query))
            scores = dot_nt(masked, ks[...])
            top = jnp.max(scores, axis=-1, keepdims=True)
            raised = jnp.exp(scores - top)
            total = jnp.sum(raised, axis=-1, keepdims=True)
            parts.append(dot_low(raised.astype(jnp.bfloat16), vs[...]) * (1.0 / total))
            logs.append(top + jnp.log(total))
        full_ref[rows, :] = jnp.where(first, parts[0], parts[1])
        log_ref[rows, :] = jnp.where(first, logs[0], logs[1])
        return carry

    lax.fori_loop(0, slots * length // tile, one, 0)
    for slot in range(slots):
        rows = slice(slot * length, (slot + 1) * length)
        outs[slot][...] = full_ref[rows, :].astype(jnp.bfloat16)


def attend(pieces):
    slots = len(pieces)
    _, length, group = pieces[0].shape
    total = slots * length
    scratch = pltpu.VMEM((total, 128), jnp.bfloat16)
    outs = pl.pallas_call(
        functools.partial(attend_kernel, slots, 256),
        grid=(group // 128,),
        in_specs=[pl.BlockSpec((3, length, 128), lambda i: (0, 0, i))] * slots,
        out_specs=[pl.BlockSpec((length, 128), lambda i: (0, i))] * slots
        + [pl.BlockSpec((total, 128), lambda i: (0, i))] * 2,
        out_shape=[jax.ShapeDtypeStruct((length, group), jnp.bfloat16)] * slots
        + [jax.ShapeDtypeStruct((total, group), jnp.float32)] * 2,
        scratch_shapes=[scratch] * 3,
        compiler_params=vmem_params(48),
        cost_estimate=pl.CostEstimate(
            flops=16 * total * total * group, bytes_accessed=8 * MIB, transcendentals=total * total * 4
        ),
        name="attend",
    )(*pieces)
    return outs[:slots], outs[slots], outs[slots + 1]


def attend_back_kernel(slots, tile, *refs):
    ins, grads = refs[:slots], refs[slots : 2 * slots]
    full_ref, log_ref = refs[2 * slots : 2 * slots + 2]
    outs = refs[2 * slots + 2 : 3 * slots + 2]
    qs, ks, vs, gs, q_turned, g_turned, dq, dk, dv = refs[3 * slots + 2 :]
    length = ins[0].shape[1]
    total = slots * length
    for slot in range(slots):
        rows = slice(slot * length, (slot + 1) * length)
        qs[rows, :] = ins[slot][0]
        ks[rows, :] = ins[slot][1]
        vs[rows, :] = ins[slot][2]
        gs[rows, :] = grads[slot][...]
        q_turned[:, rows] = ins[slot][0].T
        g_turned[:, rows] = grads[slot][...].T
    dk[...] = jnp.zeros_like(dk)
    dv[...] = jnp.zeros_like(dv)

    def one(index, carry):
        rows = pl.ds(pl.multiple_of(index * tile, tile), tile)
        first = head_mask((tile, 128), 0, 1)
        upper = head_mask((128, tile), 0, 0)
        query, grad = qs[rows, :], gs[rows, :]
        query_t, grad_t = q_turned[:, rows], g_turned[:, rows]
        product = grad.astype(jnp.float32) * full_ref[rows, :]
        masks = (first, ~first)
        masks_t = (upper, ~upper)
        zero = jnp.zeros_like(query)
        zero_t = jnp.zeros_like(query_t)
        q_low = [jnp.where(mask, query, zero) for mask in masks]
        g_low = [jnp.where(mask, grad, zero) for mask in masks]
        qt_low = [jnp.where(mask, query_t, zero_t) for mask in masks_t]
        gt_low = [jnp.where(mask, grad_t, zero_t) for mask in masks_t]
        inner = [jnp.sum(jnp.where(mask, product, 0.0), axis=-1, keepdims=True) for mask in masks]
        logs = [log_ref[rows, 0:1], log_ref[rows, HD : HD + 1]]

        def inside(k_index, sums):
            at = pl.ds(pl.multiple_of(k_index * tile, tile), tile)
            key, value = ks[at, :], vs[at, :]
            out = []
            for head in range(2):
                probs = jnp.exp(dot_nt(q_low[head], key) - logs[head])
                d_probs = dot_nt(g_low[head], value)
                d_scores = (probs * (d_probs - inner[head])).astype(jnp.bfloat16)
                dv[:, at] += dot_low(gt_low[head], probs.astype(jnp.bfloat16))
                dk[:, at] += dot_low(qt_low[head], d_scores)
                out.append(sums[head] + dot_low(d_scores, key))
            return tuple(out)

        start = jnp.zeros((tile, 128), jnp.float32)
        sums = lax.fori_loop(0, total // tile, inside, (start, start))
        dq[rows, :] = (jnp.where(first, sums[0], sums[1]) * (1.0 / math.sqrt(HD))).astype(jnp.bfloat16)
        return carry

    lax.fori_loop(0, total // tile, one, 0)
    for slot in range(slots):
        rows = slice(slot * length, (slot + 1) * length)
        outs[slot][0] = dq[rows, :]
        outs[slot][1] = dk[:, rows].T.astype(jnp.bfloat16)
        outs[slot][2] = dv[:, rows].T.astype(jnp.bfloat16)


def attend_back(pieces, grads, full, logs):
    slots = len(pieces)
    _, length, group = pieces[0].shape
    total = slots * length
    low = pltpu.VMEM((total, 128), jnp.bfloat16)
    low_t = pltpu.VMEM((128, total), jnp.bfloat16)
    full_t = pltpu.VMEM((128, total), jnp.float32)
    return pl.pallas_call(
        functools.partial(attend_back_kernel, slots, 512),
        grid=(group // 128,),
        in_specs=[pl.BlockSpec((3, length, 128), lambda i: (0, 0, i))] * slots
        + [pl.BlockSpec((length, 128), lambda i: (0, i))] * slots
        + [pl.BlockSpec((total, 128), lambda i: (0, i))] * 2,
        out_specs=[pl.BlockSpec((3, length, 128), lambda i: (0, 0, i))] * slots,
        out_shape=[jax.ShapeDtypeStruct((3, length, group), jnp.bfloat16)] * slots,
        scratch_shapes=[low] * 4 + [low_t] * 2 + [low] + [full_t] * 2,
        compiler_params=vmem_params(48),
        cost_estimate=pl.CostEstimate(
            flops=40 * total * total * group, bytes_accessed=12 * MIB, transcendentals=total * total * 4
        ),
        name="attend_back",
    )(*pieces, *grads, full, logs)


def middle_kernel(slots, me_ref, x_ref, cot_ref, mod_ref, wo_ref, wu_ref, wd_ref, *refs):
    att_refs = refs[:slots]
    datt_refs = refs[slots : 2 * slots]
    (
        out_ref,
        att_ref,
        h2_ref,
        act_ref,
        db2_ref,
        dup_ref,
        db1_ref,
        dmid_ref,
        sums_ref,
        slope,
    ) = refs[2 * slots :]
    frames = mod_ref.shape[1]
    rows = x_ref.shape[1]
    group = D // slots
    me = me_ref[0]

    def mod(index):
        return mod_ref[0, :, index * D : (index + 1) * D][:, None, :]

    def spread(value, index, plus=0.0):
        return (framed(value, frames) * (mod(index) + plus)).reshape(rows, D)

    def frame_sum(value):
        return jnp.sum(framed(value, frames), axis=1)

    branch = jnp.zeros((rows, D), jnp.float32)
    for slot in range(slots):
        at = pl.ds(pl.multiple_of((me ^ slot) * group, group), group)
        piece = att_refs[slot][...]
        att_ref[:, at] = piece
        branch += dot_low(piece, wo_ref[at, :])
    middle = x_ref[0].astype(jnp.float32) + spread(branch, 2)
    normed, root = norm_parts(middle)
    hidden = (framed(spread(normed, 4, 1.0), frames) + mod(3)).reshape(rows, D).astype(jnp.bfloat16)
    h2_ref[...] = hidden
    wide = 1024
    curve = math.sqrt(2.0 / math.pi)
    branch_two = jnp.zeros((rows, D), jnp.float32)
    for first in range(0, FF, wide):
        cut = slice(first, first + wide)
        up = dot_nt(hidden, wu_ref[cut, :])
        square = up * up
        bent = jnp.tanh(curve * up * (1.0 + 0.044715 * square))
        half = 0.5 * (1.0 + bent)
        active = (up * half).astype(jnp.bfloat16)
        slope[:, cut] = half + 0.5 * up * (1.0 - bent * bent) * (curve * (1.0 + 3 * 0.044715 * square))
        act_ref[:, cut] = active
        branch_two += dot_low(active, wd_ref[cut, :])
    cot = cot_ref[0].astype(jnp.float32)
    out_ref[0] = (middle + spread(branch_two, 5)).astype(jnp.bfloat16)
    sums_ref[0, 3] = frame_sum(cot * branch_two)
    d_branch_two = spread(cot, 5).astype(jnp.bfloat16)
    db2_ref[...] = d_branch_two
    d_hidden = jnp.zeros((rows, D), jnp.float32)
    for first in range(0, FF, wide):
        cut = slice(first, first + wide)
        d_up = (dot_nt(d_branch_two, wd_ref[cut, :]) * slope[:, cut]).astype(jnp.bfloat16)
        dup_ref[:, cut] = d_up
        d_hidden += dot_low(d_up, wu_ref[cut, :])
    sums_ref[0, 1] = frame_sum(d_hidden)
    sums_ref[0, 2] = frame_sum(d_hidden * normed)
    inner = spread(d_hidden, 4, 1.0)
    d_middle = cot + root * (
        inner
        - jnp.mean(inner, axis=-1, keepdims=True)
        - normed * jnp.mean(inner * normed, axis=-1, keepdims=True)
    )
    dmid_ref[...] = d_middle
    sums_ref[0, 0] = frame_sum(d_middle * branch)
    d_branch = spread(d_middle, 2).astype(jnp.bfloat16)
    db1_ref[...] = d_branch
    for slot in range(slots):
        at = pl.ds(pl.multiple_of((me ^ slot) * group, group), group)
        datt_refs[slot][...] = dot_nt(d_branch, wo_ref[at, :]).astype(jnp.bfloat16)


def middle(me, clip, tokens, cotangent, mod, w_out, w_up, w_down, attended):
    slots = len(attended)
    count, length, _ = tokens.shape
    tile = 256
    steps = length // tile
    group = D // slots
    frames = mod.shape[1]
    low = jnp.bfloat16

    def flat(width, kind=low):
        return jax.ShapeDtypeStruct((length, width), kind)

    def flat_spec(width):
        return pl.BlockSpec((tile, width), lambda i: (i, 0))

    outs = pl.pallas_call(
        functools.partial(middle_kernel, slots),
        grid=(steps,),
        in_specs=[
            pl.BlockSpec(memory_space=pltpu.SMEM),
            pl.BlockSpec((1, tile, D), lambda i: (clip, i, 0)),
            pl.BlockSpec((1, tile, D), lambda i: (clip, i, 0)),
            pl.BlockSpec((1, frames, 6 * D), lambda i: (clip * steps + i, 0, 0)),
            whole_spec(w_out),
            whole_spec(w_up),
            whole_spec(w_down),
        ]
        + [flat_spec(group)] * slots,
        out_specs=[flat_spec(group)] * slots
        + [pl.BlockSpec((1, tile, D), lambda i: (0, i, 0))]
        + [flat_spec(width) for width in (D, D, FF, D, FF, D, D)]
        + [pl.BlockSpec((1, 4, frames, D), lambda i: (i, 0, 0, 0))],
        out_shape=[flat(group)] * slots
        + [jax.ShapeDtypeStruct((1, length, D), low)]
        + [flat(D), flat(D), flat(FF), flat(D), flat(FF), flat(D), flat(D, jnp.float32)]
        + [jax.ShapeDtypeStruct((steps, 4, frames, D), jnp.float32)],
        scratch_shapes=[pltpu.VMEM((tile, FF), jnp.float32)],
        compiler_params=vmem_params(58),
        cost_estimate=pl.CostEstimate(
            flops=2 * length * D * (2 * D + 4 * FF), bytes_accessed=40 * MIB, transcendentals=length * FF
        ),
        name="middle",
    )(me, tokens, cotangent, mod, w_out, w_up, w_down, *attended)
    return outs[:slots], outs[slots:]


def last_kernel(slots, me_ref, x_ref, mod_ref, cos_ref, sin_ref, w_ref, dmid_ref, *refs):
    pieces = refs[:slots]
    dproj_ref, grad_ref, sums_ref = refs[slots:]
    frames = mod_ref.shape[1]
    rows = x_ref.shape[1]
    group = D // slots
    me = me_ref[0]
    cosine = cos_ref[...]
    sine = -sin_ref[...]
    d_hidden = jnp.zeros((rows, D), jnp.float32)
    for slot in range(slots):
        peer = me ^ slot
        for part in range(3):
            base = pl.multiple_of(part * D + peer * group, group)
            if part == 2:
                value = pieces[slot][part]
            else:
                value = jnp.concatenate(
                    [
                        turned(pieces[slot][part, :, at : at + 128].astype(jnp.float32), cosine, sine)
                        for at in range(0, group, 128)
                    ],
                    axis=1,
                ).astype(jnp.bfloat16)
            dproj_ref[:, pl.ds(base, group)] = value
            d_hidden += dot_low(value, w_ref[pl.ds(base, group), :])
    normed, root = norm_parts(x_ref[0].astype(jnp.float32))
    scaling = mod_ref[0, :, D : 2 * D][:, None, :]
    sums_ref[0, 0] = jnp.sum(framed(d_hidden, frames), axis=1)
    sums_ref[0, 1] = jnp.sum(framed(d_hidden * normed, frames), axis=1)
    inner = (framed(d_hidden, frames) * (1.0 + scaling)).reshape(rows, D)
    grad_ref[0] = dmid_ref[...] + root * (
        inner
        - jnp.mean(inner, axis=-1, keepdims=True)
        - normed * jnp.mean(inner * normed, axis=-1, keepdims=True)
    )


def last(me, clip, tokens, mod, cosine, sine, w_qkv, d_middle, pieces):
    slots = len(pieces)
    count, length, _ = tokens.shape
    tile = 256
    steps = length // tile
    group = D // slots
    frames = mod.shape[1]
    return pl.pallas_call(
        functools.partial(last_kernel, slots),
        grid=(steps,),
        in_specs=[
            pl.BlockSpec(memory_space=pltpu.SMEM),
            pl.BlockSpec((1, tile, D), lambda i: (clip, i, 0)),
            pl.BlockSpec((1, frames, 6 * D), lambda i: (clip * steps + i, 0, 0)),
            pl.BlockSpec((tile, 128), lambda i: (clip * steps + i, 0)),
            pl.BlockSpec((tile, 128), lambda i: (clip * steps + i, 0)),
            whole_spec(w_qkv),
            pl.BlockSpec((tile, D), lambda i: (i, 0)),
        ]
        + [pl.BlockSpec((3, tile, group), lambda i: (0, i, 0))] * slots,
        out_specs=[
            pl.BlockSpec((tile, 3 * D), lambda i: (i, 0)),
            pl.BlockSpec((1, tile, D), lambda i: (0, i, 0)),
            pl.BlockSpec((1, 2, frames, D), lambda i: (i, 0, 0, 0)),
        ],
        out_shape=[
            jax.ShapeDtypeStruct((length, 3 * D), jnp.bfloat16),
            jax.ShapeDtypeStruct((1, length, D), jnp.float32),
            jax.ShapeDtypeStruct((steps, 2, frames, D), jnp.float32),
        ],
        compiler_params=vmem_params(48),
        cost_estimate=pl.CostEstimate(
            flops=6 * length * D * D, bytes_accessed=20 * MIB, transcendentals=0
        ),
        name="last",
    )(me, tokens, mod, cosine, sine, w_qkv, d_middle, *pieces)


def weight_kernel(doubled, split_ref, *refs):
    members = len(doubled)
    out_ref = refs[-1]
    first = 0
    for member in range(members):
        left = refs[4 * member : 4 * member + 2]
        right = refs[4 * member + 2 : 4 * member + 4]
        value = dot_tn(left[0][...], right[0][...]) + dot_tn(left[1][...], right[1][...])
        if doubled[member]:
            half = value.shape[0] // 2
            value = jnp.where(split_ref[0] == 0, value[:half], value[half:])
        height = value.shape[0] // out_ref.shape[1]
        out_ref[0, :, first : first + height, :] = value.reshape(
            out_ref.shape[1], height, value.shape[1]
        ).astype(out_ref.dtype)
        first += height


def weight_sums(keep, pairs, kind, name):
    frame_devices = lax.axis_size("frame")
    row_devices = lax.axis_size("row")
    specs, operands, doubled = [], [], []
    height = 0
    for left, right in pairs:
        width = left[0].shape[1] // frame_devices
        height += width // row_devices
        doubled.append(width % 128 != 0)
        if doubled[-1]:
            spec = pl.BlockSpec((left[0].shape[0], 2 * width), lambda i, s: (0, i))
        else:
            spec = pl.BlockSpec((left[0].shape[0], width), lambda i, s: (0, 2 * i + s[0]))
        specs += [spec] * 2
        specs += [pl.BlockSpec(right[0].shape, lambda i, s: (0, 0))] * 2
        operands += [*left, *right]
    flops = sum(4 * left[0].shape[0] * left[0].shape[1] * D // 2 for left, _ in pairs)
    return pl.pallas_call(
        functools.partial(weight_kernel, tuple(doubled)),
        grid_spec=pltpu.PrefetchScalarGridSpec(
            num_scalar_prefetch=1,
            grid=(frame_devices // 2,),
            in_specs=specs,
            out_specs=pl.BlockSpec((1, row_devices, height, D), lambda i, s: (i, 0, 0, 0)),
        ),
        out_shape=jax.ShapeDtypeStruct((frame_devices // 2, row_devices, height, D), kind),
        compiler_params=vmem_params(48),
        cost_estimate=pl.CostEstimate(flops=flops, bytes_accessed=30 * MIB, transcendentals=0),
        name=name,
    )(keep, *operands)


def swap(slots):
    size = lax.axis_size("row")
    out = [slots[0]]
    for slot in range(1, size):
        out.append(lax.ppermute(slots[slot], "row", [(index, index ^ slot) for index in range(size)]))
    return out


def per_device(
    tokens,
    cotangent,
    noise_levels,
    frame_times,
    step_count,
    qkv_master,
    qkv_momentum,
    out_master,
    out_momentum,
    up_master,
    up_momentum,
    down_master,
    down_momentum,
    ada_master,
    ada_first,
    ada_second,
    table_master,
    table_first,
    table_second,
    bias_master,
    bias_first,
    bias_second,
):
    low_type = jnp.bfloat16
    full_type = jnp.float32
    clip_count, frames, rows_dev, columns, model_width = tokens.shape
    seq_local = frames * rows_dev * columns
    row_devices = lax.axis_size("row")
    token_total = clip_count * seq_local
    frame_total = clip_count * frames
    shape_five = (clip_count, frames, rows_dev, columns, model_width)
    w_table, w_ada, w_bias = (
        lax.all_gather(table_master.astype(low_type), ("frame", "row"), axis=0, tiled=True),
        lax.all_gather(ada_master.astype(low_type), ("frame", "row"), axis=1, tiled=True),
        lax.all_gather(bias_master.astype(low_type), ("frame", "row"), axis=0, tiled=True),
    )
    w_qkv, w_out, w_up, w_down = (
        lax.all_gather(item.astype(low_type), ("frame", "row"), axis=0, tiled=True)
        for item in (qkv_master.T, out_master, up_master.T, down_master)
    )
    level_flat = noise_levels.reshape(frame_total)
    level_hot = (
        level_flat[:, None] == jnp.arange(w_table.shape[0], dtype=jnp.int32)[None, :]
    ).astype(low_type)
    embedded = jnp.dot(level_hot, w_table, preferred_element_type=full_type)
    cond_low = jax.nn.silu(embedded).astype(low_type)
    modulation = jnp.dot(cond_low, w_ada, preferred_element_type=full_type) + w_bias.astype(
        full_type
    )
    grid_shape = (clip_count, frames, rows_dev, columns)
    row_first = lax.axis_index("row") * rows_dev
    time_grid = jnp.broadcast_to(frame_times.astype(full_type)[:, :, None, None], grid_shape)
    row_grid = jnp.broadcast_to(
        (row_first + jnp.arange(rows_dev, dtype=jnp.int32)).astype(full_type)[None, None, :, None],
        grid_shape,
    )
    column_grid = jnp.broadcast_to(
        jnp.arange(columns, dtype=jnp.int32).astype(full_type)[None, None, None, :], grid_shape
    )
    angles = rotary_angles(time_grid, row_grid, column_grid).reshape(clip_count, seq_local, HD // 2)
    flat_angles = angles.reshape(token_total, HD // 2)
    pair_sign = jnp.tile(jnp.array([-1.0, 1.0], full_type), HD)
    cosine = jnp.tile(jnp.repeat(jnp.cos(flat_angles), 2, axis=1), (1, 2))
    sine = jnp.tile(jnp.repeat(jnp.sin(flat_angles), 2, axis=1), (1, 2)) * pair_sign
    tile_count = token_total // 256
    mod = modulation.reshape(tile_count, frame_total // tile_count, 6 * model_width)
    me = lax.axis_index("row").astype(jnp.int32).reshape(1)
    tokens_flat = tokens.reshape(clip_count, seq_local, model_width)
    cotangent_flat = cotangent.reshape(clip_count, seq_local, model_width)
    clips = range(clip_count)
    hidden_one, pieces = [], []
    for clip in clips:
        hidden, *slots = project(me, clip, tokens_flat, mod, cosine, sine, w_qkv, row_devices)
        hidden_one.append(hidden[0])
        pieces.append(swap(slots))
    attended, full, logs = [], [], []
    for clip in clips:
        slots, full_clip, log_clip = attend(pieces[clip])
        attended.append(swap(slots))
        full.append(full_clip)
        logs.append(log_clip)
    d_attended, middles = [], []
    for clip in clips:
        slots, others = middle(
            me, clip, tokens_flat, cotangent_flat, mod, w_out, w_up, w_down, attended[clip]
        )
        d_attended.append(swap(slots))
        middles.append(others)
    block_out = jnp.concatenate([item[0] for item in middles], axis=0).reshape(shape_five)
    att_low, hidden_two, activated, d_branch_two, d_up, d_branch_one, d_middle, two_sums = (
        [item[index] for item in middles] for index in range(1, 9)
    )
    early = scatter_sum(
        [(activated, d_branch_two), (d_up, hidden_two), (att_low, d_branch_one)], "early"
    )
    d_pieces = [
        swap(attend_back(pieces[clip], d_attended[clip], full[clip], logs[clip])) for clip in clips
    ]
    lasts = [
        last(me, clip, tokens_flat, mod, cosine, sine, w_qkv, d_middle[clip], d_pieces[clip])
        for clip in clips
    ]
    input_grad = jnp.concatenate([item[1] for item in lasts], axis=0).reshape(shape_five)
    g_qkv = scatter_sum([([item[0] for item in lasts], hidden_one)], "late")

    def frames_of(sums, index):
        return jnp.concatenate([item[:, index].reshape(frames, model_width) for item in sums], axis=0)

    one_sums = [item[2] for item in lasts]
    d_modulation = jnp.concatenate(
        [frames_of(one_sums, 0), frames_of(one_sums, 1)] + [frames_of(two_sums, index) for index in range(4)],
        axis=1,
    )
    frame_devices = lax.axis_size("frame")
    device_total = frame_devices * row_devices
    both = ("frame", "row")
    levels_all = lax.all_gather(level_flat, "frame", axis=0, tiled=True)
    embedded_all = lax.all_gather(embedded.astype(low_type), "frame", axis=0, tiled=True).astype(
        full_type
    )
    cond_all = jax.nn.silu(embedded_all).astype(low_type)
    ada_width = ada_master.shape[1]
    mod_parts = lax.all_to_all(
        jnp.moveaxis(d_modulation.reshape(frame_total, device_total, ada_width), 1, 0),
        both,
        split_axis=0,
        concat_axis=0,
        tiled=True,
    )
    mod_mine = (
        jnp.sum(mod_parts.reshape(frame_devices, row_devices, frame_total, ada_width), axis=1)
        .reshape(frame_devices * frame_total, ada_width)
        .astype(low_type)
    )
    g_ada = jnp.einsum("fd,fe->de", cond_all, mod_mine, preferred_element_type=full_type)
    g_bias = jnp.sum(mod_mine.astype(full_type), axis=0)
    d_cond = lax.psum(
        jnp.einsum("fe,de->fd", mod_mine, ada_master.astype(low_type), preferred_element_type=full_type),
        both,
    )
    d_embedded = jax.vjp(jax.nn.silu, embedded_all)[1](d_cond)[0]
    device_index = lax.axis_index("frame") * row_devices + lax.axis_index("row")
    level_rows = table_master.shape[0]
    hot_mine = (
        levels_all[None, :]
        == (device_index * level_rows + jnp.arange(level_rows, dtype=jnp.int32))[:, None]
    ).astype(full_type)
    g_table = jnp.dot(hot_mine, d_embedded, precision=highest)
    heights = (qkv_master.shape[1], out_master.shape[0], up_master.shape[1], down_master.shape[0])
    g_down = early[: heights[3]]
    g_up = early[heights[3] : heights[3] + heights[2]]
    g_out = early[heights[3] + heights[2] :]
    muon_grads = (g_qkv, g_out, g_up, g_down)
    flipped = (True, False, True, False)

    def tall(value, member):
        return value.T if flipped[member] else value

    muon_moments = (qkv_momentum, out_momentum, up_momentum, down_momentum)
    muon_masters = (qkv_master, out_master, up_master, down_master)
    factors = (math.sqrt(3.0), 1.0, math.sqrt(FF / D), math.sqrt(FF / D))
    adam_local = jnp.sum(g_ada * g_ada) + jnp.sum(g_table * g_table) + jnp.sum(g_bias * g_bias)
    local_total = adam_local + sum((jnp.sum(item * item) for item in muon_grads))
    norm_value = jnp.sqrt(lax.psum(local_total, both))
    clip_factor = jnp.minimum(1.0, clip_limit / (norm_value + 1e-06))
    moments_new = []
    pieces = []
    slot = max(heights)
    for member in range(4):
        clipped = clip_factor * muon_grads[member]
        moment = momentum_decay * tall(muon_moments[member], member) + clipped
        update = (clipped + momentum_decay * moment).astype(low_type)
        moments_new.append(tall(moment, member))
        pieces.append(jnp.pad(update, ((0, slot - heights[member]), (0, 0))))
    slab = jnp.stack(pieces * (row_devices // 4))
    updates = lax.all_to_all(slab, "row", split_axis=0, concat_axis=0, tiled=True).reshape(
        row_devices * slot, model_width
    )
    everything = lax.all_gather(updates, "frame", axis=0, tiled=True)
    ortho_rows = newton(everything, updates).reshape(row_devices, slot, model_width)
    ortho_mine = lax.all_to_all(ortho_rows, "row", split_axis=0, concat_axis=0, tiled=True)
    blocks = [tall(ortho_mine[member, : heights[member]].astype(full_type), member) for member in range(4)]
    masters_new = []
    for member in range(4):
        ortho = blocks[member]
        masters_new.append(
            muon_masters[member] * (1.0 - muon_rate * weight_decay)
            - muon_rate * factors[member] * ortho
        )
    step_value = step_count.astype(full_type)[0]
    ada_first_new, ada_second_new, ada_master_new = adam_update(
        g_ada, ada_first, ada_second, ada_master, 0.03, clip_factor, step_value
    )
    table_clipped = clip_factor * g_table
    table_first_new, table_second_new, table_master_new = adam_update(
        g_table, table_first, table_second, table_master, 0.5, clip_factor, step_value
    )
    bias_first_new, bias_second_new, bias_master_new = adam_update(
        g_bias, bias_first, bias_second, bias_master, 0.5, clip_factor, step_value
    )
    return (
        block_out,
        input_grad,
        norm_value.reshape(1),
        moments_new[0],
        masters_new[0],
        moments_new[1],
        masters_new[1],
        moments_new[2],
        masters_new[2],
        moments_new[3],
        masters_new[3],
        ada_first_new,
        ada_second_new,
        ada_master_new,
        table_first_new,
        table_clipped,
        table_master_new,
        bias_first_new,
        bias_second_new,
        bias_master_new,
    )


def solution(mesh):
    return jax.shard_map(
        per_device,
        mesh=mesh,
        in_specs=(
            P("frame", None, "row", None, None),
            P("frame", None, "row", None, None),
            P("frame", None),
            P("frame", None),
            P(),
            P(None, ("frame", "row")),
            P(None, ("frame", "row")),
            P(("frame", "row"), None),
            P(("frame", "row"), None),
            P(None, ("frame", "row")),
            P(None, ("frame", "row")),
            P(("frame", "row"), None),
            P(("frame", "row"), None),
            P(None, ("frame", "row")),
            P(None, ("frame", "row")),
            P(None, ("frame", "row")),
            P(("frame", "row"), None),
            P(("frame", "row"), None),
            P(("frame", "row"), None),
            P(("frame", "row")),
            P(("frame", "row")),
            P(("frame", "row")),
        ),
        out_specs=(
            P("frame", None, "row", None, None),
            P("frame", None, "row", None, None),
            P(),
            P(None, ("frame", "row")),
            P(None, ("frame", "row")),
            P(("frame", "row"), None),
            P(("frame", "row"), None),
            P(None, ("frame", "row")),
            P(None, ("frame", "row")),
            P(("frame", "row"), None),
            P(("frame", "row"), None),
            P(None, ("frame", "row")),
            P(None, ("frame", "row")),
            P(None, ("frame", "row")),
            P(("frame", "row"), None),
            P(("frame", "row"), None),
            P(("frame", "row"), None),
            P(("frame", "row")),
            P(("frame", "row")),
            P(("frame", "row")),
        ),
        check_vma=False,
    )
```

```python
import functools
import math

import jax
import jax.numpy as jnp
from jax import lax
from jax.experimental import pallas as pl
from jax.experimental.pallas import tpu as pltpu
from jax.sharding import PartitionSpec as P

D = 1024
HEADS = 16
HD = 64
FF = 4096


highest = lax.Precision.HIGHEST
newton_one = 3.4445
newton_two = -4.775
newton_three = 2.0315
momentum_decay = 0.95
muon_rate = 1.5
weight_decay = 0.01
beta_first = 0.9
beta_second = 0.95
adam_floor = 1e-08
norm_floor = 1e-06
clip_limit = 1.0
rotary_base = 10000.0


def rotary_angles(time_grid, row_grid, column_grid):
    quarter_pairs = HD // 4
    eighth_pairs = HD // 8
    time_rates = rotary_base ** (-jnp.arange(quarter_pairs, dtype=jnp.float32) / quarter_pairs)
    space_rates = rotary_base ** (-jnp.arange(eighth_pairs, dtype=jnp.float32) / eighth_pairs)
    return jnp.concatenate(
        [
            time_grid[..., None] * time_rates,
            row_grid[..., None] * space_rates,
            column_grid[..., None] * space_rates,
        ],
        axis=-1,
    )


def adam_update(grad_item, first, second, master, rate, clip_factor, step_value):
    clipped = clip_factor * grad_item
    first_new = beta_first * first + (1.0 - beta_first) * clipped
    second_new = beta_second * second + (1.0 - beta_second) * clipped * clipped
    first_fix = 1.0 - beta_first**step_value
    second_fix = 1.0 - beta_second**step_value
    master_new = master * (1.0 - rate * weight_decay) - rate * (first_new / first_fix) / (
        jnp.sqrt(second_new / second_fix) + adam_floor
    )
    return (first_new, second_new, master_new)


def halves(value, dim, axis, bit):
    mine = (lax.axis_index(axis) >> bit) & 1
    keep = lax.dynamic_index_in_dim(value, mine, dim, keepdims=False)
    send = lax.dynamic_index_in_dim(value, 1 - mine, dim, keepdims=False)
    return keep, send.astype(jnp.bfloat16)


def joined(keep, send, axis, bit):
    size = lax.axis_size(axis)
    came = lax.ppermute(send, axis, [(index, index ^ (1 << bit)) for index in range(size)])
    return keep + came.astype(jnp.float32)


def held(value, *others):
    if not others:
        return value
    return lax.optimization_barrier((value, *others))[0]


def scatter_steps(groups, name):
    frame_bits = lax.axis_size("frame").bit_length() - 1
    row_bits = lax.axis_size("row").bit_length() - 1
    row = lax.axis_index("row")
    numbers = jnp.stack([lax.axis_index("frame") & 1, row & 1, row >> (row_bits - 1)]).astype(jnp.int32)
    size = lax.axis_size("frame")
    came = []
    for at, group in enumerate(groups):
        send = send_sums(numbers, group, f"{name}_send_{at}")
        came.append(lax.ppermute(send, "frame", [(index, index ^ 1) for index in range(size)]))
        numbers = held(numbers, send)
    keep, send = keep_sums(numbers, groups, came, name + "_keep")
    names = [("frame", bit) for bit in reversed(range(1, frame_bits))]
    names += [("row", bit) for bit in reversed(range(row_bits))]
    side_names = []
    for side in range(2):
        bit = 0 if side == 0 else row_bits - 1
        side_names.append([item for item in names if item != ("row", bit)])
        shape = (2,) * (len(names) - 1) + keep[side].shape[2:]
        keep[side] = keep[side].reshape(shape)
        send[side] = send[side].reshape(shape)
    hold = yield send
    for step in range(row_bits):
        parts = []
        for side in range(2):
            bit = step if side == 0 else row_bits - 1 - step
            parts.append(joined(held(keep[side], *hold), send[side], "row", bit))
        if step == row_bits - 1:
            break
        for side in range(2):
            bit = step + 1 if side == 0 else row_bits - 2 - step
            dim = side_names[side].index(("row", bit))
            side_names[side].pop(dim)
            keep[side], send[side] = halves(parts[side], dim, "row", bit)
        hold = yield send
    value = jnp.concatenate(parts, axis=-1)
    names = names[: frame_bits - 1]
    for bit in range(1, frame_bits):
        dim = names.index(("frame", bit))
        names.pop(dim)
        keep, send = halves(value, dim, "frame", bit)
        hold = yield [send]
        value = joined(held(keep, *hold), send, "frame", bit)
    yield value


def finished(steps, state):
    while isinstance(state, list):
        state = steps.send([])
    return state


def split_two(value):
    high = value.astype(jnp.bfloat16)
    return high, (value - high.astype(jnp.float32)).astype(jnp.bfloat16)


def dot_low(left, right):
    return lax.dot_general(left, right, (((1,), (0,)), ((), ())), preferred_element_type=jnp.float32)


def dot_nt(left, right):
    return lax.dot_general(left, right, (((1,), (1,)), ((), ())), preferred_element_type=jnp.float32)


def dot_tn(left, right):
    return lax.dot_general(left, right, (((0,), (0,)), ((), ())), preferred_element_type=jnp.float32)


MIB = 1024 * 1024


def vmem_params(mib, semantics=None):
    return pltpu.CompilerParams(vmem_limit_bytes=mib * MIB, dimension_semantics=semantics)


def whole_spec(array):
    zeros = (0,) * array.ndim
    return pl.BlockSpec(array.shape, lambda *_: zeros, pipeline_mode=pl.Buffered(1))


def turned(value, cosine, sine):
    even = lax.broadcasted_iota(jnp.int32, value.shape, 1) % 2 == 0
    width = value.shape[1]
    swapped = jnp.where(even, pltpu.roll(value, width - 1, 1), pltpu.roll(value, 1, 1))
    return value * cosine + swapped * sine


def framed(value, frames):
    rows, width = value.shape
    return value.reshape(frames, rows // frames, width)


def norm_parts(value):
    mean = jnp.mean(value, axis=-1, keepdims=True)
    centered = value - mean
    root = lax.rsqrt(jnp.mean(centered * centered, axis=-1, keepdims=True) + norm_floor)
    return centered * root, root


def project_kernel(slots, me_ref, x_ref, mod_ref, cos_ref, sin_ref, w_ref, hid_ref, *out_refs):
    frames = mod_ref.shape[1]
    group = D // slots
    normed, _ = norm_parts(x_ref[0].astype(jnp.float32))
    normed = framed(normed, frames)
    shift = mod_ref[0, :, 0:D][:, None, :]
    scaling = mod_ref[0, :, D : 2 * D][:, None, :]
    hidden = (normed * (1.0 + scaling) + shift).reshape(x_ref.shape[1], D).astype(jnp.bfloat16)
    hid_ref[0] = hidden
    cosine = cos_ref[...]
    sine = sin_ref[...]
    me = me_ref[0]
    for slot in range(slots):
        peer = me ^ slot
        for part in range(3):
            rows = pl.ds(pl.multiple_of(part * D + peer * group, group), group)
            value = dot_nt(hidden, w_ref[rows, :])
            if part == 2:
                out_refs[slot][part] = value.astype(jnp.bfloat16)
                continue
            for first in range(0, group, 128):
                piece = turned(value[:, first : first + 128], cosine, sine)
                if part == 0:
                    piece = piece * (1.0 / math.sqrt(HD))
                out_refs[slot][part, :, first : first + 128] = piece.astype(jnp.bfloat16)


def project(me, clip, tokens, mod, cosine, sine, w_qkv, slots):
    count, tall_rows, _ = tokens.shape
    tile = 256
    steps = tall_rows // tile
    group = D // slots
    out_shape = [jax.ShapeDtypeStruct((1, tall_rows, D), jnp.bfloat16)]
    out_shape += [jax.ShapeDtypeStruct((3, tall_rows, group), jnp.bfloat16)] * slots
    return pl.pallas_call(
        functools.partial(project_kernel, slots),
        grid=(steps,),
        in_specs=[
            pl.BlockSpec(memory_space=pltpu.SMEM),
            pl.BlockSpec((1, tile, D), lambda i: (clip, i, 0)),
            pl.BlockSpec((1, mod.shape[1], 6 * D), lambda i: (clip * steps + i, 0, 0)),
            pl.BlockSpec((tile, 128), lambda i: (clip * steps + i, 0)),
            pl.BlockSpec((tile, 128), lambda i: (clip * steps + i, 0)),
            whole_spec(w_qkv),
        ],
        out_specs=[pl.BlockSpec((1, tile, D), lambda i: (0, i, 0))]
        + [pl.BlockSpec((3, tile, group), lambda i: (0, i, 0))] * slots,
        out_shape=out_shape,
        compiler_params=vmem_params(60),
        cost_estimate=pl.CostEstimate(
            flops=6 * tall_rows * D * D, bytes_accessed=10 * MIB, transcendentals=0
        ),
        name="project",
    )(me, tokens, mod, cosine, sine, w_qkv)


def head_mask(shape, head, axis):
    return lax.broadcasted_iota(jnp.int32, shape, axis) // HD == head


def attend_kernel(slots, tile, *refs):
    ins, outs = refs[:slots], refs[slots : 2 * slots]
    full_ref, log_ref, qs, ks, vs = refs[2 * slots :]
    length = ins[0].shape[1]
    for slot in range(slots):
        rows = slice(slot * length, (slot + 1) * length)
        qs[rows, :] = ins[slot][0]
        ks[rows, :] = ins[slot][1]
        vs[rows, :] = ins[slot][2]

    def one(index, carry):
        rows = pl.ds(pl.multiple_of(index * tile, tile), tile)
        query = qs[rows, :]
        first = head_mask((tile, 128), 0, 1)
        parts = []
        logs = []
        for head in range(2):
            masked = jnp.where(first if head == 0 else ~first, query, jnp.zeros_like(query))
            scores = dot_nt(masked, ks[...])
            top = jnp.max(scores, axis=-1, keepdims=True)
            raised = jnp.exp(scores - top)
            total = jnp.sum(raised, axis=-1, keepdims=True)
            parts.append(dot_low(raised.astype(jnp.bfloat16), vs[...]) * (1.0 / total))
            logs.append(top + jnp.log(total))
        full_ref[rows, :] = jnp.where(first, parts[0], parts[1])
        log_ref[rows, :] = jnp.where(first, logs[0], logs[1])
        return carry

    lax.fori_loop(0, slots * length // tile, one, 0)
    for slot in range(slots):
        rows = slice(slot * length, (slot + 1) * length)
        outs[slot][...] = full_ref[rows, :].astype(jnp.bfloat16)


def attend(pieces):
    slots = len(pieces)
    _, length, group = pieces[0].shape
    total = slots * length
    scratch = pltpu.VMEM((total, 128), jnp.bfloat16)
    outs = pl.pallas_call(
        functools.partial(attend_kernel, slots, 256),
        grid=(group // 128,),
        in_specs=[pl.BlockSpec((3, length, 128), lambda i: (0, 0, i))] * slots,
        out_specs=[pl.BlockSpec((length, 128), lambda i: (0, i))] * slots
        + [pl.BlockSpec((total, 128), lambda i: (0, i))] * 2,
        out_shape=[jax.ShapeDtypeStruct((length, group), jnp.bfloat16)] * slots
        + [jax.ShapeDtypeStruct((total, group), jnp.float32)] * 2,
        scratch_shapes=[scratch] * 3,
        compiler_params=vmem_params(60),
        cost_estimate=pl.CostEstimate(
            flops=16 * total * total * group, bytes_accessed=8 * MIB, transcendentals=total * total * 4
        ),
        name="attend",
    )(*pieces)
    return outs[:slots], outs[slots], outs[slots + 1]


def attend_back_kernel(slots, tile, *refs):
    ins, grads = refs[:slots], refs[slots : 2 * slots]
    full_ref, log_ref = refs[2 * slots : 2 * slots + 2]
    outs = refs[2 * slots + 2 : 3 * slots + 2]
    qs, ks, vs, gs, q_turned, g_turned, dq, dk, dv = refs[3 * slots + 2 :]
    length = ins[0].shape[1]
    total = slots * length
    for slot in range(slots):
        rows = slice(slot * length, (slot + 1) * length)
        qs[rows, :] = ins[slot][0]
        ks[rows, :] = ins[slot][1]
        vs[rows, :] = ins[slot][2]
        gs[rows, :] = grads[slot][...]
        q_turned[:, rows] = ins[slot][0].T
        g_turned[:, rows] = grads[slot][...].T
    dk[...] = jnp.zeros_like(dk)
    dv[...] = jnp.zeros_like(dv)

    def one(index, carry):
        rows = pl.ds(pl.multiple_of(index * tile, tile), tile)
        first = head_mask((tile, 128), 0, 1)
        upper = head_mask((128, tile), 0, 0)
        query, grad = qs[rows, :], gs[rows, :]
        query_t, grad_t = q_turned[:, rows], g_turned[:, rows]
        product = grad.astype(jnp.float32) * full_ref[rows, :]
        masks = (first, ~first)
        masks_t = (upper, ~upper)
        zero = jnp.zeros_like(query)
        zero_t = jnp.zeros_like(query_t)
        q_low = [jnp.where(mask, query, zero) for mask in masks]
        g_low = [jnp.where(mask, grad, zero) for mask in masks]
        qt_low = [jnp.where(mask, query_t, zero_t) for mask in masks_t]
        gt_low = [jnp.where(mask, grad_t, zero_t) for mask in masks_t]
        inner = [jnp.sum(jnp.where(mask, product, 0.0), axis=-1, keepdims=True) for mask in masks]
        logs = [log_ref[rows, 0:1], log_ref[rows, HD : HD + 1]]

        def inside(k_index, sums):
            at = pl.ds(pl.multiple_of(k_index * tile, tile), tile)
            key, value = ks[at, :], vs[at, :]
            out = []
            for head in range(2):
                probs = jnp.exp(dot_nt(q_low[head], key) - logs[head])
                d_probs = dot_nt(g_low[head], value)
                d_scores = (probs * (d_probs - inner[head])).astype(jnp.bfloat16)
                dv[:, at] += dot_low(gt_low[head], probs.astype(jnp.bfloat16))
                dk[:, at] += dot_low(qt_low[head], d_scores)
                out.append(sums[head] + dot_low(d_scores, key))
            return tuple(out)

        start = jnp.zeros((tile, 128), jnp.float32)
        sums = lax.fori_loop(0, total // tile, inside, (start, start))
        dq[rows, :] = (jnp.where(first, sums[0], sums[1]) * (1.0 / math.sqrt(HD))).astype(jnp.bfloat16)
        return carry

    lax.fori_loop(0, total // tile, one, 0)
    for slot in range(slots):
        rows = slice(slot * length, (slot + 1) * length)
        outs[slot][0] = dq[rows, :]
        outs[slot][1] = dk[:, rows].T.astype(jnp.bfloat16)
        outs[slot][2] = dv[:, rows].T.astype(jnp.bfloat16)


def attend_back(pieces, grads, full, logs):
    slots = len(pieces)
    _, length, group = pieces[0].shape
    total = slots * length
    low = pltpu.VMEM((total, 128), jnp.bfloat16)
    low_t = pltpu.VMEM((128, total), jnp.bfloat16)
    full_t = pltpu.VMEM((128, total), jnp.float32)
    return pl.pallas_call(
        functools.partial(attend_back_kernel, slots, 512),
        grid=(group // 128,),
        in_specs=[pl.BlockSpec((3, length, 128), lambda i: (0, 0, i))] * slots
        + [pl.BlockSpec((length, 128), lambda i: (0, i))] * slots
        + [pl.BlockSpec((total, 128), lambda i: (0, i))] * 2,
        out_specs=[pl.BlockSpec((3, length, 128), lambda i: (0, 0, i))] * slots,
        out_shape=[jax.ShapeDtypeStruct((3, length, group), jnp.bfloat16)] * slots,
        scratch_shapes=[low] * 4 + [low_t] * 2 + [low] + [full_t] * 2,
        compiler_params=vmem_params(60),
        cost_estimate=pl.CostEstimate(
            flops=40 * total * total * group, bytes_accessed=12 * MIB, transcendentals=total * total * 4
        ),
        name="attend_back",
    )(*pieces, *grads, full, logs)


def part_of(ref, index, size):
    count = size // ref.shape[1]
    return ref[pl.ds(index * count, count)].reshape(size, ref.shape[2])


def middle_kernel(slots, me_ref, x_ref, cot_ref, mod_ref, wo_ref, wu_ref, wd_ref, *refs):
    att_refs = refs[:slots]
    datt_refs = refs[slots : 2 * slots]
    (
        out_ref,
        att_ref,
        h2_ref,
        act_ref,
        db2_ref,
        dup_ref,
        db1_ref,
        dmid_ref,
        sums_ref,
        slope,
    ) = refs[2 * slots :]
    frames = mod_ref.shape[1]
    rows = x_ref.shape[1]
    group = D // slots
    me = me_ref[0]

    def mod(index):
        return mod_ref[0, :, index * D : (index + 1) * D][:, None, :]

    def spread(value, index, plus=0.0):
        return (framed(value, frames) * (mod(index) + plus)).reshape(rows, D)

    def frame_sum(value):
        return jnp.sum(framed(value, frames), axis=1)

    branch = jnp.zeros((rows, D), jnp.float32)
    for slot in range(slots):
        at = pl.ds(pl.multiple_of((me ^ slot) * group, group), group)
        piece = att_refs[slot][...]
        att_ref[:, at] = piece
        branch += dot_low(piece, part_of(wo_ref, me ^ slot, group))
    middle = x_ref[0].astype(jnp.float32) + spread(branch, 2)
    normed, root = norm_parts(middle)
    hidden = (framed(spread(normed, 4, 1.0), frames) + mod(3)).reshape(rows, D).astype(jnp.bfloat16)
    h2_ref[...] = hidden
    wide = 1024
    curve = math.sqrt(2.0 / math.pi)
    branch_two = jnp.zeros((rows, D), jnp.float32)
    for first in range(0, FF, wide):
        cut = slice(first, first + wide)
        up = dot_nt(hidden, part_of(wu_ref, first // wide, wide))
        square = up * up
        bent = jnp.tanh(curve * up * (1.0 + 0.044715 * square))
        half = 0.5 * (1.0 + bent)
        active = (up * half).astype(jnp.bfloat16)
        slope[:, cut] = half + 0.5 * up * (1.0 - bent * bent) * (curve * (1.0 + 3 * 0.044715 * square))
        act_ref[:, cut] = active
        branch_two += dot_low(active, part_of(wd_ref, first // wide, wide))
    cot = cot_ref[0].astype(jnp.float32)
    out_ref[0] = (middle + spread(branch_two, 5)).astype(jnp.bfloat16)
    sums_ref[0, 3] = frame_sum(cot * branch_two)
    d_branch_two = spread(cot, 5).astype(jnp.bfloat16)
    db2_ref[...] = d_branch_two
    d_hidden = jnp.zeros((rows, D), jnp.float32)
    for first in range(0, FF, wide):
        cut = slice(first, first + wide)
        d_up = (dot_nt(d_branch_two, part_of(wd_ref, first // wide, wide)) * slope[:, cut]).astype(jnp.bfloat16)
        dup_ref[:, cut] = d_up
        d_hidden += dot_low(d_up, part_of(wu_ref, first // wide, wide))
    sums_ref[0, 1] = frame_sum(d_hidden)
    sums_ref[0, 2] = frame_sum(d_hidden * normed)
    inner = spread(d_hidden, 4, 1.0)
    d_middle = cot + root * (
        inner
        - jnp.mean(inner, axis=-1, keepdims=True)
        - normed * jnp.mean(inner * normed, axis=-1, keepdims=True)
    )
    dmid_ref[...] = d_middle
    sums_ref[0, 0] = frame_sum(d_middle * branch)
    d_branch = spread(d_middle, 2).astype(jnp.bfloat16)
    db1_ref[...] = d_branch
    for slot in range(slots):
        datt_refs[slot][...] = dot_nt(d_branch, part_of(wo_ref, me ^ slot, group)).astype(jnp.bfloat16)


def middle(me, clip, tokens, cotangent, mod, w_out, w_up, w_down, attended):
    slots = len(attended)
    count, length, _ = tokens.shape
    tile = 256
    steps = length // tile
    group = D // slots
    frames = mod.shape[1]
    low = jnp.bfloat16

    def flat(width, kind=low):
        return jax.ShapeDtypeStruct((length, width), kind)

    def flat_spec(width):
        return pl.BlockSpec((tile, width), lambda i: (i, 0))

    outs = pl.pallas_call(
        functools.partial(middle_kernel, slots),
        grid=(steps,),
        in_specs=[
            pl.BlockSpec(memory_space=pltpu.SMEM),
            pl.BlockSpec((1, tile, D), lambda i: (clip, i, 0)),
            pl.BlockSpec((1, tile, D), lambda i: (clip, i, 0)),
            pl.BlockSpec((1, frames, 6 * D), lambda i: (clip * steps + i, 0, 0)),
            *(item[1] for item in (w_out, w_up, w_down)),
        ]
        + [flat_spec(group)] * slots,
        out_specs=[flat_spec(group)] * slots
        + [pl.BlockSpec((1, tile, D), lambda i: (0, i, 0))]
        + [flat_spec(width) for width in (D, D, FF, D, FF, D, D)]
        + [pl.BlockSpec((1, 4, frames, D), lambda i: (i, 0, 0, 0))],
        out_shape=[flat(group)] * slots
        + [jax.ShapeDtypeStruct((1, length, D), low)]
        + [flat(D), flat(D), flat(FF), flat(D), flat(FF), flat(D), flat(D, jnp.float32)]
        + [jax.ShapeDtypeStruct((steps, 4, frames, D), jnp.float32)],
        scratch_shapes=[pltpu.VMEM((tile, FF), jnp.float32)],
        compiler_params=vmem_params(60),
        cost_estimate=pl.CostEstimate(
            flops=2 * length * D * (2 * D + 4 * FF), bytes_accessed=40 * MIB, transcendentals=length * FF
        ),
        name="middle",
    )(me, tokens, cotangent, mod, *(item[0] for item in (w_out, w_up, w_down)), *attended)
    return outs[:slots], outs[slots:]


def last_kernel(slots, me_ref, x_ref, mod_ref, cos_ref, sin_ref, w_ref, dmid_ref, *refs):
    pieces = refs[:slots]
    dproj_ref, grad_ref, sums_ref = refs[slots:]
    frames = mod_ref.shape[1]
    rows = x_ref.shape[1]
    group = D // slots
    me = me_ref[0]
    cosine = cos_ref[...]
    sine = -sin_ref[...]
    d_hidden = jnp.zeros((rows, D), jnp.float32)
    for slot in range(slots):
        peer = me ^ slot
        for part in range(3):
            base = pl.multiple_of(part * D + peer * group, group)
            if part == 2:
                value = pieces[slot][part]
            else:
                value = jnp.concatenate(
                    [
                        turned(pieces[slot][part, :, at : at + 128].astype(jnp.float32), cosine, sine)
                        for at in range(0, group, 128)
                    ],
                    axis=1,
                ).astype(jnp.bfloat16)
            dproj_ref[:, pl.ds(base, group)] = value
            d_hidden += dot_low(value, w_ref[pl.ds(base, group), :])
    normed, root = norm_parts(x_ref[0].astype(jnp.float32))
    scaling = mod_ref[0, :, D : 2 * D][:, None, :]
    sums_ref[0, 0] = jnp.sum(framed(d_hidden, frames), axis=1)
    sums_ref[0, 1] = jnp.sum(framed(d_hidden * normed, frames), axis=1)
    inner = (framed(d_hidden, frames) * (1.0 + scaling)).reshape(rows, D)
    grad_ref[0] = dmid_ref[...] + root * (
        inner
        - jnp.mean(inner, axis=-1, keepdims=True)
        - normed * jnp.mean(inner * normed, axis=-1, keepdims=True)
    )


def last(me, clip, tokens, mod, cosine, sine, w_qkv, d_middle, pieces):
    slots = len(pieces)
    count, length, _ = tokens.shape
    tile = 256
    steps = length // tile
    group = D // slots
    frames = mod.shape[1]
    return pl.pallas_call(
        functools.partial(last_kernel, slots),
        grid=(steps,),
        in_specs=[
            pl.BlockSpec(memory_space=pltpu.SMEM),
            pl.BlockSpec((1, tile, D), lambda i: (clip, i, 0)),
            pl.BlockSpec((1, frames, 6 * D), lambda i: (clip * steps + i, 0, 0)),
            pl.BlockSpec((tile, 128), lambda i: (clip * steps + i, 0)),
            pl.BlockSpec((tile, 128), lambda i: (clip * steps + i, 0)),
            whole_spec(w_qkv),
            pl.BlockSpec((tile, D), lambda i: (i, 0)),
        ]
        + [pl.BlockSpec((3, tile, group), lambda i: (0, i, 0))] * slots,
        out_specs=[
            pl.BlockSpec((tile, 3 * D), lambda i: (i, 0)),
            pl.BlockSpec((1, tile, D), lambda i: (0, i, 0)),
            pl.BlockSpec((1, 2, frames, D), lambda i: (i, 0, 0, 0)),
        ],
        out_shape=[
            jax.ShapeDtypeStruct((length, 3 * D), jnp.bfloat16),
            jax.ShapeDtypeStruct((1, length, D), jnp.float32),
            jax.ShapeDtypeStruct((steps, 2, frames, D), jnp.float32),
        ],
        compiler_params=vmem_params(60),
        cost_estimate=pl.CostEstimate(
            flops=6 * length * D * D, bytes_accessed=20 * MIB, transcendentals=0
        ),
        name="last",
    )(me, tokens, mod, cosine, sine, w_qkv, d_middle, *pieces)


def member_value(refs, member, doubled, parity):
    left = refs[4 * member : 4 * member + 2]
    right = refs[4 * member + 2 : 4 * member + 4]
    value = dot_tn(left[0][...], right[0][...]) + dot_tn(left[1][...], right[1][...])
    if doubled:
        half = value.shape[0] // 2
        value = jnp.where(parity == 0, value[:half], value[half:])
    return value


def send_kernel(doubled, number_ref, *refs):
    out_ref = refs[-1]
    rows = out_ref.shape[1]
    first = 0
    for member in range(len(doubled)):
        value = member_value(refs, member, doubled[member], 1 - number_ref[0])
        height = value.shape[0] // rows
        out_ref[0, :, first : first + height, :] = value.reshape(rows, height, D).astype(out_ref.dtype)
        first += height


def keep_kernel(doubled, counts, number_ref, *refs):
    members = len(doubled)
    came_refs = refs[4 * members : 4 * members + len(counts)]
    keep_refs, send_refs = refs[-4:-2], refs[-2:]
    half_rows = keep_refs[0].shape[1]
    width = D // 2
    first = 0
    member = 0
    for came_ref, count in zip(came_refs, counts):
        inside = 0
        for _ in range(count):
            value = member_value(refs, member, doubled[member], number_ref[0])
            height = value.shape[0] // (2 * half_rows)
            rows = slice(first, first + height)
            parts = [
                value[row * height : (row + 1) * height]
                + came_ref[0, row, inside : inside + height, :].astype(jnp.float32)
                for row in range(2 * half_rows)
            ]
            for place in range(half_rows):
                for side in range(2):
                    cut = slice(side * width, (side + 1) * width)
                    low = 2 * place if side == 0 else place
                    high = low + (1 if side == 0 else half_rows)
                    upper = number_ref[1 + side] == 1
                    zero, one = parts[low][:, cut], parts[high][:, cut]
                    keep_refs[side][0, place, rows, :] = jnp.where(upper, one, zero)
                    send_refs[side][0, place, rows, :] = jnp.where(upper, zero, one).astype(jnp.bfloat16)
            first += height
            inside += height
            member += 1


def weight_specs(pairs, other):
    frame_devices = lax.axis_size("frame")
    specs, operands, doubled = [], [], []
    height = 0
    for left, right in pairs:
        width = left[0].shape[1] // frame_devices
        height += width // lax.axis_size("row")
        doubled.append(width % 128 != 0)
        if doubled[-1]:
            spec = pl.BlockSpec((left[0].shape[0], 2 * width), lambda i, s: (0, i))
        elif other:
            spec = pl.BlockSpec((left[0].shape[0], width), lambda i, s: (0, 2 * i + 1 - s[0]))
        else:
            spec = pl.BlockSpec((left[0].shape[0], width), lambda i, s: (0, 2 * i + s[0]))
        specs += [spec] * 2
        specs += [pl.BlockSpec(right[0].shape, lambda i, s: (0, 0))] * 2
        operands += [*left, *right]
    flops = sum(4 * left[0].shape[0] * left[0].shape[1] * D // 2 for left, _ in pairs)
    return specs, operands, tuple(doubled), height, flops


def send_sums(numbers, pairs, name):
    specs, operands, doubled, height, flops = weight_specs(pairs, True)
    frames, rows = lax.axis_size("frame") // 2, lax.axis_size("row")
    return pl.pallas_call(
        functools.partial(send_kernel, doubled),
        grid_spec=pltpu.PrefetchScalarGridSpec(
            num_scalar_prefetch=1,
            grid=(frames,),
            in_specs=specs,
            out_specs=pl.BlockSpec((1, rows, height, D), lambda i, s: (i, 0, 0, 0)),
        ),
        out_shape=jax.ShapeDtypeStruct((frames, rows, height, D), jnp.bfloat16),
        compiler_params=vmem_params(60),
        cost_estimate=pl.CostEstimate(flops=flops, bytes_accessed=20 * MIB, transcendentals=0),
        name=name,
    )(numbers, *operands)


def keep_sums(numbers, groups, came, name):
    pairs = [pair for group in groups for pair in group]
    specs, operands, doubled, height, flops = weight_specs(pairs, False)
    frames, rows = lax.axis_size("frame") // 2, lax.axis_size("row")
    specs += [pl.BlockSpec((1,) + item.shape[1:], lambda i, s: (i, 0, 0, 0)) for item in came]
    shape = (frames, rows // 2, height, D // 2)
    out_spec = pl.BlockSpec((1,) + shape[1:], lambda i, s: (i, 0, 0, 0))
    outs = pl.pallas_call(
        functools.partial(keep_kernel, doubled, tuple(len(group) for group in groups)),
        grid_spec=pltpu.PrefetchScalarGridSpec(
            num_scalar_prefetch=1, grid=(frames,), in_specs=specs, out_specs=[out_spec] * 4
        ),
        out_shape=[jax.ShapeDtypeStruct(shape, jnp.float32)] * 2
        + [jax.ShapeDtypeStruct(shape, jnp.bfloat16)] * 2,
        compiler_params=vmem_params(60),
        cost_estimate=pl.CostEstimate(flops=flops, bytes_accessed=40 * MIB, transcendentals=0),
        name=name,
    )(numbers, *operands, *came)
    return list(outs[:2]), list(outs[2:])


def newton_kernel(rows, *refs):
    all_refs, mine_ref, out_ref = refs[:-11], refs[-11], refs[-10]
    a_ref, ah, al, nh, th, tl, qh, ql, num_ref = refs[-9:]
    width = a_ref.shape[0]
    steps = width // rows
    deep = min(1024, all_refs[0].shape[0])
    a_at, m_at, t_at = 0, 1, 2

    def block(index):
        return pl.ds(pl.multiple_of(index * rows, rows), rows)

    def on_diagonal(index):
        row_at = lax.broadcasted_iota(jnp.int32, (rows, width), 0) + index * rows
        return row_at == lax.broadcasted_iota(jnp.int32, (rows, width), 1)

    def each(make):
        def one(index, carry):
            make(index)
            return carry

        lax.fori_loop(0, steps, one, 0)

    def put(index, value, base, number_at, high, low=None):
        diagonal = on_diagonal(index)

        @pl.when(index == 0)
        def _():
            num_ref[3] = jnp.sum(jnp.where(diagonal, value, 0.0)) * (1.0 / rows)
            num_ref[4 + number_at] = base + num_ref[3]

        rest = value - jnp.where(diagonal, num_ref[3], 0.0)
        first, second = split_two(rest)
        high[block(index), :] = first
        if low is not None:
            low[block(index), :] = second

    def commit(number_at):
        num_ref[number_at] = num_ref[4 + number_at]

    def wide(high, low, at):
        return high[at, :].astype(jnp.float32) + low[at, :].astype(jnp.float32)

    squares = 0.0
    for index in range(steps):
        columns = slice(index * rows, (index + 1) * rows)
        value = jnp.zeros((rows, width), jnp.float32)
        for ref in all_refs:

            def part(k, total, ref=ref, columns=columns):
                at = pl.ds(pl.multiple_of(k * deep, deep), deep)
                return total + dot_tn(ref[at, columns], ref[at, :])

            value = lax.fori_loop(0, ref.shape[0] // deep, part, value)
        a_ref[columns, :] = value
        squares += jnp.sum(jnp.where(on_diagonal(index), value, 0.0))
    squares = jnp.full((1, 1), squares, jnp.float32)
    inverse = 1.0 / (jnp.sqrt(squares) + 1e-07)
    each(lambda index: put(index, a_ref[block(index), :] * inverse * inverse, 0.0, a_at, ah, al))
    commit(a_at)

    for number in range(5):
        two = number < 2

        def make_n(index):
            at = block(index)
            shift = num_ref[a_at]
            value = newton_three * dot_low(ah[at, :], ah[...])
            value += (newton_two + 2.0 * newton_three * shift) * wide(ah, al, at)
            base = newton_one + newton_two * shift + newton_three * shift * shift
            put(index, value, base, m_at, nh)

        each(make_n)
        commit(m_at)
        if number == 0:

            def first_q(index):
                at = block(index)
                value = nh[at, :].astype(jnp.float32) + jnp.where(on_diagonal(index), num_ref[m_at], 0.0)
                qh[at, :], ql[at, :] = split_two(value)

            each(first_q)
        else:

            def next_q(index):
                at = block(index)
                value = num_ref[m_at] * wide(qh, ql, at) + dot_low(qh[at, :], nh[...])
                if number >= 3:
                    value += dot_low(ql[at, :], nh[...])
                qh[at, :], ql[at, :] = split_two(value)

            each(next_q)
        if number == 4:
            break

        def make_t(index):
            at = block(index)
            shift, much = num_ref[a_at], num_ref[m_at]
            value = dot_low(ah[at, :], nh[...])
            if two:
                value += dot_low(al[at, :], nh[...])
            value += shift * nh[at, :].astype(jnp.float32) + much * wide(ah, al, at)
            put(index, value, shift * much, t_at, th, tl)

        each(make_t)
        commit(t_at)

        def make_a(index):
            at = block(index)
            shift, much = num_ref[t_at], num_ref[m_at]
            value = dot_low(nh[at, :], th[...])
            if two:
                value += dot_low(nh[at, :], tl[...])
            value += shift * nh[at, :].astype(jnp.float32) + much * wide(th, tl, at)
            put(index, value, shift * much, a_at, ah, al)

        each(make_a)
        commit(a_at)

    mine = mine_ref[...]
    out_ref[...] = ((dot_low(mine, qh[...]) + dot_low(mine, ql[...])) * inverse).astype(out_ref.dtype)


def newton(everything, mine, rows=256):
    width = mine.shape[1]
    low = pltpu.VMEM((width, width), jnp.bfloat16)
    return pl.pallas_call(
        functools.partial(newton_kernel, rows),
        out_shape=jax.ShapeDtypeStruct(mine.shape, jnp.bfloat16),
        in_specs=[pl.BlockSpec(memory_space=pltpu.VMEM)] * (len(everything) + 1),
        out_specs=pl.BlockSpec(memory_space=pltpu.VMEM),
        scratch_shapes=[pltpu.VMEM((width, width), jnp.float32)]
        + [low] * 7
        + [pltpu.SMEM((8,), jnp.float32)],
        compiler_params=pltpu.CompilerParams(vmem_limit_bytes=60 * 1024 * 1024),
        cost_estimate=pl.CostEstimate(flops=60 * 10**9, bytes_accessed=12 * 10**6, transcendentals=0),
        name="newton",
    )(*everything, mine)


def frame_sums_kernel(count, *refs):
    out_ref = refs[-1]
    ones, twos = refs[:count], refs[count : 2 * count]
    steps, _, frames, _ = ones[0].shape
    at = 0
    for clip in range(count):
        for step in range(steps):
            rows = slice(at, at + frames)
            for index in range(2):
                out_ref[rows, index * D : (index + 1) * D] = ones[clip][step, index]
            for index in range(4):
                out_ref[rows, (index + 2) * D : (index + 3) * D] = twos[clip][step, index]
            at += frames


def frame_sums(ones, twos):
    steps, _, frames, _ = ones[0].shape
    return pl.pallas_call(
        functools.partial(frame_sums_kernel, len(ones)),
        out_shape=jax.ShapeDtypeStruct((len(ones) * steps * frames, 6 * D), jnp.float32),
        in_specs=[pl.BlockSpec(memory_space=pltpu.VMEM)] * (2 * len(ones)),
        out_specs=pl.BlockSpec(memory_space=pltpu.VMEM),
        compiler_params=vmem_params(60),
        cost_estimate=pl.CostEstimate(flops=0, bytes_accessed=MIB, transcendentals=0),
        name="frame_sums",
    )(*ones, *twos)


def swap(slots):
    size = lax.axis_size("row")
    out = [slots[0]]
    for slot in range(1, size):
        out.append(lax.ppermute(slots[slot], "row", [(index, index ^ slot) for index in range(size)]))
    return out


def per_device(
    tokens,
    cotangent,
    noise_levels,
    frame_times,
    step_count,
    qkv_master,
    qkv_momentum,
    out_master,
    out_momentum,
    up_master,
    up_momentum,
    down_master,
    down_momentum,
    ada_master,
    ada_first,
    ada_second,
    table_master,
    table_first,
    table_second,
    bias_master,
    bias_first,
    bias_second,
):
    low_type = jnp.bfloat16
    full_type = jnp.float32
    clip_count, frames, rows_dev, columns, model_width = tokens.shape
    seq_local = frames * rows_dev * columns
    row_devices = lax.axis_size("row")
    token_total = clip_count * seq_local
    frame_total = clip_count * frames
    shape_five = (clip_count, frames, rows_dev, columns, model_width)
    both = ("frame", "row")
    frame_devices = lax.axis_size("frame")
    device_total = frame_devices * row_devices
    device_index = lax.axis_index("frame") * row_devices + lax.axis_index("row")
    heights = (qkv_master.shape[1], out_master.shape[0], up_master.shape[1], down_master.shape[0])
    w_qkv = lax.all_gather(qkv_master.T.astype(low_type), both, axis=0, tiled=True)
    shards = jnp.concatenate([down_master, up_master.T, out_master], axis=0).astype(low_type)
    gathered = lax.all_gather(shards, both, axis=0)
    if heights[1] % 16 == 0:

        def from_slab(first, height):
            return gathered, pl.BlockSpec(
                (device_total, height, model_width),
                lambda *_: (0, first // height, 0),
                pipeline_mode=pl.Buffered(1),
            )

    else:

        def from_slab(first, height):
            part = gathered[:, first : first + height].reshape(-1, model_width // row_devices, model_width)
            return part, whole_spec(part)

    w_down = from_slab(0, heights[3])
    w_up = from_slab(heights[3], heights[2])
    w_out = from_slab(heights[3] + heights[2], heights[1])
    level_flat = noise_levels.reshape(frame_total)
    levels_all = lax.all_gather(level_flat, "frame", axis=0, tiled=True)
    frames_all = frame_devices * frame_total
    frames_each = frames_all // device_total
    level_rows = table_master.shape[0]
    my_levels = device_index * level_rows + jnp.arange(level_rows, dtype=jnp.int32)
    level_hot = levels_all[:, None] == my_levels[None, :]
    found = jnp.dot(
        level_hot.astype(low_type),
        lax.optimization_barrier(table_master.astype(low_type)),
        preferred_element_type=full_type,
    )

    def to_all(value):
        return lax.all_to_all(value, both, split_axis=0, concat_axis=0, tiled=True)

    def from_all(value):
        return to_all(jnp.broadcast_to(value[None], (device_total,) + value.shape))

    embedded_mine = jnp.sum(
        to_all(found.reshape(device_total, frames_each, model_width)), axis=0
    )
    embedded_all = from_all(embedded_mine).reshape(frames_all, model_width)
    cond_all = jax.nn.silu(embedded_all).astype(low_type)
    ada_low = lax.optimization_barrier(ada_master.astype(low_type))
    bias_low = lax.optimization_barrier(bias_master.astype(low_type))
    ada_width = ada_master.shape[1]
    mod_columns = jnp.dot(cond_all, ada_low, preferred_element_type=full_type) + bias_low.astype(full_type)
    mod_columns = mod_columns.reshape(frame_devices, 1, frame_total, ada_width)
    mod_columns = jnp.broadcast_to(
        mod_columns, (frame_devices, row_devices, frame_total, ada_width)
    ).reshape(device_total, frame_total, ada_width)
    modulation = jnp.moveaxis(to_all(mod_columns), 0, 1).reshape(frame_total, 6 * model_width)
    grid_shape = (clip_count, frames, rows_dev, columns)
    row_first = lax.axis_index("row") * rows_dev
    time_grid = jnp.broadcast_to(frame_times.astype(full_type)[:, :, None, None], grid_shape)
    row_grid = jnp.broadcast_to(
        (row_first + jnp.arange(rows_dev, dtype=jnp.int32)).astype(full_type)[None, None, :, None],
        grid_shape,
    )
    column_grid = jnp.broadcast_to(
        jnp.arange(columns, dtype=jnp.int32).astype(full_type)[None, None, None, :], grid_shape
    )
    angles = rotary_angles(time_grid, row_grid, column_grid).reshape(clip_count, seq_local, HD // 2)
    flat_angles = angles.reshape(token_total, HD // 2)
    pair_sign = jnp.tile(jnp.array([-1.0, 1.0], full_type), HD)
    cosine = jnp.tile(jnp.repeat(jnp.cos(flat_angles), 2, axis=1), (1, 2))
    sine = jnp.tile(jnp.repeat(jnp.sin(flat_angles), 2, axis=1), (1, 2)) * pair_sign
    tile_count = token_total // 256
    mod = modulation.reshape(tile_count, frame_total // tile_count, 6 * model_width)
    me = lax.axis_index("row").astype(jnp.int32).reshape(1)
    tokens_flat = tokens.reshape(clip_count, seq_local, model_width)
    cotangent_flat = cotangent.reshape(clip_count, seq_local, model_width)
    clips = range(clip_count)
    hidden_one, pieces = [], []
    for clip in clips:
        hidden, *slots = project(me, clip, tokens_flat, mod, cosine, sine, w_qkv, row_devices)
        hidden_one.append(hidden[0])
        pieces.append(swap(slots))
    attended, full, logs = [], [], []
    for clip in clips:
        slots, full_clip, log_clip = attend(pieces[clip])
        attended.append(swap(slots))
        full.append(full_clip)
        logs.append(log_clip)
    d_attended, middles = [], []
    for clip in clips:
        slots, others = middle(
            me, clip, tokens_flat, cotangent_flat, mod, w_out, w_up, w_down, attended[clip]
        )
        d_attended.append(swap(slots))
        middles.append(others)
    block_out = jnp.concatenate([item[0] for item in middles], axis=0).reshape(shape_five)
    att_low, hidden_two, activated, d_branch_two, d_up, d_branch_one, d_middle, two_sums = (
        [item[index] for item in middles] for index in range(1, 9)
    )
    early = scatter_steps(
        [[(activated, d_branch_two)], [(d_up, hidden_two), (att_low, d_branch_one)]], "early"
    )

    def after(value, state):
        return [held(value[0], *state), *value[1:]]

    state = next(early)
    d_pieces = []
    for clip in clips:
        slots = attend_back(pieces[clip], after(d_attended[clip], state), full[clip], logs[clip])
        d_pieces.append(swap(slots))
        state = early.send([slots[0]])
    lasts = []
    for clip in clips:
        lasts.append(
            last(
                me, clip, tokens_flat, mod, cosine, sine, w_qkv, d_middle[clip],
                after(d_pieces[clip], state),
            )
        )
        state = early.send([lasts[clip][2]])
    early_sum = finished(early, state)
    input_grad = jnp.concatenate([item[1] for item in lasts], axis=0).reshape(shape_five)
    late = scatter_steps([[([item[0] for item in lasts], hidden_one)]], "late")
    state = next(late)
    one_sums = [item[2] for item in lasts]
    one_sums[0] = held(one_sums[0], *state)
    d_modulation = frame_sums(one_sums, two_sums)
    g_qkv = finished(late, state)

    mod_parts = to_all(jnp.moveaxis(d_modulation.reshape(frame_total, device_total, ada_width), 1, 0))
    mod_mine = (
        jnp.sum(mod_parts.reshape(frame_devices, row_devices, frame_total, ada_width), axis=1)
        .reshape(frames_all, ada_width)
        .astype(low_type)
    )
    g_ada = jnp.einsum("fd,fe->de", cond_all, mod_mine, preferred_element_type=full_type)
    g_bias = jnp.sum(mod_mine.astype(full_type), axis=0)
    d_cond_parts = jnp.einsum("fe,de->fd", mod_mine, ada_low, preferred_element_type=full_type)
    d_cond = jnp.sum(to_all(d_cond_parts.reshape(device_total, frames_each, model_width)), axis=0)
    d_embedded_mine = jax.vjp(jax.nn.silu, embedded_mine)[1](d_cond)[0]
    d_embedded = from_all(d_embedded_mine).reshape(frames_all, model_width)
    g_table = jnp.dot(level_hot.astype(full_type).T, d_embedded, precision=highest)
    g_down = early_sum[: heights[3]]
    g_up = early_sum[heights[3] : heights[3] + heights[2]]
    g_out = early_sum[heights[3] + heights[2] :]
    muon_grads = (g_qkv, g_out, g_up, g_down)
    flipped = (True, False, True, False)

    def tall(value, member):
        return value.T if flipped[member] else value

    muon_moments = (qkv_momentum, out_momentum, up_momentum, down_momentum)
    muon_masters = (qkv_master, out_master, up_master, down_master)
    factors = (math.sqrt(3.0), 1.0, math.sqrt(FF / D), math.sqrt(FF / D))
    adam_local = jnp.sum(g_ada * g_ada) + jnp.sum(g_table * g_table) + jnp.sum(g_bias * g_bias)
    local_total = adam_local + sum((jnp.sum(item * item) for item in muon_grads))
    norm_value = jnp.sqrt(jnp.sum(from_all(jnp.full((1, 128), local_total))[:, 0, 0]))
    clip_factor = jnp.minimum(1.0, clip_limit / (norm_value + 1e-06))
    moments_new = []
    updates = []
    slot_rows = max(heights)
    for member in range(4):
        clipped = clip_factor * muon_grads[member]
        moment = momentum_decay * tall(muon_moments[member], member) + clipped
        update = (clipped + momentum_decay * moment).astype(low_type)
        moments_new.append(tall(moment, member))
        updates.append(jnp.pad(update, ((0, slot_rows - heights[member]), (0, 0))))
    slab = jnp.stack(updates)
    groups = frame_devices // 2
    group_index = lax.axis_index("frame") >> 1

    def frame_swap(slots):
        out = [slots[0]]
        for slot in range(1, groups):
            pairs = [(index, index ^ (2 * slot)) for index in range(frame_devices)]
            out.append(lax.ppermute(slots[slot], "frame", pairs))
        return out

    mine = jnp.concatenate(
        frame_swap(
            [
                lax.dynamic_index_in_dim(slab, (group_index ^ slot) & 3, 0, keepdims=False)
                for slot in range(groups)
            ]
        ),
        axis=0,
    )

    def row_partner(value, bit):
        return lax.ppermute(value, "row", [(index, index ^ (1 << bit)) for index in range(row_devices)])

    row_bits = row_devices.bit_length() - 1
    cut = mine.shape[0] // 2
    grown = [mine[:cut], mine[cut:]]
    for step in range(row_bits):
        grown = [
            jnp.concatenate([grown[0], row_partner(grown[0], step)], axis=0),
            jnp.concatenate([grown[1], row_partner(grown[1], row_bits - 1 - step)], axis=0),
        ]
    others = [
        lax.ppermute(item, "frame", [(index, index ^ 1) for index in range(frame_devices)]) for item in grown
    ]
    ortho_rows = newton([*grown, *others], mine).reshape(groups, slot_rows, model_width)
    ortho_slots = jnp.stack(frame_swap([ortho_rows[slot] for slot in range(groups)]))
    ortho_mine = [
        lax.dynamic_index_in_dim(ortho_slots, (group_index & 3) ^ member, 0, keepdims=False)
        for member in range(4)
    ]
    blocks = [tall(ortho_mine[member][: heights[member]].astype(full_type), member) for member in range(4)]
    masters_new = []
    for member in range(4):
        ortho = blocks[member]
        masters_new.append(
            muon_masters[member] * (1.0 - muon_rate * weight_decay)
            - muon_rate * factors[member] * ortho
        )
    step_value = step_count.astype(full_type)[0]
    ada_first_new, ada_second_new, ada_master_new = adam_update(
        g_ada, ada_first, ada_second, ada_master, 0.03, clip_factor, step_value
    )
    table_clipped = clip_factor * g_table
    table_first_new, table_second_new, table_master_new = adam_update(
        g_table, table_first, table_second, table_master, 0.5, clip_factor, step_value
    )
    bias_first_new, bias_second_new, bias_master_new = adam_update(
        g_bias, bias_first, bias_second, bias_master, 0.5, clip_factor, step_value
    )
    return (
        block_out,
        input_grad,
        norm_value.reshape(1),
        moments_new[0],
        masters_new[0],
        moments_new[1],
        masters_new[1],
        moments_new[2],
        masters_new[2],
        moments_new[3],
        masters_new[3],
        ada_first_new,
        ada_second_new,
        ada_master_new,
        table_first_new,
        table_clipped,
        table_master_new,
        bias_first_new,
        bias_second_new,
        bias_master_new,
    )


def solution(mesh):
    return jax.shard_map(
        per_device,
        mesh=mesh,
        in_specs=(
            P("frame", None, "row", None, None),
            P("frame", None, "row", None, None),
            P("frame", None),
            P("frame", None),
            P(),
            P(None, ("frame", "row")),
            P(None, ("frame", "row")),
            P(("frame", "row"), None),
            P(("frame", "row"), None),
            P(None, ("frame", "row")),
            P(None, ("frame", "row")),
            P(("frame", "row"), None),
            P(("frame", "row"), None),
            P(None, ("frame", "row")),
            P(None, ("frame", "row")),
            P(None, ("frame", "row")),
            P(("frame", "row"), None),
            P(("frame", "row"), None),
            P(("frame", "row"), None),
            P(("frame", "row")),
            P(("frame", "row")),
            P(("frame", "row")),
        ),
        out_specs=(
            P("frame", None, "row", None, None),
            P("frame", None, "row", None, None),
            P(),
            P(None, ("frame", "row")),
            P(None, ("frame", "row")),
            P(("frame", "row"), None),
            P(("frame", "row"), None),
            P(None, ("frame", "row")),
            P(None, ("frame", "row")),
            P(("frame", "row"), None),
            P(("frame", "row"), None),
            P(None, ("frame", "row")),
            P(None, ("frame", "row")),
            P(None, ("frame", "row")),
            P(("frame", "row"), None),
            P(("frame", "row"), None),
            P(("frame", "row"), None),
            P(("frame", "row")),
            P(("frame", "row")),
            P(("frame", "row")),
        ),
        check_vma=False,
    )
```

```python
import functools
import math

import jax
import jax.numpy as jnp
from jax import lax
from jax.experimental import pallas as pl
from jax.experimental.pallas import tpu as pltpu
from jax.sharding import PartitionSpec as P

D = 1024
HEADS = 16
HD = 64
FF = 4096


highest = lax.Precision.HIGHEST
newton_one = 3.4445
newton_two = -4.775
newton_three = 2.0315
momentum_decay = 0.95
muon_rate = 1.5
weight_decay = 0.01
beta_first = 0.9
beta_second = 0.95
adam_floor = 1e-08
norm_floor = 1e-06
clip_limit = 1.0
rotary_base = 10000.0


def rotary_angles(time_grid, row_grid, column_grid):
    quarter_pairs = HD // 4
    eighth_pairs = HD // 8
    time_rates = rotary_base ** (-jnp.arange(quarter_pairs, dtype=jnp.float32) / quarter_pairs)
    space_rates = rotary_base ** (-jnp.arange(eighth_pairs, dtype=jnp.float32) / eighth_pairs)
    return jnp.concatenate(
        [
            time_grid[..., None] * time_rates,
            row_grid[..., None] * space_rates,
            column_grid[..., None] * space_rates,
        ],
        axis=-1,
    )


def adam_update(grad_item, first, second, master, rate, clip_factor, step_value):
    clipped = clip_factor * grad_item
    first_new = beta_first * first + (1.0 - beta_first) * clipped
    second_new = beta_second * second + (1.0 - beta_second) * clipped * clipped
    first_fix = 1.0 - beta_first**step_value
    second_fix = 1.0 - beta_second**step_value
    master_new = master * (1.0 - rate * weight_decay) - rate * (first_new / first_fix) / (
        jnp.sqrt(second_new / second_fix) + adam_floor
    )
    return (first_new, second_new, master_new)


def halves(value, dim, axis, bit):
    mine = (lax.axis_index(axis) >> bit) & 1
    keep = lax.dynamic_index_in_dim(value, mine, dim, keepdims=False)
    send = lax.dynamic_index_in_dim(value, 1 - mine, dim, keepdims=False)
    return keep, send.astype(jnp.bfloat16)


def joined(keep, send, axis, bit):
    size = lax.axis_size(axis)
    came = lax.ppermute(send, axis, [(index, index ^ (1 << bit)) for index in range(size)])
    return keep + came.astype(jnp.float32)


def held(value, *others):
    if not others:
        return value
    return lax.optimization_barrier((value, *others))[0]


def scatter_steps(groups, name, by_frame, ready):
    frame_bits = lax.axis_size("frame").bit_length() - 1
    row_bits = lax.axis_size("row").bit_length() - 1
    row, frame = lax.axis_index("row"), lax.axis_index("frame")
    numbers = jnp.stack([frame & 1, row & 1, row >> (row_bits - 1), (frame >> 1) & 1]).astype(jnp.int32)
    numbers = held(numbers, *ready)
    size = lax.axis_size("frame")
    came = []
    for at, group in enumerate(groups):
        send = send_sums(numbers, group, f"{name}_send_{at}")
        came.append(lax.ppermute(send, "frame", [(index, index ^ 1) for index in range(size)]))
        numbers = held(numbers, send)
    keep, send = keep_sums(numbers, groups, came, name + "_keep", by_frame)
    hold = yield send
    names = [("frame", bit) for bit in reversed(range(1, frame_bits))]
    names += [("row", bit) for bit in reversed(range(row_bits))]
    rest = [("frame", bit) for bit in range(1, frame_bits)]
    side_names = []
    if by_frame:
        names.remove(("frame", 1))
        rest.remove(("frame", 1))
        value = joined(held(keep[0], *hold), send[0], "frame", 1)
        value = value.reshape((2,) * len(names) + value.shape[2:])
        width = value.shape[-1] // 2
        keep, send = [], []
        for side in range(2):
            bit = 0 if side == 0 else row_bits - 1
            side_names.append([item for item in names if item != ("row", bit)])
            part = value[..., side * width : (side + 1) * width]
            kept, sent = halves(part, names.index(("row", bit)), "row", bit)
            keep.append(kept)
            send.append(sent)
        hold = yield send
    else:
        for side in range(2):
            bit = 0 if side == 0 else row_bits - 1
            side_names.append([item for item in names if item != ("row", bit)])
            shape = (2,) * (len(names) - 1) + keep[side].shape[2:]
            keep[side] = keep[side].reshape(shape)
            send[side] = send[side].reshape(shape)
    for step in range(row_bits):
        parts = []
        for side in range(2):
            bit = step if side == 0 else row_bits - 1 - step
            parts.append(joined(held(keep[side], *hold), send[side], "row", bit))
        if step == row_bits - 1:
            break
        for side in range(2):
            bit = step + 1 if side == 0 else row_bits - 2 - step
            dim = side_names[side].index(("row", bit))
            side_names[side].pop(dim)
            keep[side], send[side] = halves(parts[side], dim, "row", bit)
        hold = yield send
    value = jnp.concatenate(parts, axis=-1)
    names = [item for item in names if item[0] == "frame"]
    for item in rest:
        dim = names.index(item)
        names.pop(dim)
        keep, send = halves(value, dim, *item)
        hold = yield [send]
        value = joined(held(keep, *hold), send, *item)
    yield value


def finished(steps, state):
    while isinstance(state, list):
        state = steps.send([])
    return state


def split_two(value):
    high = value.astype(jnp.bfloat16)
    return high, (value - high.astype(jnp.float32)).astype(jnp.bfloat16)


def dot_low(left, right):
    return lax.dot_general(left, right, (((1,), (0,)), ((), ())), preferred_element_type=jnp.float32)


def dot_nt(left, right):
    return lax.dot_general(left, right, (((1,), (1,)), ((), ())), preferred_element_type=jnp.float32)


def dot_tn(left, right):
    return lax.dot_general(left, right, (((0,), (0,)), ((), ())), preferred_element_type=jnp.float32)


MIB = 1024 * 1024


def vmem_params(mib, semantics=None):
    return pltpu.CompilerParams(vmem_limit_bytes=mib * MIB, dimension_semantics=semantics)


def whole_spec(array):
    zeros = (0,) * array.ndim
    return pl.BlockSpec(array.shape, lambda *_: zeros, pipeline_mode=pl.Buffered(1))


def turned(value, cosine, sine):
    even = lax.broadcasted_iota(jnp.int32, value.shape, 1) % 2 == 0
    width = value.shape[1]
    swapped = jnp.where(even, pltpu.roll(value, width - 1, 1), pltpu.roll(value, 1, 1))
    return value * cosine + swapped * sine


def framed(value, frames):
    rows, width = value.shape
    return value.reshape(frames, rows // frames, width)


def norm_parts(value):
    mean = jnp.mean(value, axis=-1, keepdims=True)
    centered = value - mean
    root = lax.rsqrt(jnp.mean(centered * centered, axis=-1, keepdims=True) + norm_floor)
    return centered * root, root


def project_kernel(slots, me_ref, x_ref, mod_ref, cos_ref, sin_ref, w_ref, hid_ref, *out_refs):
    frames = mod_ref.shape[1]
    group = D // slots
    normed, _ = norm_parts(x_ref[0].astype(jnp.float32))
    normed = framed(normed, frames)
    shift = mod_ref[0, :, 0:D][:, None, :]
    scaling = mod_ref[0, :, D : 2 * D][:, None, :]
    hidden = (normed * (1.0 + scaling) + shift).reshape(x_ref.shape[1], D).astype(jnp.bfloat16)
    hid_ref[0] = hidden
    cosine = cos_ref[...]
    sine = sin_ref[...]
    me = me_ref[0]
    for slot in range(slots):
        peer = me ^ slot
        for part in range(3):
            rows = pl.ds(pl.multiple_of(part * D + peer * group, group), group)
            value = dot_nt(hidden, w_ref[rows, :])
            if part == 2:
                for pair in range(group // 128):
                    out_refs[pair * slots + slot][part] = value[:, pair * 128 : (pair + 1) * 128].astype(
                        jnp.bfloat16
                    )
                continue
            for pair in range(group // 128):
                piece = turned(value[:, pair * 128 : (pair + 1) * 128], cosine, sine)
                if part == 0:
                    piece = piece * (1.0 / math.sqrt(HD))
                out_refs[pair * slots + slot][part] = piece.astype(jnp.bfloat16)


def project(me, clip, tokens, mod, cosine, sine, w_qkv, slots):
    _, tall_rows, _ = tokens.shape
    tile = 256
    steps = tall_rows // tile
    out_shape = [jax.ShapeDtypeStruct((1, tall_rows, D), jnp.bfloat16)]
    count = D // 128
    out_shape += [jax.ShapeDtypeStruct((3, tall_rows, 128), jnp.bfloat16)] * count
    return pl.pallas_call(
        functools.partial(project_kernel, slots),
        grid=(steps,),
        in_specs=[
            pl.BlockSpec(memory_space=pltpu.SMEM),
            pl.BlockSpec((1, tile, D), lambda i: (clip, i, 0)),
            pl.BlockSpec((1, mod.shape[1], 6 * D), lambda i: (clip * steps + i, 0, 0)),
            pl.BlockSpec((tile, 128), lambda i: (clip * steps + i, 0)),
            pl.BlockSpec((tile, 128), lambda i: (clip * steps + i, 0)),
            whole_spec(w_qkv),
        ],
        out_specs=[pl.BlockSpec((1, tile, D), lambda i: (0, i, 0))]
        + [pl.BlockSpec((3, tile, 128), lambda i: (0, i, 0))] * count,
        out_shape=out_shape,
        compiler_params=vmem_params(60),
        cost_estimate=pl.CostEstimate(
            flops=6 * tall_rows * D * D, bytes_accessed=10 * MIB, transcendentals=0
        ),
        name="project",
    )(me, tokens, mod, cosine, sine, w_qkv)


def head_mask(shape, head, axis):
    return lax.broadcasted_iota(jnp.int32, shape, axis) // HD == head


def attend_kernel(slots, tile, *refs):
    ins, outs = refs[:slots], refs[slots : 2 * slots]
    full_ref, log_ref, qs, ks, vs = refs[2 * slots :]
    length = ins[0].shape[1]
    for slot in range(slots):
        rows = slice(slot * length, (slot + 1) * length)
        qs[rows, :] = ins[slot][0]
        ks[rows, :] = ins[slot][1]
        vs[rows, :] = ins[slot][2]

    def one(index, carry):
        rows = pl.ds(pl.multiple_of(index * tile, tile), tile)
        query = qs[rows, :]
        first = head_mask((tile, 128), 0, 1)
        parts = []
        logs = []
        for head in range(2):
            masked = jnp.where(first if head == 0 else ~first, query, jnp.zeros_like(query))
            scores = dot_nt(masked, ks[...])
            top = jnp.max(scores, axis=-1, keepdims=True)
            raised = jnp.exp(scores - top)
            total = jnp.sum(raised, axis=-1, keepdims=True)
            parts.append(dot_low(raised.astype(jnp.bfloat16), vs[...]) * (1.0 / total))
            logs.append(top + jnp.log(total))
        full_ref[rows, :] = jnp.where(first, parts[0], parts[1])
        log_ref[rows, :] = jnp.where(first, logs[0], logs[1])
        return carry

    lax.fori_loop(0, slots * length // tile, one, 0)
    for slot in range(slots):
        rows = slice(slot * length, (slot + 1) * length)
        outs[slot][...] = full_ref[rows, :].astype(jnp.bfloat16)


def attend(pieces):
    slots = len(pieces)
    _, length, group = pieces[0].shape
    total = slots * length
    scratch = pltpu.VMEM((total, 128), jnp.bfloat16)
    outs = pl.pallas_call(
        functools.partial(attend_kernel, slots, 256),
        grid=(group // 128,),
        in_specs=[pl.BlockSpec((3, length, 128), lambda i: (0, 0, i))] * slots,
        out_specs=[pl.BlockSpec((length, 128), lambda i: (0, i))] * slots
        + [pl.BlockSpec((total, 128), lambda i: (0, i))] * 2,
        out_shape=[jax.ShapeDtypeStruct((length, group), jnp.bfloat16)] * slots
        + [jax.ShapeDtypeStruct((total, group), jnp.float32)] * 2,
        scratch_shapes=[scratch] * 3,
        compiler_params=vmem_params(60),
        cost_estimate=pl.CostEstimate(
            flops=16 * total * total * group, bytes_accessed=8 * MIB, transcendentals=total * total * 4
        ),
        name="attend",
    )(*pieces)
    return outs[:slots], outs[slots], outs[slots + 1]


def attend_back_kernel(slots, tile, *refs):
    ins, grads = refs[:slots], refs[slots : 2 * slots]
    full_ref, log_ref = refs[2 * slots : 2 * slots + 2]
    outs = refs[2 * slots + 2 : 3 * slots + 2]
    qs, ks, vs, gs, q_turned, g_turned, dq, dk, dv = refs[3 * slots + 2 :]
    length = ins[0].shape[1]
    total = slots * length
    for slot in range(slots):
        rows = slice(slot * length, (slot + 1) * length)
        qs[rows, :] = ins[slot][0]
        ks[rows, :] = ins[slot][1]
        vs[rows, :] = ins[slot][2]
        gs[rows, :] = grads[slot][...]
        q_turned[:, rows] = ins[slot][0].T
        g_turned[:, rows] = grads[slot][...].T
    dk[...] = jnp.zeros_like(dk)
    dv[...] = jnp.zeros_like(dv)

    def one(index, carry):
        rows = pl.ds(pl.multiple_of(index * tile, tile), tile)
        first = head_mask((tile, 128), 0, 1)
        upper = head_mask((128, tile), 0, 0)
        query, grad = qs[rows, :], gs[rows, :]
        query_t, grad_t = q_turned[:, rows], g_turned[:, rows]
        product = grad.astype(jnp.float32) * full_ref[rows, :]
        masks = (first, ~first)
        masks_t = (upper, ~upper)
        zero = jnp.zeros_like(query)
        zero_t = jnp.zeros_like(query_t)
        q_low = [jnp.where(mask, query, zero) for mask in masks]
        g_low = [jnp.where(mask, grad, zero) for mask in masks]
        qt_low = [jnp.where(mask, query_t, zero_t) for mask in masks_t]
        gt_low = [jnp.where(mask, grad_t, zero_t) for mask in masks_t]
        inner = [jnp.sum(jnp.where(mask, product, 0.0), axis=-1, keepdims=True) for mask in masks]
        logs = [log_ref[rows, 0:1], log_ref[rows, HD : HD + 1]]

        def inside(k_index, sums):
            at = pl.ds(pl.multiple_of(k_index * tile, tile), tile)
            key, value = ks[at, :], vs[at, :]
            out = []
            for head in range(2):
                probs = jnp.exp(dot_nt(q_low[head], key) - logs[head])
                d_probs = dot_nt(g_low[head], value)
                d_scores = (probs * (d_probs - inner[head])).astype(jnp.bfloat16)
                dv[:, at] += dot_low(gt_low[head], probs.astype(jnp.bfloat16))
                dk[:, at] += dot_low(qt_low[head], d_scores)
                out.append(sums[head] + dot_low(d_scores, key))
            return tuple(out)

        start = jnp.zeros((tile, 128), jnp.float32)
        sums = lax.fori_loop(0, total // tile, inside, (start, start))
        dq[rows, :] = (jnp.where(first, sums[0], sums[1]) * (1.0 / math.sqrt(HD))).astype(jnp.bfloat16)
        return carry

    lax.fori_loop(0, total // tile, one, 0)
    for slot in range(slots):
        rows = slice(slot * length, (slot + 1) * length)
        outs[slot][0] = dq[rows, :]
        outs[slot][1] = dk[:, rows].T.astype(jnp.bfloat16)
        outs[slot][2] = dv[:, rows].T.astype(jnp.bfloat16)


def attend_back(pieces, grads, full, logs):
    slots = len(pieces)
    _, length, group = pieces[0].shape
    total = slots * length
    low = pltpu.VMEM((total, 128), jnp.bfloat16)
    low_t = pltpu.VMEM((128, total), jnp.bfloat16)
    full_t = pltpu.VMEM((128, total), jnp.float32)
    return pl.pallas_call(
        functools.partial(attend_back_kernel, slots, 512),
        grid=(group // 128,),
        in_specs=[pl.BlockSpec((3, length, 128), lambda i: (0, 0, i))] * slots
        + [pl.BlockSpec((length, 128), lambda i: (0, i))] * slots
        + [pl.BlockSpec((total, 128), lambda i: (0, i))] * 2,
        out_specs=[pl.BlockSpec((3, length, 128), lambda i: (0, 0, i))] * slots,
        out_shape=[jax.ShapeDtypeStruct((3, length, group), jnp.bfloat16)] * slots,
        scratch_shapes=[low] * 4 + [low_t] * 2 + [low] + [full_t] * 2,
        compiler_params=vmem_params(60),
        cost_estimate=pl.CostEstimate(
            flops=40 * total * total * group, bytes_accessed=12 * MIB, transcendentals=total * total * 4
        ),
        name="attend_back",
    )(*pieces, *grads, full, logs)


def part_of(ref, index, size):
    count = size // ref.shape[1]
    return ref[pl.ds(index * count, count)].reshape(size, ref.shape[2])


def middle_kernel(slots, me_ref, x_ref, cot_ref, mod_ref, wo_ref, wu_ref, wd_ref, *refs):
    count = D // 128
    pairs = count // slots
    att_refs = refs[:count]
    datt_refs = refs[count : 2 * count]
    (
        out_ref,
        att_ref,
        h2_ref,
        act_ref,
        db2_ref,
        dup_ref,
        db1_ref,
        dmid_ref,
        sums_ref,
        slope,
    ) = refs[2 * count :]
    frames = mod_ref.shape[1]
    rows = x_ref.shape[1]
    group = D // slots
    me = me_ref[0]

    def mod(index):
        return mod_ref[0, :, index * D : (index + 1) * D][:, None, :]

    def spread(value, index, plus=0.0):
        return (framed(value, frames) * (mod(index) + plus)).reshape(rows, D)

    def frame_sum(value):
        return jnp.sum(framed(value, frames), axis=1)

    branch = jnp.zeros((rows, D), jnp.float32)
    for slot in range(slots):
        at = pl.ds(pl.multiple_of((me ^ slot) * group, group), group)
        piece = jnp.concatenate([att_refs[pair * slots + slot][...] for pair in range(pairs)], axis=1)
        att_ref[:, at] = piece
        branch += dot_low(piece, part_of(wo_ref, me ^ slot, group))
    middle = x_ref[0].astype(jnp.float32) + spread(branch, 2)
    normed, root = norm_parts(middle)
    hidden = (framed(spread(normed, 4, 1.0), frames) + mod(3)).reshape(rows, D).astype(jnp.bfloat16)
    h2_ref[...] = hidden
    wide = 1024
    curve = math.sqrt(2.0 / math.pi)
    branch_two = jnp.zeros((rows, D), jnp.float32)
    for first in range(0, FF, wide):
        cut = slice(first, first + wide)
        up = dot_nt(hidden, part_of(wu_ref, first // wide, wide))
        square = up * up
        bent = jnp.tanh(curve * up * (1.0 + 0.044715 * square))
        half = 0.5 * (1.0 + bent)
        active = (up * half).astype(jnp.bfloat16)
        slope[:, cut] = half + 0.5 * up * (1.0 - bent * bent) * (curve * (1.0 + 3 * 0.044715 * square))
        act_ref[:, cut] = active
        branch_two += dot_low(active, part_of(wd_ref, first // wide, wide))
    cot = cot_ref[0].astype(jnp.float32)
    out_ref[0] = (middle + spread(branch_two, 5)).astype(jnp.bfloat16)
    sums_ref[0, 3] = frame_sum(cot * branch_two)
    d_branch_two = spread(cot, 5).astype(jnp.bfloat16)
    db2_ref[...] = d_branch_two
    d_hidden = jnp.zeros((rows, D), jnp.float32)
    for first in range(0, FF, wide):
        cut = slice(first, first + wide)
        d_up = (dot_nt(d_branch_two, part_of(wd_ref, first // wide, wide)) * slope[:, cut]).astype(jnp.bfloat16)
        dup_ref[:, cut] = d_up
        d_hidden += dot_low(d_up, part_of(wu_ref, first // wide, wide))
    sums_ref[0, 1] = frame_sum(d_hidden)
    sums_ref[0, 2] = frame_sum(d_hidden * normed)
    inner = spread(d_hidden, 4, 1.0)
    d_middle = cot + root * (
        inner
        - jnp.mean(inner, axis=-1, keepdims=True)
        - normed * jnp.mean(inner * normed, axis=-1, keepdims=True)
    )
    dmid_ref[...] = d_middle
    sums_ref[0, 0] = frame_sum(d_middle * branch)
    d_branch = spread(d_middle, 2).astype(jnp.bfloat16)
    db1_ref[...] = d_branch
    for slot in range(slots):
        value = dot_nt(d_branch, part_of(wo_ref, me ^ slot, group)).astype(jnp.bfloat16)
        for pair in range(pairs):
            datt_refs[pair * slots + slot][...] = value[:, pair * 128 : (pair + 1) * 128]


def middle(me, clip, tokens, cotangent, mod, w_out, w_up, w_down, attended, slots):
    count = len(attended)
    _, length, _ = tokens.shape
    tile = 256
    steps = length // tile
    frames = mod.shape[1]
    low = jnp.bfloat16

    def flat(width, kind=low):
        return jax.ShapeDtypeStruct((length, width), kind)

    def flat_spec(width):
        return pl.BlockSpec((tile, width), lambda i: (i, 0))

    outs = pl.pallas_call(
        functools.partial(middle_kernel, slots),
        grid=(steps,),
        in_specs=[
            pl.BlockSpec(memory_space=pltpu.SMEM),
            pl.BlockSpec((1, tile, D), lambda i: (clip, i, 0)),
            pl.BlockSpec((1, tile, D), lambda i: (clip, i, 0)),
            pl.BlockSpec((1, frames, 6 * D), lambda i: (clip * steps + i, 0, 0)),
            *(item[1] for item in (w_out, w_up, w_down)),
        ]
        + [flat_spec(128)] * count,
        out_specs=[flat_spec(128)] * count
        + [pl.BlockSpec((1, tile, D), lambda i: (0, i, 0))]
        + [flat_spec(width) for width in (D, D, FF, D, FF, D, D)]
        + [pl.BlockSpec((1, 4, frames, D), lambda i: (i, 0, 0, 0))],
        out_shape=[flat(128)] * count
        + [jax.ShapeDtypeStruct((1, length, D), low)]
        + [flat(D), flat(D), flat(FF), flat(D), flat(FF), flat(D), flat(D, jnp.float32)]
        + [jax.ShapeDtypeStruct((steps, 4, frames, D), jnp.float32)],
        scratch_shapes=[pltpu.VMEM((tile, FF), jnp.float32)],
        compiler_params=vmem_params(60),
        cost_estimate=pl.CostEstimate(
            flops=2 * length * D * (2 * D + 4 * FF), bytes_accessed=40 * MIB, transcendentals=length * FF
        ),
        name="middle",
    )(me, tokens, cotangent, mod, *(item[0] for item in (w_out, w_up, w_down)), *attended)
    return outs[:count], outs[count:]


def last_kernel(slots, me_ref, x_ref, mod_ref, cos_ref, sin_ref, w_ref, dmid_ref, *refs):
    count = D // 128
    pairs = count // slots
    pieces = refs[:count]
    dproj_ref, grad_ref, sums_ref = refs[count:]
    frames = mod_ref.shape[1]
    rows = x_ref.shape[1]
    group = D // slots
    me = me_ref[0]
    cosine = cos_ref[...]
    sine = -sin_ref[...]
    d_hidden = jnp.zeros((rows, D), jnp.float32)
    for slot in range(slots):
        peer = me ^ slot
        for part in range(3):
            base = pl.multiple_of(part * D + peer * group, group)
            if part == 2:
                value = jnp.concatenate([pieces[pair * slots + slot][part] for pair in range(pairs)], axis=1)
            else:
                value = jnp.concatenate(
                    [
                        turned(pieces[pair * slots + slot][part].astype(jnp.float32), cosine, sine)
                        for pair in range(pairs)
                    ],
                    axis=1,
                ).astype(jnp.bfloat16)
            dproj_ref[:, pl.ds(base, group)] = value
            d_hidden += dot_low(value, w_ref[pl.ds(base, group), :])
    normed, root = norm_parts(x_ref[0].astype(jnp.float32))
    scaling = mod_ref[0, :, D : 2 * D][:, None, :]
    sums_ref[0, 0] = jnp.sum(framed(d_hidden, frames), axis=1)
    sums_ref[0, 1] = jnp.sum(framed(d_hidden * normed, frames), axis=1)
    inner = (framed(d_hidden, frames) * (1.0 + scaling)).reshape(rows, D)
    grad_ref[0] = dmid_ref[...] + root * (
        inner
        - jnp.mean(inner, axis=-1, keepdims=True)
        - normed * jnp.mean(inner * normed, axis=-1, keepdims=True)
    )


def last(me, clip, tokens, mod, cosine, sine, w_qkv, d_middle, pieces, slots):
    count = len(pieces)
    _, length, _ = tokens.shape
    tile = 256
    steps = length // tile
    frames = mod.shape[1]
    return pl.pallas_call(
        functools.partial(last_kernel, slots),
        grid=(steps,),
        in_specs=[
            pl.BlockSpec(memory_space=pltpu.SMEM),
            pl.BlockSpec((1, tile, D), lambda i: (clip, i, 0)),
            pl.BlockSpec((1, frames, 6 * D), lambda i: (clip * steps + i, 0, 0)),
            pl.BlockSpec((tile, 128), lambda i: (clip * steps + i, 0)),
            pl.BlockSpec((tile, 128), lambda i: (clip * steps + i, 0)),
            whole_spec(w_qkv),
            pl.BlockSpec((tile, D), lambda i: (i, 0)),
        ]
        + [pl.BlockSpec((3, tile, 128), lambda i: (0, i, 0))] * count,
        out_specs=[
            pl.BlockSpec((tile, 3 * D), lambda i: (i, 0)),
            pl.BlockSpec((1, tile, D), lambda i: (0, i, 0)),
            pl.BlockSpec((1, 2, frames, D), lambda i: (i, 0, 0, 0)),
        ],
        out_shape=[
            jax.ShapeDtypeStruct((length, 3 * D), jnp.bfloat16),
            jax.ShapeDtypeStruct((1, length, D), jnp.float32),
            jax.ShapeDtypeStruct((steps, 2, frames, D), jnp.float32),
        ],
        compiler_params=vmem_params(60),
        cost_estimate=pl.CostEstimate(
            flops=6 * length * D * D, bytes_accessed=20 * MIB, transcendentals=0
        ),
        name="last",
    )(me, tokens, mod, cosine, sine, w_qkv, d_middle, *pieces)


def member_value(refs, member, doubled, parity):
    left = refs[4 * member : 4 * member + 2]
    right = refs[4 * member + 2 : 4 * member + 4]
    value = dot_tn(left[0][...], right[0][...]) + dot_tn(left[1][...], right[1][...])
    if doubled:
        half = value.shape[0] // 2
        value = jnp.where(parity == 0, value[:half], value[half:])
    return value


def send_kernel(doubled, number_ref, *refs):
    out_ref = refs[-1]
    rows = out_ref.shape[1]
    first = 0
    for member in range(len(doubled)):
        value = member_value(refs, member, doubled[member], 1 - number_ref[0])
        height = value.shape[0] // rows
        out_ref[0, :, first : first + height, :] = value.reshape(rows, height, D).astype(out_ref.dtype)
        first += height


def keep_kernel(doubled, counts, number_ref, *refs):
    members = len(doubled)
    came_refs = refs[4 * members : 4 * members + len(counts)]
    keep_refs, send_refs = refs[-4:-2], refs[-2:]
    half_rows = keep_refs[0].shape[1]
    width = D // 2
    first = 0
    member = 0
    for came_ref, count in zip(came_refs, counts):
        inside = 0
        for _ in range(count):
            value = member_value(refs, member, doubled[member], number_ref[0])
            height = value.shape[0] // (2 * half_rows)
            rows = slice(first, first + height)
            parts = [
                value[row * height : (row + 1) * height]
                + came_ref[0, row, inside : inside + height, :].astype(jnp.float32)
                for row in range(2 * half_rows)
            ]
            for place in range(half_rows):
                for side in range(2):
                    cut = slice(side * width, (side + 1) * width)
                    low = 2 * place if side == 0 else place
                    high = low + (1 if side == 0 else half_rows)
                    upper = number_ref[1 + side] == 1
                    zero, one = parts[low][:, cut], parts[high][:, cut]
                    keep_refs[side][0, place, rows, :] = jnp.where(upper, one, zero)
                    send_refs[side][0, place, rows, :] = jnp.where(upper, zero, one).astype(jnp.bfloat16)
            first += height
            inside += height
            member += 1


def keep_frame_kernel(doubled, counts, number_ref, *refs):
    members = len(doubled)
    came_refs = refs[4 * members : 4 * members + len(counts)]
    keep_ref, send_ref = refs[-2:]
    rows = keep_ref.shape[1]
    kept = lax.rem(pl.program_id(0), 2) == number_ref[3]
    first = 0
    member = 0
    for came_ref, count in zip(came_refs, counts):
        inside = 0
        for _ in range(count):
            value = member_value(refs, member, doubled[member], number_ref[0])
            height = value.shape[0] // rows
            value = value.reshape(rows, height, D)
            value += came_ref[0, :, inside : inside + height, :].astype(jnp.float32)
            at = slice(first, first + height)

            @pl.when(kept)
            def _(value=value, at=at):
                keep_ref[0, :, at, :] = value

            @pl.when(jnp.logical_not(kept))
            def _(value=value, at=at):
                send_ref[0, :, at, :] = value.astype(jnp.bfloat16)

            first += height
            inside += height
            member += 1


def weight_specs(pairs, other):
    frame_devices = lax.axis_size("frame")
    specs, operands, doubled = [], [], []
    height = 0
    for left, right in pairs:
        width = left[0].shape[1] // frame_devices
        height += width // lax.axis_size("row")
        doubled.append(width % 128 != 0)
        if doubled[-1]:
            spec = pl.BlockSpec((left[0].shape[0], 2 * width), lambda i, s: (0, i))
        elif other:
            spec = pl.BlockSpec((left[0].shape[0], width), lambda i, s: (0, 2 * i + 1 - s[0]))
        else:
            spec = pl.BlockSpec((left[0].shape[0], width), lambda i, s: (0, 2 * i + s[0]))
        specs += [spec] * 2
        specs += [pl.BlockSpec(right[0].shape, lambda i, s: (0, 0))] * 2
        operands += [*left, *right]
    flops = sum(4 * left[0].shape[0] * left[0].shape[1] * D // 2 for left, _ in pairs)
    return specs, operands, tuple(doubled), height, flops


def send_sums(numbers, pairs, name):
    specs, operands, doubled, height, flops = weight_specs(pairs, True)
    frames, rows = lax.axis_size("frame") // 2, lax.axis_size("row")
    return pl.pallas_call(
        functools.partial(send_kernel, doubled),
        grid_spec=pltpu.PrefetchScalarGridSpec(
            num_scalar_prefetch=1,
            grid=(frames,),
            in_specs=specs,
            out_specs=pl.BlockSpec((1, rows, height, D), lambda i, s: (i, 0, 0, 0)),
        ),
        out_shape=jax.ShapeDtypeStruct((frames, rows, height, D), jnp.bfloat16),
        compiler_params=vmem_params(60),
        cost_estimate=pl.CostEstimate(flops=flops, bytes_accessed=20 * MIB, transcendentals=0),
        name=name,
    )(numbers, *operands)


def keep_sums(numbers, groups, came, name, by_frame):
    pairs = [pair for group in groups for pair in group]
    specs, operands, doubled, height, flops = weight_specs(pairs, False)
    frames, rows = lax.axis_size("frame") // 2, lax.axis_size("row")
    specs += [pl.BlockSpec((1,) + item.shape[1:], lambda i, s: (i, 0, 0, 0)) for item in came]
    if by_frame:
        kernel = keep_frame_kernel
        shape = (frames // 2, rows, height, D)
        out_spec = pl.BlockSpec((1,) + shape[1:], lambda i, s: (i // 2, 0, 0, 0))
    else:
        kernel = keep_kernel
        shape = (frames, rows // 2, height, D // 2)
        out_spec = pl.BlockSpec((1,) + shape[1:], lambda i, s: (i, 0, 0, 0))
    each = 1 if by_frame else 2
    outs = pl.pallas_call(
        functools.partial(kernel, doubled, tuple(len(group) for group in groups)),
        grid_spec=pltpu.PrefetchScalarGridSpec(
            num_scalar_prefetch=1, grid=(frames,), in_specs=specs, out_specs=[out_spec] * (2 * each)
        ),
        out_shape=[jax.ShapeDtypeStruct(shape, jnp.float32)] * each
        + [jax.ShapeDtypeStruct(shape, jnp.bfloat16)] * each,
        compiler_params=vmem_params(60),
        cost_estimate=pl.CostEstimate(flops=flops, bytes_accessed=40 * MIB, transcendentals=0),
        name=name,
    )(numbers, *operands, *came)
    return list(outs[:each]), list(outs[each:])


def newton_kernel(rows, unroll, pieces, scale_ref, *refs):
    g_refs, m_refs, out_ref = refs[:pieces], refs[pieces : 2 * pieces], refs[2 * pieces]
    x_ref, a_ref, t_ref, q_ref, eye_ref, ah, al, nh, th, tl, qh, ql, num_ref = refs[2 * pieces + 1 :]
    width = a_ref.shape[0]
    steps = width // rows
    deep = g_refs[0].shape[0]
    a_at, m_at, t_at, shift_at, sum_at = 0, 1, 2, 3, 8

    def block(index):
        return pl.ds(pl.multiple_of(index * rows, rows), rows)

    def each(make):
        def one(index, carry):
            make(index)
            return carry

        lax.fori_loop(0, steps, one, 0, unroll=unroll)

    def mean():
        total = num_ref[sum_at]
        for index in range(1, steps):
            total += num_ref[sum_at + index]
        return total * (1.0 / width)

    for piece in range(pieces):

        def mix(index, carry, piece=piece):
            at = pl.ds(pl.multiple_of(index * 128, 128), 128)
            to = pl.ds(pl.multiple_of(piece * deep + index * 128, 128), 128)
            value = scale_ref[0] * g_refs[piece][at, :].astype(jnp.float32)
            value += scale_ref[1] * m_refs[piece][at, :].astype(jnp.float32)
            x_ref[to, :] = value.astype(jnp.bfloat16)
            return carry

        lax.fori_loop(0, deep // 128, mix, 0)
    eye_ref[...] = jnp.where(
        lax.broadcasted_iota(jnp.int32, (rows, rows), 0) == lax.broadcasted_iota(jnp.int32, (rows, rows), 1),
        1.0,
        0.0,
    )
    squares = 0.0
    for index in range(steps):
        columns = slice(index * rows, (index + 1) * rows)
        value = dot_tn(x_ref[:, columns], x_ref[:, index * rows :])
        t_ref[columns, index * rows :] = value
        for other in range(index + 1, steps):
            there = slice(other * rows, (other + 1) * rows)
            t_ref[there, columns] = t_ref[columns, there].T
        squares += jnp.sum(value[:, :rows] * eye_ref[...])
    inverse = 1.0 / (jnp.sqrt(jnp.full((1, 1), squares, jnp.float32)) + 1e-07)
    scale = jnp.sum(inverse)
    scale = scale * scale
    num_ref[a_at] = squares * scale * (1.0 / width)

    def chunks(index):
        for chunk in range(steps):
            yield chunk, slice(chunk * rows, (chunk + 1) * rows), jnp.where(index == chunk, 1.0, 0.0)

    def first_split(index):
        at = block(index)
        total = 0.0
        for _, cut, here in chunks(index):
            value = t_ref[at, cut] * scale - (here * num_ref[a_at]) * eye_ref[...]
            a_ref[at, cut] = value
            ah[at, cut], al[at, cut] = split_two(value)
            total += jnp.sum(value * value)
        num_ref[sum_at + index] = total

    each(first_split)

    for number in range(5):
        two = number < 2
        shift = num_ref[a_at]
        fix = newton_three * mean()
        num_ref[m_at] = newton_one + newton_two * shift + newton_three * shift * shift + fix
        slope = newton_two + 2.0 * newton_three * shift

        def make_n(index):
            at = block(index)
            total = 0.0
            for _, cut, here in chunks(index):
                value = newton_three * dot_low(ah[at, :], ah[:, cut])
                value += slope * a_ref[at, cut] - (here * fix) * eye_ref[...]
                nh[at, cut] = value.astype(jnp.bfloat16)
                total += jnp.sum(value * a_ref[at, cut])
            num_ref[sum_at + index] = total

        each(make_n)
        much = num_ref[m_at]
        keep_low = number < 4 and number >= 2
        if number == 0:

            def first_q(index):
                at = block(index)
                for _, cut, here in chunks(index):
                    value = nh[at, cut].astype(jnp.float32) + (here * much) * eye_ref[...]
                    q_ref[at, cut] = value
                    qh[at, cut] = value.astype(jnp.bfloat16)

            each(first_q)
        else:

            def next_q(index):
                at = block(index)
                high = qh[at, :]
                rest = ql[at, :] if number >= 3 else None
                for _, cut, _ in chunks(index):
                    value = much * q_ref[at, cut] + dot_low(high, nh[:, cut])
                    if number >= 3:
                        value += dot_low(rest, nh[:, cut])
                    t_ref[at, cut] = value
                for _, cut, _ in chunks(index):
                    value = t_ref[at, cut]
                    first, second = split_two(value)
                    qh[at, cut] = first
                    if number >= 2:
                        ql[at, cut] = second
                    if number < 4:
                        q_ref[at, cut] = value

            each(next_q)
        if number == 4:
            break
        fix_t = mean()
        num_ref[t_at] = shift * much + fix_t

        def make_t(index):
            at = block(index)
            total = 0.0
            for _, cut, here in chunks(index):
                value = dot_low(ah[at, :], nh[:, cut])
                if two:
                    value += dot_low(al[at, :], nh[:, cut])
                near = nh[at, cut].astype(jnp.float32)
                value += shift * near + much * a_ref[at, cut] - (here * fix_t) * eye_ref[...]
                t_ref[at, cut] = value
                if two:
                    th[at, cut], tl[at, cut] = split_two(value)
                else:
                    th[at, cut] = value.astype(jnp.bfloat16)
                total += jnp.sum(value * near)
            num_ref[sum_at + index] = total

        each(make_t)
        fix_a = mean()
        t_shift = num_ref[t_at]
        num_ref[a_at] = t_shift * much + fix_a

        def make_a(index):
            at = block(index)
            total = 0.0
            for _, cut, here in chunks(index):
                value = dot_low(nh[at, :], th[:, cut])
                if two:
                    value += dot_low(nh[at, :], tl[:, cut])
                near = nh[at, cut].astype(jnp.float32)
                value += t_shift * near + much * t_ref[at, cut] - (here * fix_a) * eye_ref[...]
                a_ref[at, cut] = value
                if number == 0:
                    ah[at, cut], al[at, cut] = split_two(value)
                else:
                    ah[at, cut] = value.astype(jnp.bfloat16)
                total += jnp.sum(value * value)
            num_ref[sum_at + index] = total

        each(make_a)

    half = out_ref.shape[0] // 2
    for side in range(2):
        mine = x_ref[side * deep : side * deep + half, :]
        out_ref[side * half : (side + 1) * half, :] = (
            (dot_low(mine, qh[...]) + dot_low(mine, ql[...])) * inverse
        ).astype(out_ref.dtype)


def newton(scales, grads, moments, mine_rows, rows=256, unroll=4):
    width = grads[0].shape[1]
    pieces = len(grads)
    low = pltpu.VMEM((width, width), jnp.bfloat16)
    full = pltpu.VMEM((width, width), jnp.float32)
    vmem = pl.BlockSpec(memory_space=pltpu.VMEM)
    return pl.pallas_call(
        functools.partial(newton_kernel, rows, unroll, pieces),
        out_shape=jax.ShapeDtypeStruct((mine_rows, width), jnp.bfloat16),
        in_specs=[pl.BlockSpec(memory_space=pltpu.SMEM)] + [vmem] * (2 * pieces),
        out_specs=vmem,
        scratch_shapes=[pltpu.VMEM((pieces * grads[0].shape[0], width), jnp.bfloat16)]
        + [full] * 3
        + [pltpu.VMEM((rows, rows), jnp.float32)]
        + [low] * 7
        + [pltpu.SMEM((16,), jnp.float32)],
        compiler_params=vmem_params(60),
        cost_estimate=pl.CostEstimate(flops=60 * 10**9, bytes_accessed=20 * 10**6, transcendentals=0),
        name="newton",
    )(scales, *grads, *moments)


def frame_sums_kernel(count, *refs):
    out_ref = refs[-1]
    ones, twos = refs[:count], refs[count : 2 * count]
    steps, _, frames, _ = ones[0].shape
    at = 0
    for clip in range(count):
        for step in range(steps):
            rows = slice(at, at + frames)
            for index in range(2):
                out_ref[rows, index * D : (index + 1) * D] = ones[clip][step, index]
            for index in range(4):
                out_ref[rows, (index + 2) * D : (index + 3) * D] = twos[clip][step, index]
            at += frames


def frame_sums(ones, twos):
    steps, _, frames, _ = ones[0].shape
    return pl.pallas_call(
        functools.partial(frame_sums_kernel, len(ones)),
        out_shape=jax.ShapeDtypeStruct((len(ones) * steps * frames, 6 * D), jnp.float32),
        in_specs=[pl.BlockSpec(memory_space=pltpu.VMEM)] * (2 * len(ones)),
        out_specs=pl.BlockSpec(memory_space=pltpu.VMEM),
        compiler_params=vmem_params(60),
        cost_estimate=pl.CostEstimate(flops=0, bytes_accessed=MIB, transcendentals=0),
        name="frame_sums",
    )(*ones, *twos)


def swap(slots):
    size = lax.axis_size("row")
    out = [slots[0]]
    for slot in range(1, size):
        out.append(lax.ppermute(slots[slot], "row", [(index, index ^ slot) for index in range(size)]))
    return out


def frame_swap(slots):
    size = lax.axis_size("frame")
    out = [slots[0]]
    for slot in range(1, size // 2):
        pairs = [(index, index ^ (2 * slot)) for index in range(size)]
        out.append(lax.ppermute(slots[slot], "frame", pairs))
    return out


def plane_steps(members):
    size = lax.axis_size("row")
    row_bits = size.bit_length() - 1
    groups = lax.axis_size("frame") // 2
    group_index = lax.axis_index("frame") >> 1
    height = max(item.shape[0] for item in members)
    slab = jnp.stack([jnp.pad(item, ((0, height - item.shape[0]), (0, 0))) for item in members])
    slots = [
        lax.dynamic_index_in_dim(slab, (group_index ^ slot) & 3, 0, keepdims=False) for slot in range(groups)
    ]
    hold = yield slots
    slots = frame_swap(slots)
    slots[0] = held(slots[0], *hold)
    mine = jnp.concatenate(slots, axis=0)
    cut = mine.shape[0] // 2
    grown = [mine[:cut], mine[cut:]]
    for step in range(row_bits):
        hold = yield grown
        for side in range(2):
            bit = step if side == 0 else row_bits - 1 - step
            pairs = [(index, index ^ (1 << bit)) for index in range(size)]
            came = lax.ppermute(grown[side], "row", pairs)
            grown[side] = jnp.concatenate([held(grown[side], *hold), came], axis=0)
    frame_size = lax.axis_size("frame")
    pairs = [(index, index ^ 1) for index in range(frame_size)]
    yield (*grown, *(lax.ppermute(item, "frame", pairs) for item in grown))


def per_device(
    tokens,
    cotangent,
    noise_levels,
    frame_times,
    step_count,
    qkv_master,
    qkv_momentum,
    out_master,
    out_momentum,
    up_master,
    up_momentum,
    down_master,
    down_momentum,
    ada_master,
    ada_first,
    ada_second,
    table_master,
    table_first,
    table_second,
    bias_master,
    bias_first,
    bias_second,
):
    low_type = jnp.bfloat16
    full_type = jnp.float32
    clip_count, frames, rows_dev, columns, model_width = tokens.shape
    seq_local = frames * rows_dev * columns
    row_devices = lax.axis_size("row")
    token_total = clip_count * seq_local
    frame_total = clip_count * frames
    shape_five = (clip_count, frames, rows_dev, columns, model_width)
    both = ("frame", "row")
    frame_devices = lax.axis_size("frame")
    device_total = frame_devices * row_devices
    device_index = lax.axis_index("frame") * row_devices + lax.axis_index("row")
    heights = (qkv_master.shape[1], out_master.shape[0], up_master.shape[1], down_master.shape[0])
    w_qkv = lax.all_gather(qkv_master.T.astype(low_type), both, axis=0, tiled=True)
    shards = jnp.concatenate([down_master, up_master.T, out_master], axis=0).astype(low_type)
    gathered = lax.all_gather(shards, both, axis=0)
    if heights[1] % 16 == 0:

        def from_slab(first, height):
            return gathered, pl.BlockSpec(
                (device_total, height, model_width),
                lambda *_: (0, first // height, 0),
                pipeline_mode=pl.Buffered(1),
            )

    else:

        def from_slab(first, height):
            part = gathered[:, first : first + height].reshape(-1, model_width // row_devices, model_width)
            return part, whole_spec(part)

    w_down = from_slab(0, heights[3])
    w_up = from_slab(heights[3], heights[2])
    w_out = from_slab(heights[3] + heights[2], heights[1])
    level_flat = noise_levels.reshape(frame_total)
    levels_all = lax.all_gather(level_flat, "frame", axis=0, tiled=True)
    frames_all = frame_devices * frame_total
    frames_each = frames_all // device_total
    level_rows = table_master.shape[0]
    my_levels = device_index * level_rows + jnp.arange(level_rows, dtype=jnp.int32)
    level_hot = levels_all[:, None] == my_levels[None, :]
    found = jnp.dot(
        level_hot.astype(low_type),
        lax.optimization_barrier(table_master.astype(low_type)),
        preferred_element_type=full_type,
    )

    def to_all(value):
        return lax.all_to_all(value, both, split_axis=0, concat_axis=0, tiled=True)

    def from_all(value):
        return to_all(jnp.broadcast_to(value[None], (device_total,) + value.shape))

    embedded_mine = jnp.sum(
        to_all(found.reshape(device_total, frames_each, model_width)), axis=0
    )
    embedded_all = from_all(embedded_mine).reshape(frames_all, model_width)
    cond_all = jax.nn.silu(embedded_all).astype(low_type)
    ada_low = lax.optimization_barrier(ada_master.astype(low_type))
    bias_low = lax.optimization_barrier(bias_master.astype(low_type))
    ada_width = ada_master.shape[1]
    mod_columns = jnp.dot(cond_all, ada_low, preferred_element_type=full_type) + bias_low.astype(full_type)
    mod_columns = mod_columns.reshape(frame_devices, 1, frame_total, ada_width)
    mod_columns = jnp.broadcast_to(
        mod_columns, (frame_devices, row_devices, frame_total, ada_width)
    ).reshape(device_total, frame_total, ada_width)
    modulation = jnp.moveaxis(to_all(mod_columns), 0, 1).reshape(frame_total, 6 * model_width)
    grid_shape = (clip_count, frames, rows_dev, columns)
    row_first = lax.axis_index("row") * rows_dev
    time_grid = jnp.broadcast_to(frame_times.astype(full_type)[:, :, None, None], grid_shape)
    row_grid = jnp.broadcast_to(
        (row_first + jnp.arange(rows_dev, dtype=jnp.int32)).astype(full_type)[None, None, :, None],
        grid_shape,
    )
    column_grid = jnp.broadcast_to(
        jnp.arange(columns, dtype=jnp.int32).astype(full_type)[None, None, None, :], grid_shape
    )
    angles = rotary_angles(time_grid, row_grid, column_grid).reshape(clip_count, seq_local, HD // 2)
    flat_angles = angles.reshape(token_total, HD // 2)
    pair_sign = jnp.tile(jnp.array([-1.0, 1.0], full_type), HD)
    cosine = jnp.tile(jnp.repeat(jnp.cos(flat_angles), 2, axis=1), (1, 2))
    sine = jnp.tile(jnp.repeat(jnp.sin(flat_angles), 2, axis=1), (1, 2)) * pair_sign
    tile_count = token_total // 256
    mod = modulation.reshape(tile_count, frame_total // tile_count, 6 * model_width)
    me = lax.axis_index("row").astype(jnp.int32).reshape(1)
    tokens_flat = tokens.reshape(clip_count, seq_local, model_width)
    cotangent_flat = cotangent.reshape(clip_count, seq_local, model_width)
    clips = range(clip_count)
    pair_count = D // 128 // row_devices
    units = [(clip, pair) for clip in clips for pair in range(pair_count)]

    def of_unit(slots, pair):
        return slots[pair * row_devices : (pair + 1) * row_devices]

    def after(value, state):
        return [held(value[0], *state), *value[1:]]

    def of_clip(by_unit, clip):
        return [item for pair in range(pair_count) for item in by_unit[clip, pair]]

    hidden_one, pieces = [], {}
    for clip in clips:
        hidden, *slots = project(me, clip, tokens_flat, mod, cosine, sine, w_qkv, row_devices)
        hidden_one.append(hidden[0])
        for pair in range(pair_count):
            pieces[clip, pair] = swap(of_unit(slots, pair))
    attended, full, logs = {}, {}, {}
    for at, unit in enumerate(units):
        ready = list(attended[units[at - 2]][1:]) if at >= 2 else []
        if at >= 1:
            ready.append(slots[0])
        slots, full[unit], logs[unit] = attend(after(pieces[unit], ready))
        attended[unit] = swap(slots)
    moments_tall = [
        item.astype(low_type) for item in (qkv_momentum.T, out_momentum, up_momentum.T, down_momentum)
    ]
    moments_tall[0] = held(moments_tall[0], attended[units[pair_count - 1]][-1])
    moment_steps = plane_steps(moments_tall)
    moment_rows = next(moment_steps)
    d_attended, middles = {}, []
    for clip in clips:
        slots, others = middle(
            me, clip, tokens_flat, cotangent_flat, mod, w_out, w_up, w_down,
            after(of_clip(attended, clip), moment_rows), row_devices,
        )
        for pair in range(pair_count):
            d_attended[clip, pair] = swap(of_unit(slots, pair))
        middles.append(others)
        moment_rows = moment_steps.send([others[0]])
    block_out = jnp.concatenate([item[0] for item in middles], axis=0).reshape(shape_five)
    att_low, hidden_two, activated, d_branch_two, d_up, d_branch_one, d_middle, two_sums = (
        [item[index] for item in middles] for index in range(1, 9)
    )
    early = scatter_steps(
        [[(activated, d_branch_two)], [(d_up, hidden_two), (att_low, d_branch_one)]], "early", True, moment_rows
    )
    state = next(early)
    d_pieces = {}
    while not isinstance(moment_rows, tuple):
        moment_rows = moment_steps.send(list(state))
    for at, unit in enumerate(units):
        ready = list(d_pieces[units[at - 2]][1:]) if at >= 2 else list(state)
        if at >= 1:
            ready.append(slots[0])
        if at == 1:
            ready += moment_rows
        slots = attend_back(pieces[unit], after(d_attended[unit], ready), full[unit], logs[unit])
        d_pieces[unit] = swap(slots)
    state = early.send([slots[0]])
    lasts = []
    for clip in clips:
        lasts.append(
            last(
                me, clip, tokens_flat, mod, cosine, sine, w_qkv, d_middle[clip],
                after(of_clip(d_pieces, clip), state), row_devices,
            )
        )
        state = early.send([lasts[clip][2]])
    input_grad = jnp.concatenate([item[1] for item in lasts], axis=0).reshape(shape_five)
    late = scatter_steps([[([item[0] for item in lasts], hidden_one)]], "late", False, [])
    late_state = next(late)
    early_sum = finished(early, state)
    state = late_state
    one_sums = [item[2] for item in lasts]
    one_sums[0] = held(one_sums[0], *state)
    d_modulation = frame_sums(one_sums, two_sums)
    g_qkv = finished(late, state)

    mod_parts = to_all(jnp.moveaxis(d_modulation.reshape(frame_total, device_total, ada_width), 1, 0))
    mod_mine = (
        jnp.sum(mod_parts.reshape(frame_devices, row_devices, frame_total, ada_width), axis=1)
        .reshape(frames_all, ada_width)
        .astype(low_type)
    )
    g_ada = jnp.einsum("fd,fe->de", cond_all, mod_mine, preferred_element_type=full_type)
    g_bias = jnp.sum(mod_mine.astype(full_type), axis=0)
    d_cond_parts = jnp.einsum("fe,de->fd", mod_mine, ada_low, preferred_element_type=full_type)
    d_cond = jnp.sum(to_all(d_cond_parts.reshape(device_total, frames_each, model_width)), axis=0)
    d_embedded_mine = jax.vjp(jax.nn.silu, embedded_mine)[1](d_cond)[0]
    d_embedded = from_all(d_embedded_mine).reshape(frames_all, model_width)
    g_table = jnp.dot(level_hot.astype(full_type).T, d_embedded, precision=highest)
    g_down = early_sum[: heights[3]]
    g_up = early_sum[heights[3] : heights[3] + heights[2]]
    g_out = early_sum[heights[3] + heights[2] :]
    muon_grads = (g_qkv, g_out, g_up, g_down)
    flipped = (True, False, True, False)

    def tall(value, member):
        return value.T if flipped[member] else value

    muon_moments = (qkv_momentum, out_momentum, up_momentum, down_momentum)
    muon_masters = (qkv_master, out_master, up_master, down_master)
    factors = (math.sqrt(3.0), 1.0, math.sqrt(FF / D), math.sqrt(FF / D))
    adam_local = jnp.sum(g_ada * g_ada) + jnp.sum(g_table * g_table) + jnp.sum(g_bias * g_bias)
    local_total = adam_local + sum((jnp.sum(item * item) for item in muon_grads))
    norm_value = jnp.sqrt(jnp.sum(from_all(jnp.full((1, 128), local_total))[:, 0, 0]))
    clip_factor = jnp.minimum(1.0, clip_limit / (norm_value + 1e-06))
    grad_steps = plane_steps([item.astype(low_type) for item in muon_grads])
    grad_rows = next(grad_steps)
    while not isinstance(grad_rows, tuple):
        grad_rows = grad_steps.send([])
    moments_new = []
    for member in range(4):
        clipped = clip_factor * muon_grads[member]
        moments_new.append(
            tall(momentum_decay * tall(muon_moments[member], member) + clipped, member)
        )
    scales = jnp.stack(
        [clip_factor * (1.0 + momentum_decay), jnp.full((), momentum_decay * momentum_decay, full_type)]
    )
    slot_rows = max(heights)
    groups = frame_devices // 2
    ortho_rows = newton(scales, grad_rows, moment_rows, groups * slot_rows)
    ortho_rows = ortho_rows.reshape(groups, slot_rows, model_width)
    ortho_slots = jnp.stack(frame_swap([ortho_rows[slot] for slot in range(groups)]))
    group_index = lax.axis_index("frame") >> 1
    ortho_mine = [
        lax.dynamic_index_in_dim(ortho_slots, (group_index & 3) ^ member, 0, keepdims=False)
        for member in range(4)
    ]
    blocks = [tall(ortho_mine[member][: heights[member]].astype(full_type), member) for member in range(4)]
    masters_new = []
    for member in range(4):
        ortho = blocks[member]
        masters_new.append(
            muon_masters[member] * (1.0 - muon_rate * weight_decay)
            - muon_rate * factors[member] * ortho
        )
    step_value = step_count.astype(full_type)[0]
    ada_first_new, ada_second_new, ada_master_new = adam_update(
        g_ada, ada_first, ada_second, ada_master, 0.03, clip_factor, step_value
    )
    table_clipped = clip_factor * g_table
    table_first_new, table_second_new, table_master_new = adam_update(
        g_table, table_first, table_second, table_master, 0.5, clip_factor, step_value
    )
    bias_first_new, bias_second_new, bias_master_new = adam_update(
        g_bias, bias_first, bias_second, bias_master, 0.5, clip_factor, step_value
    )
    return (
        block_out,
        input_grad,
        norm_value.reshape(1),
        moments_new[0],
        masters_new[0],
        moments_new[1],
        masters_new[1],
        moments_new[2],
        masters_new[2],
        moments_new[3],
        masters_new[3],
        ada_first_new,
        ada_second_new,
        ada_master_new,
        table_first_new,
        table_clipped,
        table_master_new,
        bias_first_new,
        bias_second_new,
        bias_master_new,
    )


def solution(mesh):
    return jax.shard_map(
        per_device,
        mesh=mesh,
        in_specs=(
            P("frame", None, "row", None, None),
            P("frame", None, "row", None, None),
            P("frame", None),
            P("frame", None),
            P(),
            P(None, ("frame", "row")),
            P(None, ("frame", "row")),
            P(("frame", "row"), None),
            P(("frame", "row"), None),
            P(None, ("frame", "row")),
            P(None, ("frame", "row")),
            P(("frame", "row"), None),
            P(("frame", "row"), None),
            P(None, ("frame", "row")),
            P(None, ("frame", "row")),
            P(None, ("frame", "row")),
            P(("frame", "row"), None),
            P(("frame", "row"), None),
            P(("frame", "row"), None),
            P(("frame", "row")),
            P(("frame", "row")),
            P(("frame", "row")),
        ),
        out_specs=(
            P("frame", None, "row", None, None),
            P("frame", None, "row", None, None),
            P(),
            P(None, ("frame", "row")),
            P(None, ("frame", "row")),
            P(("frame", "row"), None),
            P(("frame", "row"), None),
            P(None, ("frame", "row")),
            P(None, ("frame", "row")),
            P(("frame", "row"), None),
            P(("frame", "row"), None),
            P(None, ("frame", "row")),
            P(None, ("frame", "row")),
            P(None, ("frame", "row")),
            P(("frame", "row"), None),
            P(("frame", "row"), None),
            P(("frame", "row"), None),
            P(("frame", "row")),
            P(("frame", "row")),
            P(("frame", "row")),
        ),
        check_vma=False,
    )
```

```python
import functools
import math

import jax
import jax.numpy as jnp
from jax import lax
from jax.experimental import pallas as pl
from jax.experimental.pallas import tpu as pltpu
from jax.sharding import PartitionSpec as P

D = 1024
HEADS = 16
HD = 64
FF = 4096


highest = lax.Precision.HIGHEST
newton_one = 3.4445
newton_two = -4.775
newton_three = 2.0315
momentum_decay = 0.95
muon_rate = 1.5
weight_decay = 0.01
beta_first = 0.9
beta_second = 0.95
adam_floor = 1e-08
norm_floor = 1e-06
clip_limit = 1.0
rotary_base = 10000.0


def rotary_angles(time_grid, row_grid, column_grid):
    quarter_pairs = HD // 4
    eighth_pairs = HD // 8
    time_rates = rotary_base ** (-jnp.arange(quarter_pairs, dtype=jnp.float32) / quarter_pairs)
    space_rates = rotary_base ** (-jnp.arange(eighth_pairs, dtype=jnp.float32) / eighth_pairs)
    return jnp.concatenate(
        [
            time_grid[..., None] * time_rates,
            row_grid[..., None] * space_rates,
            column_grid[..., None] * space_rates,
        ],
        axis=-1,
    )


def adam_update(grad_item, first, second, master, rate, clip_factor, step_value):
    clipped = clip_factor * grad_item
    first_new = beta_first * first + (1.0 - beta_first) * clipped
    second_new = beta_second * second + (1.0 - beta_second) * clipped * clipped
    first_fix = 1.0 - beta_first**step_value
    second_fix = 1.0 - beta_second**step_value
    master_new = master * (1.0 - rate * weight_decay) - rate * (first_new / first_fix) / (
        jnp.sqrt(second_new / second_fix) + adam_floor
    )
    return (first_new, second_new, master_new)


def halves(value, dim, axis, bit):
    mine = (lax.axis_index(axis) >> bit) & 1
    keep = lax.dynamic_index_in_dim(value, mine, dim, keepdims=False)
    send = lax.dynamic_index_in_dim(value, 1 - mine, dim, keepdims=False)
    return keep, send.astype(jnp.bfloat16)


def joined(keep, send, axis, bit):
    size = lax.axis_size(axis)
    came = lax.ppermute(send, axis, [(index, index ^ (1 << bit)) for index in range(size)])
    return keep + came.astype(jnp.float32)


def held(value, *others):
    if not others:
        return value
    return lax.optimization_barrier((value, *others))[0]


def scatter_steps(groups, name, by_frame, ready):
    frame_bits = lax.axis_size("frame").bit_length() - 1
    row_bits = lax.axis_size("row").bit_length() - 1
    row, frame = lax.axis_index("row"), lax.axis_index("frame")
    numbers = jnp.stack([frame & 1, row & 1, row >> (row_bits - 1), (frame >> 1) & 1]).astype(jnp.int32)
    numbers = held(numbers, *ready)
    size = lax.axis_size("frame")
    came = []
    for at, group in enumerate(groups):
        send = send_sums(numbers, group, f"{name}_send_{at}")
        came.append(lax.ppermute(send, "frame", [(index, index ^ 1) for index in range(size)]))
        numbers = held(numbers, send)
    keep, send = keep_sums(numbers, groups, came, name + "_keep", by_frame)
    hold = yield send
    names = [("frame", bit) for bit in reversed(range(1, frame_bits))]
    names += [("row", bit) for bit in reversed(range(row_bits))]
    rest = [("frame", bit) for bit in range(1, frame_bits)]
    side_names = []
    if by_frame:
        names.remove(("frame", 1))
        rest.remove(("frame", 1))
        value = joined(held(keep[0], *hold), send[0], "frame", 1)
        value = value.reshape((2,) * len(names) + value.shape[2:])
        width = value.shape[-1] // 2
        keep, send = [], []
        for side in range(2):
            bit = 0 if side == 0 else row_bits - 1
            side_names.append([item for item in names if item != ("row", bit)])
            part = value[..., side * width : (side + 1) * width]
            kept, sent = halves(part, names.index(("row", bit)), "row", bit)
            keep.append(kept)
            send.append(sent)
        hold = yield send
    else:
        for side in range(2):
            bit = 0 if side == 0 else row_bits - 1
            side_names.append([item for item in names if item != ("row", bit)])
            shape = (2,) * (len(names) - 1) + keep[side].shape[2:]
            keep[side] = keep[side].reshape(shape)
            send[side] = send[side].reshape(shape)
    for step in range(row_bits):
        parts = []
        for side in range(2):
            bit = step if side == 0 else row_bits - 1 - step
            parts.append(joined(held(keep[side], *hold), send[side], "row", bit))
        if step == row_bits - 1:
            break
        for side in range(2):
            bit = step + 1 if side == 0 else row_bits - 2 - step
            dim = side_names[side].index(("row", bit))
            side_names[side].pop(dim)
            keep[side], send[side] = halves(parts[side], dim, "row", bit)
        hold = yield send
    value = jnp.concatenate(parts, axis=-1)
    value = value.reshape((-1,) + value.shape[-2:])
    count = value.shape[0]
    low = rest[0][1] if rest else 0
    mine = frame >> low
    keep = lax.dynamic_index_in_dim(value, mine & (count - 1), 0, keepdims=False)
    sends = [
        lax.dynamic_index_in_dim(value, (mine ^ slot) & (count - 1), 0, keepdims=False).astype(jnp.bfloat16)
        for slot in range(1, count)
    ]
    hold = yield sends
    keep = held(keep, *hold)
    for slot, send in enumerate(sends, 1):
        pairs = [(index, index ^ (slot << low)) for index in range(size)]
        keep = keep + lax.ppermute(send, "frame", pairs).astype(jnp.float32)
    yield keep


def finished(steps, state):
    while isinstance(state, list):
        state = steps.send([])
    return state


def split_two(value):
    high = value.astype(jnp.bfloat16)
    return high, (value - high.astype(jnp.float32)).astype(jnp.bfloat16)


def dot_low(left, right):
    return lax.dot_general(left, right, (((1,), (0,)), ((), ())), preferred_element_type=jnp.float32)


def dot_nt(left, right):
    return lax.dot_general(left, right, (((1,), (1,)), ((), ())), preferred_element_type=jnp.float32)


def dot_tn(left, right):
    return lax.dot_general(left, right, (((0,), (0,)), ((), ())), preferred_element_type=jnp.float32)


MIB = 1024 * 1024


def vmem_params(mib, semantics=None):
    return pltpu.CompilerParams(vmem_limit_bytes=mib * MIB, dimension_semantics=semantics)


def whole_spec(array):
    zeros = (0,) * array.ndim
    return pl.BlockSpec(array.shape, lambda *_: zeros, pipeline_mode=pl.Buffered(1))


def turned(value, cosine, sine):
    even = lax.broadcasted_iota(jnp.int32, value.shape, 1) % 2 == 0
    width = value.shape[1]
    swapped = jnp.where(even, pltpu.roll(value, width - 1, 1), pltpu.roll(value, 1, 1))
    return value * cosine + swapped * sine


def framed(value, frames):
    rows, width = value.shape
    return value.reshape(frames, rows // frames, width)


def norm_parts(value):
    mean = jnp.mean(value, axis=-1, keepdims=True)
    centered = value - mean
    root = lax.rsqrt(jnp.mean(centered * centered, axis=-1, keepdims=True) + norm_floor)
    return centered * root, root


def project_kernel(slots, me_ref, x_ref, mod_ref, cos_ref, sin_ref, w_ref, hid_ref, *out_refs):
    frames = mod_ref.shape[1]
    group = D // slots
    normed, _ = norm_parts(x_ref[0].astype(jnp.float32))
    normed = framed(normed, frames)
    shift = mod_ref[0, :, 0:D][:, None, :]
    scaling = mod_ref[0, :, D : 2 * D][:, None, :]
    hidden = (normed * (1.0 + scaling) + shift).reshape(x_ref.shape[1], D).astype(jnp.bfloat16)
    hid_ref[0] = hidden
    cosine = cos_ref[...]
    sine = sin_ref[...]
    me = me_ref[0]
    for slot in range(slots):
        peer = me ^ slot
        for part in range(3):
            rows = pl.ds(pl.multiple_of(part * D + peer * group, group), group)
            value = dot_nt(hidden, w_ref[rows, :])
            if part == 2:
                out_refs[slot][part] = value.astype(jnp.bfloat16)
                continue
            for first in range(0, group, 128):
                piece = turned(value[:, first : first + 128], cosine, sine)
                if part == 0:
                    piece = piece * (1.0 / math.sqrt(HD))
                out_refs[slot][part, :, first : first + 128] = piece.astype(jnp.bfloat16)


def project(me, clip, tokens, mod, cosine, sine, w_qkv, slots):
    count, tall_rows, _ = tokens.shape
    tile = 256
    steps = tall_rows // tile
    group = D // slots
    out_shape = [jax.ShapeDtypeStruct((1, tall_rows, D), jnp.bfloat16)]
    out_shape += [jax.ShapeDtypeStruct((3, tall_rows, group), jnp.bfloat16)] * slots
    return pl.pallas_call(
        functools.partial(project_kernel, slots),
        grid=(steps,),
        in_specs=[
            pl.BlockSpec(memory_space=pltpu.SMEM),
            pl.BlockSpec((1, tile, D), lambda i: (clip, i, 0)),
            pl.BlockSpec((1, mod.shape[1], 6 * D), lambda i: (clip * steps + i, 0, 0)),
            pl.BlockSpec((tile, 128), lambda i: (clip * steps + i, 0)),
            pl.BlockSpec((tile, 128), lambda i: (clip * steps + i, 0)),
            whole_spec(w_qkv),
        ],
        out_specs=[pl.BlockSpec((1, tile, D), lambda i: (0, i, 0))]
        + [pl.BlockSpec((3, tile, group), lambda i: (0, i, 0))] * slots,
        out_shape=out_shape,
        compiler_params=vmem_params(60),
        cost_estimate=pl.CostEstimate(
            flops=6 * tall_rows * D * D, bytes_accessed=10 * MIB, transcendentals=0
        ),
        name="project",
    )(me, tokens, mod, cosine, sine, w_qkv)


def head_mask(shape, head, axis):
    return lax.broadcasted_iota(jnp.int32, shape, axis) // HD == head


def attend_kernel(slots, tile, *refs):
    ins, outs = refs[:slots], refs[slots : 2 * slots]
    full_ref, log_ref, qs, ks, vs = refs[2 * slots :]
    length = ins[0].shape[1]
    for slot in range(slots):
        rows = slice(slot * length, (slot + 1) * length)
        qs[rows, :] = ins[slot][0]
        ks[rows, :] = ins[slot][1]
        vs[rows, :] = ins[slot][2]

    def one(index, carry):
        rows = pl.ds(pl.multiple_of(index * tile, tile), tile)
        query = qs[rows, :]
        first = head_mask((tile, 128), 0, 1)
        parts = []
        logs = []
        for head in range(2):
            masked = jnp.where(first if head == 0 else ~first, query, jnp.zeros_like(query))
            scores = dot_nt(masked, ks[...])
            top = jnp.max(scores, axis=-1, keepdims=True)
            raised = jnp.exp(scores - top)
            total = jnp.sum(raised, axis=-1, keepdims=True)
            parts.append(dot_low(raised.astype(jnp.bfloat16), vs[...]) * (1.0 / total))
            logs.append(top + jnp.log(total))
        full_ref[rows, :] = jnp.where(first, parts[0], parts[1])
        log_ref[rows, :] = jnp.where(first, logs[0], logs[1])
        return carry

    lax.fori_loop(0, slots * length // tile, one, 0)
    for slot in range(slots):
        rows = slice(slot * length, (slot + 1) * length)
        outs[slot][...] = full_ref[rows, :].astype(jnp.bfloat16)


def attend(pieces):
    slots = len(pieces)
    _, length, group = pieces[0].shape
    total = slots * length
    scratch = pltpu.VMEM((total, 128), jnp.bfloat16)
    outs = pl.pallas_call(
        functools.partial(attend_kernel, slots, 256),
        grid=(group // 128,),
        in_specs=[pl.BlockSpec((3, length, 128), lambda i: (0, 0, i))] * slots,
        out_specs=[pl.BlockSpec((length, 128), lambda i: (0, i))] * slots
        + [pl.BlockSpec((total, 128), lambda i: (0, i))] * 2,
        out_shape=[jax.ShapeDtypeStruct((length, group), jnp.bfloat16)] * slots
        + [jax.ShapeDtypeStruct((total, group), jnp.float32)] * 2,
        scratch_shapes=[scratch] * 3,
        compiler_params=vmem_params(60),
        cost_estimate=pl.CostEstimate(
            flops=16 * total * total * group, bytes_accessed=8 * MIB, transcendentals=total * total * 4
        ),
        name="attend",
    )(*pieces)
    return outs[:slots], outs[slots], outs[slots + 1]


def attend_back_kernel(slots, tile, *refs):
    ins, grads = refs[:slots], refs[slots : 2 * slots]
    full_ref, log_ref = refs[2 * slots : 2 * slots + 2]
    outs = refs[2 * slots + 2 : 3 * slots + 2]
    qs, ks, vs, gs, q_turned, g_turned, dq, dk, dv = refs[3 * slots + 2 :]
    length = ins[0].shape[1]
    total = slots * length
    for slot in range(slots):
        rows = slice(slot * length, (slot + 1) * length)
        qs[rows, :] = ins[slot][0]
        ks[rows, :] = ins[slot][1]
        vs[rows, :] = ins[slot][2]
        gs[rows, :] = grads[slot][...]
        q_turned[:, rows] = ins[slot][0].T
        g_turned[:, rows] = grads[slot][...].T
    dk[...] = jnp.zeros_like(dk)
    dv[...] = jnp.zeros_like(dv)

    def one(index, carry):
        rows = pl.ds(pl.multiple_of(index * tile, tile), tile)
        first = head_mask((tile, 128), 0, 1)
        upper = head_mask((128, tile), 0, 0)
        query, grad = qs[rows, :], gs[rows, :]
        query_t, grad_t = q_turned[:, rows], g_turned[:, rows]
        product = grad.astype(jnp.float32) * full_ref[rows, :]
        masks = (first, ~first)
        masks_t = (upper, ~upper)
        zero = jnp.zeros_like(query)
        zero_t = jnp.zeros_like(query_t)
        q_low = [jnp.where(mask, query, zero) for mask in masks]
        g_low = [jnp.where(mask, grad, zero) for mask in masks]
        qt_low = [jnp.where(mask, query_t, zero_t) for mask in masks_t]
        gt_low = [jnp.where(mask, grad_t, zero_t) for mask in masks_t]
        inner = [jnp.sum(jnp.where(mask, product, 0.0), axis=-1, keepdims=True) for mask in masks]
        logs = [log_ref[rows, 0:1], log_ref[rows, HD : HD + 1]]

        def inside(k_index, sums):
            at = pl.ds(pl.multiple_of(k_index * tile, tile), tile)
            key, value = ks[at, :], vs[at, :]
            out = []
            for head in range(2):
                probs = jnp.exp(dot_nt(q_low[head], key) - logs[head])
                d_probs = dot_nt(g_low[head], value)
                d_scores = (probs * (d_probs - inner[head])).astype(jnp.bfloat16)
                dv[:, at] += dot_low(gt_low[head], probs.astype(jnp.bfloat16))
                dk[:, at] += dot_low(qt_low[head], d_scores)
                out.append(sums[head] + dot_low(d_scores, key))
            return tuple(out)

        start = jnp.zeros((tile, 128), jnp.float32)
        sums = lax.fori_loop(0, total // tile, inside, (start, start))
        dq[rows, :] = (jnp.where(first, sums[0], sums[1]) * (1.0 / math.sqrt(HD))).astype(jnp.bfloat16)
        return carry

    lax.fori_loop(0, total // tile, one, 0)
    for slot in range(slots):
        rows = slice(slot * length, (slot + 1) * length)
        outs[slot][0] = dq[rows, :]
        outs[slot][1] = dk[:, rows].T.astype(jnp.bfloat16)
        outs[slot][2] = dv[:, rows].T.astype(jnp.bfloat16)


def attend_back(pieces, grads, full, logs, pair=None):
    slots = len(pieces)
    _, length, group = pieces[0].shape
    first = 0 if pair is None else pair
    count = group // 128 if pair is None else 1
    group = 128 * count
    total = slots * length
    low = pltpu.VMEM((total, 128), jnp.bfloat16)
    low_t = pltpu.VMEM((128, total), jnp.bfloat16)
    full_t = pltpu.VMEM((128, total), jnp.float32)
    return pl.pallas_call(
        functools.partial(attend_back_kernel, slots, 512),
        grid=(count,),
        in_specs=[pl.BlockSpec((3, length, 128), lambda i: (0, 0, i + first))] * slots
        + [pl.BlockSpec((length, 128), lambda i: (0, i + first))] * slots
        + [pl.BlockSpec((total, 128), lambda i: (0, i + first))] * 2,
        out_specs=[pl.BlockSpec((3, length, 128), lambda i: (0, 0, i))] * slots,
        out_shape=[jax.ShapeDtypeStruct((3, length, group), jnp.bfloat16)] * slots,
        scratch_shapes=[low] * 4 + [low_t] * 2 + [low] + [full_t] * 2,
        compiler_params=vmem_params(60),
        cost_estimate=pl.CostEstimate(
            flops=40 * total * total * group, bytes_accessed=12 * MIB, transcendentals=total * total * 4
        ),
        name="attend_back",
    )(*pieces, *grads, full, logs)


def part_of(ref, index, size):
    count = size // ref.shape[1]
    return ref[pl.ds(index * count, count)].reshape(size, ref.shape[2])


def middle_kernel(slots, me_ref, x_ref, cot_ref, mod_ref, wo_ref, wu_ref, wd_ref, *refs):
    att_refs = refs[:slots]
    datt_refs = refs[slots : 2 * slots]
    (
        out_ref,
        att_ref,
        h2_ref,
        act_ref,
        db2_ref,
        dup_ref,
        db1_ref,
        dmid_ref,
        sums_ref,
        slope,
    ) = refs[2 * slots :]
    frames = mod_ref.shape[1]
    rows = x_ref.shape[1]
    group = D // slots
    me = me_ref[0]

    def mod(index):
        return mod_ref[0, :, index * D : (index + 1) * D][:, None, :]

    def spread(value, index, plus=0.0):
        return (framed(value, frames) * (mod(index) + plus)).reshape(rows, D)

    def frame_sum(value):
        return jnp.sum(framed(value, frames), axis=1)

    branch = jnp.zeros((rows, D), jnp.float32)
    for slot in range(slots):
        at = pl.ds(pl.multiple_of((me ^ slot) * group, group), group)
        piece = att_refs[slot][...]
        att_ref[:, at] = piece
        branch += dot_low(piece, part_of(wo_ref, me ^ slot, group))
    middle = x_ref[0].astype(jnp.float32) + spread(branch, 2)
    normed, root = norm_parts(middle)
    hidden = (framed(spread(normed, 4, 1.0), frames) + mod(3)).reshape(rows, D).astype(jnp.bfloat16)
    h2_ref[...] = hidden
    wide = 1024
    curve = math.sqrt(2.0 / math.pi)
    branch_two = jnp.zeros((rows, D), jnp.float32)
    for first in range(0, FF, wide):
        cut = slice(first, first + wide)
        up = dot_nt(hidden, part_of(wu_ref, first // wide, wide))
        square = up * up
        bent = jnp.tanh(curve * up * (1.0 + 0.044715 * square))
        half = 0.5 * (1.0 + bent)
        active = (up * half).astype(jnp.bfloat16)
        slope[:, cut] = half + 0.5 * up * (1.0 - bent * bent) * (curve * (1.0 + 3 * 0.044715 * square))
        act_ref[:, cut] = active
        branch_two += dot_low(active, part_of(wd_ref, first // wide, wide))
    cot = cot_ref[0].astype(jnp.float32)
    out_ref[0] = (middle + spread(branch_two, 5)).astype(jnp.bfloat16)
    sums_ref[0, 3] = frame_sum(cot * branch_two)
    d_branch_two = spread(cot, 5).astype(jnp.bfloat16)
    db2_ref[...] = d_branch_two
    d_hidden = jnp.zeros((rows, D), jnp.float32)
    for first in range(0, FF, wide):
        cut = slice(first, first + wide)
        d_up = (dot_nt(d_branch_two, part_of(wd_ref, first // wide, wide)) * slope[:, cut]).astype(jnp.bfloat16)
        dup_ref[:, cut] = d_up
        d_hidden += dot_low(d_up, part_of(wu_ref, first // wide, wide))
    sums_ref[0, 1] = frame_sum(d_hidden)
    sums_ref[0, 2] = frame_sum(d_hidden * normed)
    inner = spread(d_hidden, 4, 1.0)
    d_middle = cot + root * (
        inner
        - jnp.mean(inner, axis=-1, keepdims=True)
        - normed * jnp.mean(inner * normed, axis=-1, keepdims=True)
    )
    dmid_ref[...] = d_middle
    sums_ref[0, 0] = frame_sum(d_middle * branch)
    d_branch = spread(d_middle, 2).astype(jnp.bfloat16)
    db1_ref[...] = d_branch
    for slot in range(slots):
        datt_refs[slot][...] = dot_nt(d_branch, part_of(wo_ref, me ^ slot, group)).astype(jnp.bfloat16)


def middle(me, clip, tokens, cotangent, mod, w_out, w_up, w_down, attended):
    slots = len(attended)
    count, length, _ = tokens.shape
    tile = 256
    steps = length // tile
    group = D // slots
    frames = mod.shape[1]
    low = jnp.bfloat16

    def flat(width, kind=low):
        return jax.ShapeDtypeStruct((length, width), kind)

    def flat_spec(width):
        return pl.BlockSpec((tile, width), lambda i: (i, 0))

    outs = pl.pallas_call(
        functools.partial(middle_kernel, slots),
        grid=(steps,),
        in_specs=[
            pl.BlockSpec(memory_space=pltpu.SMEM),
            pl.BlockSpec((1, tile, D), lambda i: (clip, i, 0)),
            pl.BlockSpec((1, tile, D), lambda i: (clip, i, 0)),
            pl.BlockSpec((1, frames, 6 * D), lambda i: (clip * steps + i, 0, 0)),
            *(item[1] for item in (w_out, w_up, w_down)),
        ]
        + [flat_spec(group)] * slots,
        out_specs=[flat_spec(group)] * slots
        + [pl.BlockSpec((1, tile, D), lambda i: (0, i, 0))]
        + [flat_spec(width) for width in (D, D, FF, D, FF, D, D)]
        + [pl.BlockSpec((1, 4, frames, D), lambda i: (i, 0, 0, 0))],
        out_shape=[flat(group)] * slots
        + [jax.ShapeDtypeStruct((1, length, D), low)]
        + [flat(D), flat(D), flat(FF), flat(D), flat(FF), flat(D), flat(D, jnp.float32)]
        + [jax.ShapeDtypeStruct((steps, 4, frames, D), jnp.float32)],
        scratch_shapes=[pltpu.VMEM((tile, FF), jnp.float32)],
        compiler_params=vmem_params(60),
        cost_estimate=pl.CostEstimate(
            flops=2 * length * D * (2 * D + 4 * FF), bytes_accessed=40 * MIB, transcendentals=length * FF
        ),
        name="middle",
    )(me, tokens, cotangent, mod, *(item[0] for item in (w_out, w_up, w_down)), *attended)
    return outs[:slots], outs[slots:]


def last_kernel(slots, me_ref, x_ref, mod_ref, cos_ref, sin_ref, w_ref, dmid_ref, *refs):
    pieces = refs[:-3]
    dproj_ref, grad_ref, sums_ref = refs[-3:]
    frames = mod_ref.shape[1]
    rows = x_ref.shape[1]
    group = D // slots
    pairs = len(pieces) // slots
    narrow = group // pairs
    me = me_ref[0]
    cosine = cos_ref[...]
    sine = -sin_ref[...]
    d_hidden = jnp.zeros((rows, D), jnp.float32)
    for slot in range(slots):
        peer = me ^ slot
        for part in range(3):
            base = pl.multiple_of(part * D + peer * group, group)
            if part == 2:
                value = jnp.concatenate([pieces[pair * slots + slot][part] for pair in range(pairs)], axis=1)
            else:
                value = jnp.concatenate(
                    [
                        turned(
                            pieces[at // narrow * slots + slot][
                                part, :, at % narrow : at % narrow + 128
                            ].astype(jnp.float32),
                            cosine,
                            sine,
                        )
                        for at in range(0, group, 128)
                    ],
                    axis=1,
                ).astype(jnp.bfloat16)
            dproj_ref[:, pl.ds(base, group)] = value
            d_hidden += dot_low(value, w_ref[pl.ds(base, group), :])
    normed, root = norm_parts(x_ref[0].astype(jnp.float32))
    scaling = mod_ref[0, :, D : 2 * D][:, None, :]
    sums_ref[0, 0] = jnp.sum(framed(d_hidden, frames), axis=1)
    sums_ref[0, 1] = jnp.sum(framed(d_hidden * normed, frames), axis=1)
    inner = (framed(d_hidden, frames) * (1.0 + scaling)).reshape(rows, D)
    grad_ref[0] = dmid_ref[...] + root * (
        inner
        - jnp.mean(inner, axis=-1, keepdims=True)
        - normed * jnp.mean(inner * normed, axis=-1, keepdims=True)
    )


def last(me, clip, tokens, mod, cosine, sine, w_qkv, d_middle, pieces, slots):
    count, length, _ = tokens.shape
    tile = 256
    steps = length // tile
    narrow = pieces[0].shape[2]
    frames = mod.shape[1]
    return pl.pallas_call(
        functools.partial(last_kernel, slots),
        grid=(steps,),
        in_specs=[
            pl.BlockSpec(memory_space=pltpu.SMEM),
            pl.BlockSpec((1, tile, D), lambda i: (clip, i, 0)),
            pl.BlockSpec((1, frames, 6 * D), lambda i: (clip * steps + i, 0, 0)),
            pl.BlockSpec((tile, 128), lambda i: (clip * steps + i, 0)),
            pl.BlockSpec((tile, 128), lambda i: (clip * steps + i, 0)),
            whole_spec(w_qkv),
            pl.BlockSpec((tile, D), lambda i: (i, 0)),
        ]
        + [pl.BlockSpec((3, tile, narrow), lambda i: (0, i, 0))] * len(pieces),
        out_specs=[
            pl.BlockSpec((tile, 3 * D), lambda i: (i, 0)),
            pl.BlockSpec((1, tile, D), lambda i: (0, i, 0)),
            pl.BlockSpec((1, 2, frames, D), lambda i: (i, 0, 0, 0)),
        ],
        out_shape=[
            jax.ShapeDtypeStruct((length, 3 * D), jnp.bfloat16),
            jax.ShapeDtypeStruct((1, length, D), jnp.float32),
            jax.ShapeDtypeStruct((steps, 2, frames, D), jnp.float32),
        ],
        compiler_params=vmem_params(60),
        cost_estimate=pl.CostEstimate(
            flops=6 * length * D * D, bytes_accessed=20 * MIB, transcendentals=0
        ),
        name="last",
    )(me, tokens, mod, cosine, sine, w_qkv, d_middle, *pieces)


def member_value(refs, member, doubled, parity):
    left = refs[4 * member : 4 * member + 2]
    right = refs[4 * member + 2 : 4 * member + 4]
    value = dot_tn(left[0][...], right[0][...]) + dot_tn(left[1][...], right[1][...])
    if doubled:
        half = value.shape[0] // 2
        value = jnp.where(parity == 0, value[:half], value[half:])
    return value


def send_kernel(doubled, number_ref, *refs):
    out_ref = refs[-1]
    rows = out_ref.shape[1]
    first = 0
    for member in range(len(doubled)):
        value = member_value(refs, member, doubled[member], 1 - number_ref[0])
        height = value.shape[0] // rows
        out_ref[0, :, first : first + height, :] = value.reshape(rows, height, D).astype(out_ref.dtype)
        first += height


def keep_kernel(doubled, counts, number_ref, *refs):
    members = len(doubled)
    came_refs = refs[4 * members : 4 * members + len(counts)]
    keep_refs, send_refs = refs[-4:-2], refs[-2:]
    half_rows = keep_refs[0].shape[1]
    width = D // 2
    first = 0
    member = 0
    for came_ref, count in zip(came_refs, counts):
        inside = 0
        for _ in range(count):
            value = member_value(refs, member, doubled[member], number_ref[0])
            height = value.shape[0] // (2 * half_rows)
            rows = slice(first, first + height)
            parts = [
                value[row * height : (row + 1) * height]
                + came_ref[0, row, inside : inside + height, :].astype(jnp.float32)
                for row in range(2 * half_rows)
            ]
            for place in range(half_rows):
                for side in range(2):
                    cut = slice(side * width, (side + 1) * width)
                    low = 2 * place if side == 0 else place
                    high = low + (1 if side == 0 else half_rows)
                    upper = number_ref[1 + side] == 1
                    zero, one = parts[low][:, cut], parts[high][:, cut]
                    keep_refs[side][0, place, rows, :] = jnp.where(upper, one, zero)
                    send_refs[side][0, place, rows, :] = jnp.where(upper, zero, one).astype(jnp.bfloat16)
            first += height
            inside += height
            member += 1


def keep_frame_kernel(doubled, counts, number_ref, *refs):
    members = len(doubled)
    came_refs = refs[4 * members : 4 * members + len(counts)]
    keep_ref, send_ref = refs[-2:]
    rows = keep_ref.shape[1]
    kept = lax.rem(pl.program_id(0), 2) == number_ref[3]
    first = 0
    member = 0
    for came_ref, count in zip(came_refs, counts):
        inside = 0
        for _ in range(count):
            value = member_value(refs, member, doubled[member], number_ref[0])
            height = value.shape[0] // rows
            value = value.reshape(rows, height, D)
            value += came_ref[0, :, inside : inside + height, :].astype(jnp.float32)
            at = slice(first, first + height)

            @pl.when(kept)
            def _(value=value, at=at):
                keep_ref[0, :, at, :] = value

            @pl.when(jnp.logical_not(kept))
            def _(value=value, at=at):
                send_ref[0, :, at, :] = value.astype(jnp.bfloat16)

            first += height
            inside += height
            member += 1


def weight_specs(pairs, other):
    frame_devices = lax.axis_size("frame")
    specs, operands, doubled = [], [], []
    height = 0
    for left, right in pairs:
        width = left[0].shape[1] // frame_devices
        height += width // lax.axis_size("row")
        doubled.append(width % 128 != 0)
        if doubled[-1]:
            spec = pl.BlockSpec((left[0].shape[0], 2 * width), lambda i, s: (0, i))
        elif other:
            spec = pl.BlockSpec((left[0].shape[0], width), lambda i, s: (0, 2 * i + 1 - s[0]))
        else:
            spec = pl.BlockSpec((left[0].shape[0], width), lambda i, s: (0, 2 * i + s[0]))
        specs += [spec] * 2
        specs += [pl.BlockSpec(right[0].shape, lambda i, s: (0, 0))] * 2
        operands += [*left, *right]
    flops = sum(4 * left[0].shape[0] * left[0].shape[1] * D // 2 for left, _ in pairs)
    return specs, operands, tuple(doubled), height, flops


def send_sums(numbers, pairs, name):
    specs, operands, doubled, height, flops = weight_specs(pairs, True)
    frames, rows = lax.axis_size("frame") // 2, lax.axis_size("row")
    return pl.pallas_call(
        functools.partial(send_kernel, doubled),
        grid_spec=pltpu.PrefetchScalarGridSpec(
            num_scalar_prefetch=1,
            grid=(frames,),
            in_specs=specs,
            out_specs=pl.BlockSpec((1, rows, height, D), lambda i, s: (i, 0, 0, 0)),
        ),
        out_shape=jax.ShapeDtypeStruct((frames, rows, height, D), jnp.bfloat16),
        compiler_params=vmem_params(60),
        cost_estimate=pl.CostEstimate(flops=flops, bytes_accessed=20 * MIB, transcendentals=0),
        name=name,
    )(numbers, *operands)


def keep_sums(numbers, groups, came, name, by_frame):
    pairs = [pair for group in groups for pair in group]
    specs, operands, doubled, height, flops = weight_specs(pairs, False)
    frames, rows = lax.axis_size("frame") // 2, lax.axis_size("row")
    specs += [pl.BlockSpec((1,) + item.shape[1:], lambda i, s: (i, 0, 0, 0)) for item in came]
    if by_frame:
        kernel = keep_frame_kernel
        shape = (frames // 2, rows, height, D)
        out_spec = pl.BlockSpec((1,) + shape[1:], lambda i, s: (i // 2, 0, 0, 0))
    else:
        kernel = keep_kernel
        shape = (frames, rows // 2, height, D // 2)
        out_spec = pl.BlockSpec((1,) + shape[1:], lambda i, s: (i, 0, 0, 0))
    each = 1 if by_frame else 2
    outs = pl.pallas_call(
        functools.partial(kernel, doubled, tuple(len(group) for group in groups)),
        grid_spec=pltpu.PrefetchScalarGridSpec(
            num_scalar_prefetch=1, grid=(frames,), in_specs=specs, out_specs=[out_spec] * (2 * each)
        ),
        out_shape=[jax.ShapeDtypeStruct(shape, jnp.float32)] * each
        + [jax.ShapeDtypeStruct(shape, jnp.bfloat16)] * each,
        compiler_params=vmem_params(60),
        cost_estimate=pl.CostEstimate(flops=flops, bytes_accessed=40 * MIB, transcendentals=0),
        name=name,
    )(numbers, *operands, *came)
    return list(outs[:each]), list(outs[each:])


def newton_kernel(rows, unroll, pieces, *refs):
    x_refs, out_ref = refs[:pieces], refs[pieces]
    a_ref, t_ref, q_ref, eye_ref, ah, al, nh, th, tl, qh, ql, num_ref = refs[pieces + 1 :]
    width = a_ref.shape[0]
    steps = width // rows
    a_at, m_at, t_at, shift_at, sum_at = 0, 1, 2, 3, 8

    def block(index):
        return pl.ds(pl.multiple_of(index * rows, rows), rows)

    def each(make):
        def one(index, carry):
            make(index)
            return carry

        lax.fori_loop(0, steps, one, 0, unroll=unroll)

    def mean():
        total = num_ref[sum_at]
        for index in range(1, steps):
            total += num_ref[sum_at + index]
        return total * (1.0 / width)

    eye_ref[...] = jnp.where(
        lax.broadcasted_iota(jnp.int32, (rows, rows), 0) == lax.broadcasted_iota(jnp.int32, (rows, rows), 1),
        1.0,
        0.0,
    )
    squares = 0.0
    for index in range(steps):
        columns = slice(index * rows, (index + 1) * rows)
        value = sum(dot_tn(ref[:, columns], ref[:, index * rows :]) for ref in x_refs)
        t_ref[columns, index * rows :] = value
        for other in range(index + 1, steps):
            there = slice(other * rows, (other + 1) * rows)
            t_ref[there, columns] = t_ref[columns, there].T
        squares += jnp.sum(value[:, :rows] * eye_ref[...])
    inverse = 1.0 / (jnp.sqrt(jnp.full((1, 1), squares, jnp.float32)) + 1e-07)
    scale = jnp.sum(inverse)
    scale = scale * scale
    num_ref[a_at] = squares * scale * (1.0 / width)

    def chunks(index):
        for chunk in range(steps):
            yield chunk, slice(chunk * rows, (chunk + 1) * rows), jnp.where(index == chunk, 1.0, 0.0)

    def first_split(index):
        at = block(index)
        total = 0.0
        for _, cut, here in chunks(index):
            value = t_ref[at, cut] * scale - (here * num_ref[a_at]) * eye_ref[...]
            a_ref[at, cut] = value
            ah[at, cut], al[at, cut] = split_two(value)
            total += jnp.sum(value * value)
        num_ref[sum_at + index] = total

    each(first_split)

    for number in range(5):
        two = number < 2
        shift = num_ref[a_at]
        fix = newton_three * mean()
        num_ref[m_at] = newton_one + newton_two * shift + newton_three * shift * shift + fix
        slope = newton_two + 2.0 * newton_three * shift

        def make_n(index):
            at = block(index)
            total = 0.0
            for _, cut, here in chunks(index):
                value = newton_three * dot_low(ah[at, :], ah[:, cut])
                value += slope * a_ref[at, cut] - (here * fix) * eye_ref[...]
                nh[at, cut] = value.astype(jnp.bfloat16)
                total += jnp.sum(value * a_ref[at, cut])
            num_ref[sum_at + index] = total

        each(make_n)
        much = num_ref[m_at]
        keep_low = number < 4 and number >= 2
        if number == 0:

            def first_q(index):
                at = block(index)
                for _, cut, here in chunks(index):
                    value = nh[at, cut].astype(jnp.float32) + (here * much) * eye_ref[...]
                    q_ref[at, cut] = value
                    qh[at, cut] = value.astype(jnp.bfloat16)

            each(first_q)
        else:

            def next_q(index):
                at = block(index)
                high = qh[at, :]
                rest = ql[at, :] if number >= 3 else None
                for _, cut, _ in chunks(index):
                    value = much * q_ref[at, cut] + dot_low(high, nh[:, cut])
                    if number >= 3:
                        value += dot_low(rest, nh[:, cut])
                    t_ref[at, cut] = value
                for _, cut, _ in chunks(index):
                    value = t_ref[at, cut]
                    first, second = split_two(value)
                    qh[at, cut] = first
                    if number >= 2:
                        ql[at, cut] = second
                    if number < 4:
                        q_ref[at, cut] = value

            each(next_q)
        if number == 4:
            break
        fix_t = mean()
        num_ref[t_at] = shift * much + fix_t

        def make_t(index):
            at = block(index)
            total = 0.0
            for _, cut, here in chunks(index):
                value = dot_low(ah[at, :], nh[:, cut])
                if two:
                    value += dot_low(al[at, :], nh[:, cut])
                near = nh[at, cut].astype(jnp.float32)
                value += shift * near + much * a_ref[at, cut] - (here * fix_t) * eye_ref[...]
                t_ref[at, cut] = value
                if two:
                    th[at, cut], tl[at, cut] = split_two(value)
                else:
                    th[at, cut] = value.astype(jnp.bfloat16)
                total += jnp.sum(value * near)
            num_ref[sum_at + index] = total

        each(make_t)
        fix_a = mean()
        t_shift = num_ref[t_at]
        num_ref[a_at] = t_shift * much + fix_a

        def make_a(index):
            at = block(index)
            total = 0.0
            for _, cut, here in chunks(index):
                value = dot_low(nh[at, :], th[:, cut])
                if two:
                    value += dot_low(nh[at, :], tl[:, cut])
                near = nh[at, cut].astype(jnp.float32)
                value += t_shift * near + much * t_ref[at, cut] - (here * fix_a) * eye_ref[...]
                a_ref[at, cut] = value
                if number == 0:
                    ah[at, cut], al[at, cut] = split_two(value)
                else:
                    ah[at, cut] = value.astype(jnp.bfloat16)
                total += jnp.sum(value * value)
            num_ref[sum_at + index] = total

        each(make_a)

    half = out_ref.shape[0] // 2
    for side in range(2):
        mine = x_refs[side][0:half, :]
        out_ref[side * half : (side + 1) * half, :] = (
            (dot_low(mine, qh[...]) + dot_low(mine, ql[...])) * inverse
        ).astype(out_ref.dtype)


def newton(grads, mine_rows, rows=256, unroll=4):
    width = grads[0].shape[1]
    pieces = len(grads)
    low = pltpu.VMEM((width, width), jnp.bfloat16)
    full = pltpu.VMEM((width, width), jnp.float32)
    vmem = pl.BlockSpec(memory_space=pltpu.VMEM)
    return pl.pallas_call(
        functools.partial(newton_kernel, rows, unroll, pieces),
        out_shape=jax.ShapeDtypeStruct((mine_rows, width), jnp.bfloat16),
        in_specs=[vmem] * pieces,
        out_specs=vmem,
        scratch_shapes=[full] * 3
        + [pltpu.VMEM((rows, rows), jnp.float32)]
        + [low] * 7
        + [pltpu.SMEM((16,), jnp.float32)],
        compiler_params=vmem_params(60),
        cost_estimate=pl.CostEstimate(flops=60 * 10**9, bytes_accessed=20 * 10**6, transcendentals=0),
        name="newton",
    )(*grads)


def frame_sums_kernel(count, *refs):
    out_ref = refs[-1]
    ones, twos = refs[:count], refs[count : 2 * count]
    steps, _, frames, _ = ones[0].shape
    at = 0
    for clip in range(count):
        for step in range(steps):
            rows = slice(at, at + frames)
            for index in range(2):
                out_ref[rows, index * D : (index + 1) * D] = ones[clip][step, index]
            for index in range(4):
                out_ref[rows, (index + 2) * D : (index + 3) * D] = twos[clip][step, index]
            at += frames


def frame_sums(ones, twos):
    steps, _, frames, _ = ones[0].shape
    return pl.pallas_call(
        functools.partial(frame_sums_kernel, len(ones)),
        out_shape=jax.ShapeDtypeStruct((len(ones) * steps * frames, 6 * D), jnp.float32),
        in_specs=[pl.BlockSpec(memory_space=pltpu.VMEM)] * (2 * len(ones)),
        out_specs=pl.BlockSpec(memory_space=pltpu.VMEM),
        compiler_params=vmem_params(60),
        cost_estimate=pl.CostEstimate(flops=0, bytes_accessed=MIB, transcendentals=0),
        name="frame_sums",
    )(*ones, *twos)


def swap(slots):
    size = lax.axis_size("row")
    out = [slots[0]]
    for slot in range(1, size):
        out.append(lax.ppermute(slots[slot], "row", [(index, index ^ slot) for index in range(size)]))
    return out


def frame_swap(slots):
    size = lax.axis_size("frame")
    out = [slots[0]]
    for slot in range(1, size // 2):
        pairs = [(index, index ^ (2 * slot)) for index in range(size)]
        out.append(lax.ppermute(slots[slot], "frame", pairs))
    return out


def plane_steps(members):
    size = lax.axis_size("row")
    row_bits = size.bit_length() - 1
    groups = lax.axis_size("frame") // 2
    group_index = lax.axis_index("frame") >> 1
    height = max(item.shape[0] for item in members)
    slab = jnp.stack([jnp.pad(item, ((0, height - item.shape[0]), (0, 0))) for item in members])
    slots = [
        lax.dynamic_index_in_dim(slab, (group_index ^ slot) & 3, 0, keepdims=False) for slot in range(groups)
    ]
    hold = yield slots
    slots = frame_swap(slots)
    slots[0] = held(slots[0], *hold)
    mine = jnp.concatenate(slots, axis=0)
    cut = mine.shape[0] // 2
    grown = [mine[:cut], mine[cut:]]
    for step in range(row_bits):
        hold = yield grown
        for side in range(2):
            bit = step if side == 0 else row_bits - 1 - step
            pairs = [(index, index ^ (1 << bit)) for index in range(size)]
            came = lax.ppermute(grown[side], "row", pairs)
            grown[side] = jnp.concatenate([held(grown[side], *hold), came], axis=0)
    frame_size = lax.axis_size("frame")
    pairs = [(index, index ^ 1) for index in range(frame_size)]
    yield (*grown, *(lax.ppermute(item, "frame", pairs) for item in grown))


def per_device(
    tokens,
    cotangent,
    noise_levels,
    frame_times,
    step_count,
    qkv_master,
    qkv_momentum,
    out_master,
    out_momentum,
    up_master,
    up_momentum,
    down_master,
    down_momentum,
    ada_master,
    ada_first,
    ada_second,
    table_master,
    table_first,
    table_second,
    bias_master,
    bias_first,
    bias_second,
):
    low_type = jnp.bfloat16
    full_type = jnp.float32
    clip_count, frames, rows_dev, columns, model_width = tokens.shape
    seq_local = frames * rows_dev * columns
    row_devices = lax.axis_size("row")
    token_total = clip_count * seq_local
    frame_total = clip_count * frames
    shape_five = (clip_count, frames, rows_dev, columns, model_width)
    both = ("frame", "row")
    frame_devices = lax.axis_size("frame")
    device_total = frame_devices * row_devices
    device_index = lax.axis_index("frame") * row_devices + lax.axis_index("row")
    heights = (qkv_master.shape[1], out_master.shape[0], up_master.shape[1], down_master.shape[0])
    w_qkv = lax.all_gather(qkv_master.T.astype(low_type), both, axis=0, tiled=True)
    shards = jnp.concatenate([down_master, up_master.T, out_master], axis=0).astype(low_type)
    gathered = lax.all_gather(shards, both, axis=0)
    if heights[1] % 16 == 0:

        def from_slab(first, height):
            return gathered, pl.BlockSpec(
                (device_total, height, model_width),
                lambda *_: (0, first // height, 0),
                pipeline_mode=pl.Buffered(1),
            )

    else:

        def from_slab(first, height):
            part = gathered[:, first : first + height].reshape(-1, model_width // row_devices, model_width)
            return part, whole_spec(part)

    w_down = from_slab(0, heights[3])
    w_up = from_slab(heights[3], heights[2])
    w_out = from_slab(heights[3] + heights[2], heights[1])
    level_flat = noise_levels.reshape(frame_total)
    levels_all = lax.all_gather(level_flat, "frame", axis=0, tiled=True)
    frames_all = frame_devices * frame_total
    frames_each = frames_all // device_total
    level_rows = table_master.shape[0]
    my_levels = device_index * level_rows + jnp.arange(level_rows, dtype=jnp.int32)
    level_hot = levels_all[:, None] == my_levels[None, :]
    found = jnp.dot(
        level_hot.astype(low_type),
        lax.optimization_barrier(table_master.astype(low_type)),
        preferred_element_type=full_type,
    )

    def to_all(value):
        return lax.all_to_all(value, both, split_axis=0, concat_axis=0, tiled=True)

    def from_all(value):
        return to_all(jnp.broadcast_to(value[None], (device_total,) + value.shape))

    embedded_mine = jnp.sum(
        to_all(found.reshape(device_total, frames_each, model_width)), axis=0
    )
    embedded_all = from_all(embedded_mine).reshape(frames_all, model_width)
    cond_all = jax.nn.silu(embedded_all).astype(low_type)
    ada_low = lax.optimization_barrier(ada_master.astype(low_type))
    bias_low = lax.optimization_barrier(bias_master.astype(low_type))
    ada_width = ada_master.shape[1]
    mod_columns = jnp.dot(cond_all, ada_low, preferred_element_type=full_type) + bias_low.astype(full_type)
    mod_columns = mod_columns.reshape(frame_devices, 1, frame_total, ada_width)
    mod_columns = jnp.broadcast_to(
        mod_columns, (frame_devices, row_devices, frame_total, ada_width)
    ).reshape(device_total, frame_total, ada_width)
    modulation = jnp.moveaxis(to_all(mod_columns), 0, 1).reshape(frame_total, 6 * model_width)
    grid_shape = (clip_count, frames, rows_dev, columns)
    row_first = lax.axis_index("row") * rows_dev
    time_grid = jnp.broadcast_to(frame_times.astype(full_type)[:, :, None, None], grid_shape)
    row_grid = jnp.broadcast_to(
        (row_first + jnp.arange(rows_dev, dtype=jnp.int32)).astype(full_type)[None, None, :, None],
        grid_shape,
    )
    column_grid = jnp.broadcast_to(
        jnp.arange(columns, dtype=jnp.int32).astype(full_type)[None, None, None, :], grid_shape
    )
    angles = rotary_angles(time_grid, row_grid, column_grid).reshape(clip_count, seq_local, HD // 2)
    flat_angles = angles.reshape(token_total, HD // 2)
    pair_sign = jnp.tile(jnp.array([-1.0, 1.0], full_type), HD)
    cosine = jnp.tile(jnp.repeat(jnp.cos(flat_angles), 2, axis=1), (1, 2))
    sine = jnp.tile(jnp.repeat(jnp.sin(flat_angles), 2, axis=1), (1, 2)) * pair_sign
    tile_count = token_total // 256
    mod = modulation.reshape(tile_count, frame_total // tile_count, 6 * model_width)
    me = lax.axis_index("row").astype(jnp.int32).reshape(1)
    tokens_flat = tokens.reshape(clip_count, seq_local, model_width)
    cotangent_flat = cotangent.reshape(clip_count, seq_local, model_width)
    clips = range(clip_count)
    hidden_one, pieces = [], []
    for clip in clips:
        hidden, *slots = project(me, clip, tokens_flat, mod, cosine, sine, w_qkv, row_devices)
        hidden_one.append(hidden[0])
        pieces.append(swap(slots))
    attended, full, logs = [], [], []
    for clip in clips:
        slots, full_clip, log_clip = attend(pieces[clip])
        attended.append(swap(slots))
        full.append(full_clip)
        logs.append(log_clip)
    d_attended, middles = [], []
    for clip in clips:
        slots, others = middle(
            me, clip, tokens_flat, cotangent_flat, mod, w_out, w_up, w_down, attended[clip]
        )
        d_attended.append(swap(slots))
        middles.append(others)
    block_out = jnp.concatenate([item[0] for item in middles], axis=0).reshape(shape_five)
    att_low, hidden_two, activated, d_branch_two, d_up, d_branch_one, d_middle, two_sums = (
        [item[index] for item in middles] for index in range(1, 9)
    )
    early = scatter_steps(
        [[(activated, d_branch_two)], [(d_up, hidden_two), (att_low, d_branch_one)]], "early", True, []
    )

    def after(value, state):
        return [held(value[0], *state), *value[1:]]

    ready = next(early)
    d_pieces = []
    for clip in clips:
        if clip < clip_count - 1:
            slots = attend_back(pieces[clip], after(d_attended[clip], ready), full[clip], logs[clip])
            before = swap(slots)
            d_pieces.append(before)
            ready = [slots[0]]
            continue
        parts = []
        for pair in range(D // 128 // row_devices):
            slots = attend_back(pieces[clip], after(d_attended[clip], ready), full[clip], logs[clip], pair)
            parts += swap(slots)
            ready = [slots[0], *before[1:]]
        d_pieces.append(parts)
    state = early.send([slots[0]])
    lasts = []
    for clip in clips:
        lasts.append(
            last(
                me, clip, tokens_flat, mod, cosine, sine, w_qkv, d_middle[clip],
                after(d_pieces[clip], state), row_devices,
            )
        )
        if clip < clip_count - 1:
            state = early.send([lasts[clip][2]])
    input_grad = jnp.concatenate([item[1] for item in lasts], axis=0).reshape(shape_five)
    one_sums = [item[2] for item in lasts]
    d_modulation = frame_sums(one_sums, two_sums)
    late = scatter_steps([[([item[0] for item in lasts], hidden_one)]], "late", False, [d_modulation])
    late_state = next(late)
    early_sum = finished(early, early.send(late_state))
    state = late_state
    g_qkv = finished(late, state)

    mod_parts = to_all(jnp.moveaxis(d_modulation.reshape(frame_total, device_total, ada_width), 1, 0))
    mod_parts = held(mod_parts, *late_state)
    mod_mine = (
        jnp.sum(mod_parts.reshape(frame_devices, row_devices, frame_total, ada_width), axis=1)
        .reshape(frames_all, ada_width)
        .astype(low_type)
    )
    g_ada = jnp.einsum("fd,fe->de", cond_all, mod_mine, preferred_element_type=full_type)
    g_bias = jnp.sum(mod_mine.astype(full_type), axis=0)
    d_cond_parts = jnp.einsum("fe,de->fd", mod_mine, ada_low, preferred_element_type=full_type)
    d_cond = jnp.sum(to_all(d_cond_parts.reshape(device_total, frames_each, model_width)), axis=0)
    d_embedded_mine = jax.vjp(jax.nn.silu, embedded_mine)[1](d_cond)[0]
    d_embedded = from_all(d_embedded_mine).reshape(frames_all, model_width)
    g_table = jnp.dot(level_hot.astype(full_type).T, d_embedded, precision=highest)
    g_down = early_sum[: heights[3]]
    g_up = early_sum[heights[3] : heights[3] + heights[2]]
    g_out = early_sum[heights[3] + heights[2] :]
    muon_grads = (g_qkv, g_out, g_up, g_down)
    flipped = (True, False, True, False)

    def tall(value, member):
        return value.T if flipped[member] else value

    muon_moments = (qkv_momentum, out_momentum, up_momentum, down_momentum)
    muon_masters = (qkv_master, out_master, up_master, down_master)
    factors = (math.sqrt(3.0), 1.0, math.sqrt(FF / D), math.sqrt(FF / D))
    adam_local = jnp.sum(g_ada * g_ada) + jnp.sum(g_table * g_table) + jnp.sum(g_bias * g_bias)
    local_total = adam_local + sum((jnp.sum(item * item) for item in muon_grads))
    norm_value = jnp.sqrt(jnp.sum(from_all(jnp.full((1, 128), local_total))[:, 0, 0]))
    clip_factor = jnp.minimum(1.0, clip_limit / (norm_value + 1e-06))
    moments_new = []
    updates = []
    slot_rows = max(heights)
    for member in range(4):
        clipped = clip_factor * muon_grads[member]
        moment = momentum_decay * tall(muon_moments[member], member) + clipped
        update = (clipped + momentum_decay * moment).astype(low_type)
        moments_new.append(tall(moment, member))
        updates.append(update)
    row_steps = plane_steps(updates)
    update_rows = next(row_steps)
    while not isinstance(update_rows, tuple):
        update_rows = row_steps.send([])
    groups = frame_devices // 2
    group_index = lax.axis_index("frame") >> 1
    ortho_rows = newton(update_rows, groups * slot_rows).reshape(groups, slot_rows, model_width)
    ortho_slots = jnp.stack(frame_swap([ortho_rows[slot] for slot in range(groups)]))
    ortho_mine = [
        lax.dynamic_index_in_dim(ortho_slots, (group_index & 3) ^ member, 0, keepdims=False)
        for member in range(4)
    ]
    blocks = [tall(ortho_mine[member][: heights[member]].astype(full_type), member) for member in range(4)]
    masters_new = []
    for member in range(4):
        ortho = blocks[member]
        masters_new.append(
            muon_masters[member] * (1.0 - muon_rate * weight_decay)
            - muon_rate * factors[member] * ortho
        )
    step_value = step_count.astype(full_type)[0]
    ada_first_new, ada_second_new, ada_master_new = adam_update(
        g_ada, ada_first, ada_second, ada_master, 0.03, clip_factor, step_value
    )
    table_clipped = clip_factor * g_table
    table_first_new, table_second_new, table_master_new = adam_update(
        g_table, table_first, table_second, table_master, 0.5, clip_factor, step_value
    )
    bias_first_new, bias_second_new, bias_master_new = adam_update(
        g_bias, bias_first, bias_second, bias_master, 0.5, clip_factor, step_value
    )
    return (
        block_out,
        input_grad,
        norm_value.reshape(1),
        moments_new[0],
        masters_new[0],
        moments_new[1],
        masters_new[1],
        moments_new[2],
        masters_new[2],
        moments_new[3],
        masters_new[3],
        ada_first_new,
        ada_second_new,
        ada_master_new,
        table_first_new,
        table_clipped,
        table_master_new,
        bias_first_new,
        bias_second_new,
        bias_master_new,
    )


def solution(mesh):
    return jax.shard_map(
        per_device,
        mesh=mesh,
        in_specs=(
            P("frame", None, "row", None, None),
            P("frame", None, "row", None, None),
            P("frame", None),
            P("frame", None),
            P(),
            P(None, ("frame", "row")),
            P(None, ("frame", "row")),
            P(("frame", "row"), None),
            P(("frame", "row"), None),
            P(None, ("frame", "row")),
            P(None, ("frame", "row")),
            P(("frame", "row"), None),
            P(("frame", "row"), None),
            P(None, ("frame", "row")),
            P(None, ("frame", "row")),
            P(None, ("frame", "row")),
            P(("frame", "row"), None),
            P(("frame", "row"), None),
            P(("frame", "row"), None),
            P(("frame", "row")),
            P(("frame", "row")),
            P(("frame", "row")),
        ),
        out_specs=(
            P("frame", None, "row", None, None),
            P("frame", None, "row", None, None),
            P(),
            P(None, ("frame", "row")),
            P(None, ("frame", "row")),
            P(("frame", "row"), None),
            P(("frame", "row"), None),
            P(None, ("frame", "row")),
            P(None, ("frame", "row")),
            P(("frame", "row"), None),
            P(("frame", "row"), None),
            P(None, ("frame", "row")),
            P(None, ("frame", "row")),
            P(None, ("frame", "row")),
            P(("frame", "row"), None),
            P(("frame", "row"), None),
            P(("frame", "row"), None),
            P(("frame", "row")),
            P(("frame", "row")),
            P(("frame", "row")),
        ),
        check_vma=False,
    )
```

```python
import functools
import math

import jax
import jax.numpy as jnp
from jax import lax
from jax.experimental import pallas as pl
from jax.experimental.pallas import tpu as pltpu
from jax.sharding import PartitionSpec as P

D = 1024
HEADS = 16
HD = 64
FF = 4096


highest = lax.Precision.HIGHEST
newton_one = 3.4445
newton_two = -4.775
newton_three = 2.0315
momentum_decay = 0.95
muon_rate = 1.5
weight_decay = 0.01
beta_first = 0.9
beta_second = 0.95
adam_floor = 1e-08
norm_floor = 1e-06
clip_limit = 1.0
rotary_base = 10000.0


def rotary_angles(time_grid, row_grid, column_grid):
    quarter_pairs = HD // 4
    eighth_pairs = HD // 8
    time_rates = rotary_base ** (-jnp.arange(quarter_pairs, dtype=jnp.float32) / quarter_pairs)
    space_rates = rotary_base ** (-jnp.arange(eighth_pairs, dtype=jnp.float32) / eighth_pairs)
    return jnp.concatenate(
        [
            time_grid[..., None] * time_rates,
            row_grid[..., None] * space_rates,
            column_grid[..., None] * space_rates,
        ],
        axis=-1,
    )


def adam_update(grad_item, first, second, master, rate, clip_factor, step_value):
    clipped = clip_factor * grad_item
    first_new = beta_first * first + (1.0 - beta_first) * clipped
    second_new = beta_second * second + (1.0 - beta_second) * clipped * clipped
    first_fix = 1.0 - beta_first**step_value
    second_fix = 1.0 - beta_second**step_value
    master_new = master * (1.0 - rate * weight_decay) - rate * (first_new / first_fix) / (
        jnp.sqrt(second_new / second_fix) + adam_floor
    )
    return (first_new, second_new, master_new)


def halves(value, dim, axis, bit):
    mine = (lax.axis_index(axis) >> bit) & 1
    keep = lax.dynamic_index_in_dim(value, mine, dim, keepdims=False)
    send = lax.dynamic_index_in_dim(value, 1 - mine, dim, keepdims=False)
    return keep, send.astype(jnp.bfloat16)


def joined(keep, send, axis, bit):
    size = lax.axis_size(axis)
    came = lax.ppermute(send, axis, [(index, index ^ (1 << bit)) for index in range(size)])
    return keep + came.astype(jnp.float32)


def held(value, *others):
    if not others:
        return value
    return lax.optimization_barrier((value, *others))[0]


def scatter_steps(groups, name, by_frame, ready, keep_ready=()):
    frame_bits = lax.axis_size("frame").bit_length() - 1
    row_bits = lax.axis_size("row").bit_length() - 1
    row, frame = lax.axis_index("row"), lax.axis_index("frame")
    numbers = jnp.stack([frame & 1, row & 1, row >> (row_bits - 1), (frame >> 1) & 1]).astype(jnp.int32)
    numbers = held(numbers, *ready)
    size = lax.axis_size("frame")
    came = []
    for at, group in enumerate(groups):
        send = send_sums(numbers, group, f"{name}_send_{at}")
        came.append(lax.ppermute(send, "frame", [(index, index ^ 1) for index in range(size)]))
        numbers = held(numbers, send)
    numbers = held(numbers, *keep_ready)
    keep, send = keep_sums(numbers, groups, came, name + "_keep", by_frame)
    hold = yield send
    names = [("frame", bit) for bit in reversed(range(1, frame_bits))]
    names += [("row", bit) for bit in reversed(range(row_bits))]
    rest = [("frame", bit) for bit in range(1, frame_bits)]
    side_names = []
    if by_frame:
        names.remove(("frame", 1))
        rest.remove(("frame", 1))
        value = joined(held(keep[0], *hold), send[0], "frame", 1)
        value = value.reshape((2,) * len(names) + value.shape[2:])
        width = value.shape[-1] // 2
        keep, send = [], []
        for side in range(2):
            bit = 0 if side == 0 else row_bits - 1
            side_names.append([item for item in names if item != ("row", bit)])
            part = value[..., side * width : (side + 1) * width]
            kept, sent = halves(part, names.index(("row", bit)), "row", bit)
            keep.append(kept)
            send.append(sent)
        hold = yield send
    else:
        for side in range(2):
            bit = 0 if side == 0 else row_bits - 1
            side_names.append([item for item in names if item != ("row", bit)])
            shape = (2,) * (len(names) - 1) + keep[side].shape[2:]
            keep[side] = keep[side].reshape(shape)
            send[side] = send[side].reshape(shape)
    for step in range(row_bits):
        parts = []
        for side in range(2):
            bit = step if side == 0 else row_bits - 1 - step
            parts.append(joined(held(keep[side], *hold), send[side], "row", bit))
        if step == row_bits - 1:
            break
        for side in range(2):
            bit = step + 1 if side == 0 else row_bits - 2 - step
            dim = side_names[side].index(("row", bit))
            side_names[side].pop(dim)
            keep[side], send[side] = halves(parts[side], dim, "row", bit)
        hold = yield send
    value = jnp.concatenate(parts, axis=-1)
    value = value.reshape((-1,) + value.shape[-2:])
    count = value.shape[0]
    low = rest[0][1] if rest else 0
    mine = frame >> low
    keep = lax.dynamic_index_in_dim(value, mine & (count - 1), 0, keepdims=False)
    sends = [
        lax.dynamic_index_in_dim(value, (mine ^ slot) & (count - 1), 0, keepdims=False).astype(jnp.bfloat16)
        for slot in range(1, count)
    ]
    hold = yield sends
    keep = held(keep, *hold)
    for slot, send in enumerate(sends, 1):
        pairs = [(index, index ^ (slot << low)) for index in range(size)]
        keep = keep + lax.ppermute(send, "frame", pairs).astype(jnp.float32)
    yield keep


def finished(steps, state):
    while isinstance(state, list):
        state = steps.send([])
    return state


def split_two(value):
    high = value.astype(jnp.bfloat16)
    return high, (value - high.astype(jnp.float32)).astype(jnp.bfloat16)


def dot_low(left, right):
    return lax.dot_general(left, right, (((1,), (0,)), ((), ())), preferred_element_type=jnp.float32)


def dot_nt(left, right):
    return lax.dot_general(left, right, (((1,), (1,)), ((), ())), preferred_element_type=jnp.float32)


def dot_tn(left, right):
    return lax.dot_general(left, right, (((0,), (0,)), ((), ())), preferred_element_type=jnp.float32)


MIB = 1024 * 1024


def vmem_params(mib, semantics=None):
    return pltpu.CompilerParams(vmem_limit_bytes=mib * MIB, dimension_semantics=semantics)


def whole_spec(array):
    zeros = (0,) * array.ndim
    return pl.BlockSpec(array.shape, lambda *_: zeros, pipeline_mode=pl.Buffered(1))


def turned(value, cosine, sine):
    even = lax.broadcasted_iota(jnp.int32, value.shape, 1) % 2 == 0
    width = value.shape[1]
    swapped = jnp.where(even, pltpu.roll(value, width - 1, 1), pltpu.roll(value, 1, 1))
    return value * cosine + swapped * sine


def framed(value, frames):
    rows, width = value.shape
    return value.reshape(frames, rows // frames, width)


def norm_parts(value):
    mean = jnp.mean(value, axis=-1, keepdims=True)
    centered = value - mean
    root = lax.rsqrt(jnp.mean(centered * centered, axis=-1, keepdims=True) + norm_floor)
    return centered * root, root


def project_kernel(slots, me_ref, x_ref, mod_ref, cos_ref, sin_ref, w_ref, hid_ref, *out_refs):
    frames = mod_ref.shape[1]
    group = D // slots
    normed, _ = norm_parts(x_ref[0].astype(jnp.float32))
    normed = framed(normed, frames)
    shift = mod_ref[0, :, 0:D][:, None, :]
    scaling = mod_ref[0, :, D : 2 * D][:, None, :]
    hidden = (normed * (1.0 + scaling) + shift).reshape(x_ref.shape[1], D).astype(jnp.bfloat16)
    hid_ref[0] = hidden
    cosine = cos_ref[...]
    sine = sin_ref[...]
    me = me_ref[0]
    for slot in range(slots):
        peer = me ^ slot
        for part in range(3):
            rows = pl.ds(pl.multiple_of(part * D + peer * group, group), group)
            value = dot_nt(hidden, w_ref[rows, :])
            if part == 2:
                out_refs[slot][part] = value.astype(jnp.bfloat16)
                continue
            for first in range(0, group, 128):
                piece = turned(value[:, first : first + 128], cosine, sine)
                if part == 0:
                    piece = piece * (1.0 / math.sqrt(HD))
                out_refs[slot][part, :, first : first + 128] = piece.astype(jnp.bfloat16)


def project(me, clip, tokens, mod, cosine, sine, w_qkv, slots):
    count, tall_rows, _ = tokens.shape
    tile = 256
    steps = tall_rows // tile
    group = D // slots
    out_shape = [jax.ShapeDtypeStruct((1, tall_rows, D), jnp.bfloat16)]
    out_shape += [jax.ShapeDtypeStruct((3, tall_rows, group), jnp.bfloat16)] * slots
    return pl.pallas_call(
        functools.partial(project_kernel, slots),
        grid=(steps,),
        in_specs=[
            pl.BlockSpec(memory_space=pltpu.SMEM),
            pl.BlockSpec((1, tile, D), lambda i: (clip, i, 0)),
            pl.BlockSpec((1, mod.shape[1], 6 * D), lambda i: (clip * steps + i, 0, 0)),
            pl.BlockSpec((tile, 128), lambda i: (clip * steps + i, 0)),
            pl.BlockSpec((tile, 128), lambda i: (clip * steps + i, 0)),
            whole_spec(w_qkv),
        ],
        out_specs=[pl.BlockSpec((1, tile, D), lambda i: (0, i, 0))]
        + [pl.BlockSpec((3, tile, group), lambda i: (0, i, 0))] * slots,
        out_shape=out_shape,
        compiler_params=vmem_params(60),
        cost_estimate=pl.CostEstimate(
            flops=6 * tall_rows * D * D, bytes_accessed=10 * MIB, transcendentals=0
        ),
        name="project",
    )(me, tokens, mod, cosine, sine, w_qkv)


def head_mask(shape, head, axis):
    return lax.broadcasted_iota(jnp.int32, shape, axis) // HD == head


def attend_kernel(slots, tile, *refs):
    ins, outs = refs[:slots], refs[slots : 2 * slots]
    full_ref, log_ref, qs, ks, vs = refs[2 * slots :]
    length = ins[0].shape[1]
    for slot in range(slots):
        rows = slice(slot * length, (slot + 1) * length)
        qs[rows, :] = ins[slot][0]
        ks[rows, :] = ins[slot][1]
        vs[rows, :] = ins[slot][2]

    def one(index, carry):
        rows = pl.ds(pl.multiple_of(index * tile, tile), tile)
        query = qs[rows, :]
        first = head_mask((tile, 128), 0, 1)
        parts = []
        logs = []
        for head in range(2):
            masked = jnp.where(first if head == 0 else ~first, query, jnp.zeros_like(query))
            scores = dot_nt(masked, ks[...])
            top = jnp.max(scores, axis=-1, keepdims=True)
            raised = jnp.exp(scores - top)
            total = jnp.sum(raised, axis=-1, keepdims=True)
            parts.append(dot_low(raised.astype(jnp.bfloat16), vs[...]) * (1.0 / total))
            logs.append(top + jnp.log(total))
        full_ref[rows, :] = jnp.where(first, parts[0], parts[1])
        log_ref[rows, :] = jnp.where(first, logs[0], logs[1])
        return carry

    lax.fori_loop(0, slots * length // tile, one, 0)
    for slot in range(slots):
        rows = slice(slot * length, (slot + 1) * length)
        outs[slot][...] = full_ref[rows, :].astype(jnp.bfloat16)


def attend(pieces):
    slots = len(pieces)
    _, length, group = pieces[0].shape
    total = slots * length
    scratch = pltpu.VMEM((total, 128), jnp.bfloat16)
    outs = pl.pallas_call(
        functools.partial(attend_kernel, slots, 256),
        grid=(group // 128,),
        in_specs=[pl.BlockSpec((3, length, 128), lambda i: (0, 0, i))] * slots,
        out_specs=[pl.BlockSpec((length, 128), lambda i: (0, i))] * slots
        + [pl.BlockSpec((total, 128), lambda i: (0, i))] * 2,
        out_shape=[jax.ShapeDtypeStruct((length, group), jnp.bfloat16)] * slots
        + [jax.ShapeDtypeStruct((total, group), jnp.float32)] * 2,
        scratch_shapes=[scratch] * 3,
        compiler_params=vmem_params(60),
        cost_estimate=pl.CostEstimate(
            flops=16 * total * total * group, bytes_accessed=8 * MIB, transcendentals=total * total * 4
        ),
        name="attend",
    )(*pieces)
    return outs[:slots], outs[slots], outs[slots + 1]


def attend_back_kernel(slots, tile, *refs):
    ins, grads = refs[:slots], refs[slots : 2 * slots]
    full_ref, log_ref = refs[2 * slots : 2 * slots + 2]
    outs = refs[2 * slots + 2 : 3 * slots + 2]
    qs, ks, vs, gs, q_turned, g_turned, dq, dk, dv = refs[3 * slots + 2 :]
    length = ins[0].shape[1]
    total = slots * length
    for slot in range(slots):
        rows = slice(slot * length, (slot + 1) * length)
        qs[rows, :] = ins[slot][0]
        ks[rows, :] = ins[slot][1]
        vs[rows, :] = ins[slot][2]
        gs[rows, :] = grads[slot][...]
        q_turned[:, rows] = ins[slot][0].T
        g_turned[:, rows] = grads[slot][...].T
    dk[...] = jnp.zeros_like(dk)
    dv[...] = jnp.zeros_like(dv)

    def one(index, carry):
        rows = pl.ds(pl.multiple_of(index * tile, tile), tile)
        first = head_mask((tile, 128), 0, 1)
        upper = head_mask((128, tile), 0, 0)
        query, grad = qs[rows, :], gs[rows, :]
        query_t, grad_t = q_turned[:, rows], g_turned[:, rows]
        product = grad.astype(jnp.float32) * full_ref[rows, :]
        masks = (first, ~first)
        masks_t = (upper, ~upper)
        zero = jnp.zeros_like(query)
        zero_t = jnp.zeros_like(query_t)
        q_low = [jnp.where(mask, query, zero) for mask in masks]
        g_low = [jnp.where(mask, grad, zero) for mask in masks]
        qt_low = [jnp.where(mask, query_t, zero_t) for mask in masks_t]
        gt_low = [jnp.where(mask, grad_t, zero_t) for mask in masks_t]
        inner = [jnp.sum(jnp.where(mask, product, 0.0), axis=-1, keepdims=True) for mask in masks]
        logs = [log_ref[rows, 0:1], log_ref[rows, HD : HD + 1]]

        def inside(k_index, sums):
            at = pl.ds(pl.multiple_of(k_index * tile, tile), tile)
            key, value = ks[at, :], vs[at, :]
            out = []
            for head in range(2):
                probs = jnp.exp(dot_nt(q_low[head], key) - logs[head])
                d_probs = dot_nt(g_low[head], value)
                d_scores = (probs * (d_probs - inner[head])).astype(jnp.bfloat16)
                dv[:, at] += dot_low(gt_low[head], probs.astype(jnp.bfloat16))
                dk[:, at] += dot_low(qt_low[head], d_scores)
                out.append(sums[head] + dot_low(d_scores, key))
            return tuple(out)

        start = jnp.zeros((tile, 128), jnp.float32)
        sums = lax.fori_loop(0, total // tile, inside, (start, start))
        dq[rows, :] = (jnp.where(first, sums[0], sums[1]) * (1.0 / math.sqrt(HD))).astype(jnp.bfloat16)
        return carry

    lax.fori_loop(0, total // tile, one, 0)
    for slot in range(slots):
        rows = slice(slot * length, (slot + 1) * length)
        outs[slot][0] = dq[rows, :]
        outs[slot][1] = dk[:, rows].T.astype(jnp.bfloat16)
        outs[slot][2] = dv[:, rows].T.astype(jnp.bfloat16)


def attend_back(pieces, grads, full, logs, pair=None):
    slots = len(pieces)
    _, length, group = pieces[0].shape
    first = 0 if pair is None else pair
    count = group // 128 if pair is None else 1
    group = 128 * count
    total = slots * length
    low = pltpu.VMEM((total, 128), jnp.bfloat16)
    low_t = pltpu.VMEM((128, total), jnp.bfloat16)
    full_t = pltpu.VMEM((128, total), jnp.float32)
    return pl.pallas_call(
        functools.partial(attend_back_kernel, slots, 512),
        grid=(count,),
        in_specs=[pl.BlockSpec((3, length, 128), lambda i: (0, 0, i + first))] * slots
        + [pl.BlockSpec((length, 128), lambda i: (0, i + first))] * slots
        + [pl.BlockSpec((total, 128), lambda i: (0, i + first))] * 2,
        out_specs=[pl.BlockSpec((3, length, 128), lambda i: (0, 0, i))] * slots,
        out_shape=[jax.ShapeDtypeStruct((3, length, group), jnp.bfloat16)] * slots,
        scratch_shapes=[low] * 4 + [low_t] * 2 + [low] + [full_t] * 2,
        compiler_params=vmem_params(60),
        cost_estimate=pl.CostEstimate(
            flops=40 * total * total * group, bytes_accessed=12 * MIB, transcendentals=total * total * 4
        ),
        name="attend_back",
    )(*pieces, *grads, full, logs)


def part_of(ref, index, size):
    count = size // ref.shape[1]
    return ref[pl.ds(index * count, count)].reshape(size, ref.shape[2])


def middle_kernel(slots, me_ref, x_ref, cot_ref, mod_ref, wo_ref, wu_ref, wd_ref, *refs):
    att_refs = refs[:slots]
    datt_refs = refs[slots : 2 * slots]
    (
        out_ref,
        att_ref,
        h2_ref,
        act_ref,
        db2_ref,
        dup_ref,
        db1_ref,
        dmid_ref,
        sums_ref,
        slope,
    ) = refs[2 * slots :]
    frames = mod_ref.shape[1]
    rows = x_ref.shape[1]
    group = D // slots
    me = me_ref[0]

    def mod(index):
        return mod_ref[0, :, index * D : (index + 1) * D][:, None, :]

    def spread(value, index, plus=0.0):
        return (framed(value, frames) * (mod(index) + plus)).reshape(rows, D)

    def frame_sum(value):
        return jnp.sum(framed(value, frames), axis=1)

    branch = jnp.zeros((rows, D), jnp.float32)
    for slot in range(slots):
        at = pl.ds(pl.multiple_of((me ^ slot) * group, group), group)
        piece = att_refs[slot][...]
        att_ref[:, at] = piece
        branch += dot_low(piece, part_of(wo_ref, me ^ slot, group))
    middle = x_ref[0].astype(jnp.float32) + spread(branch, 2)
    normed, root = norm_parts(middle)
    hidden = (framed(spread(normed, 4, 1.0), frames) + mod(3)).reshape(rows, D).astype(jnp.bfloat16)
    h2_ref[...] = hidden
    wide = 1024
    curve = math.sqrt(2.0 / math.pi)
    branch_two = jnp.zeros((rows, D), jnp.float32)
    for first in range(0, FF, wide):
        cut = slice(first, first + wide)
        up = dot_nt(hidden, part_of(wu_ref, first // wide, wide))
        square = up * up
        bent = jnp.tanh(curve * up * (1.0 + 0.044715 * square))
        half = 0.5 * (1.0 + bent)
        active = (up * half).astype(jnp.bfloat16)
        slope[:, cut] = half + 0.5 * up * (1.0 - bent * bent) * (curve * (1.0 + 3 * 0.044715 * square))
        act_ref[:, cut] = active
        branch_two += dot_low(active, part_of(wd_ref, first // wide, wide))
    cot = cot_ref[0].astype(jnp.float32)
    out_ref[0] = (middle + spread(branch_two, 5)).astype(jnp.bfloat16)
    sums_ref[0, 3] = frame_sum(cot * branch_two)
    d_branch_two = spread(cot, 5).astype(jnp.bfloat16)
    db2_ref[...] = d_branch_two
    d_hidden = jnp.zeros((rows, D), jnp.float32)
    for first in range(0, FF, wide):
        cut = slice(first, first + wide)
        d_up = (dot_nt(d_branch_two, part_of(wd_ref, first // wide, wide)) * slope[:, cut]).astype(jnp.bfloat16)
        dup_ref[:, cut] = d_up
        d_hidden += dot_low(d_up, part_of(wu_ref, first // wide, wide))
    sums_ref[0, 1] = frame_sum(d_hidden)
    sums_ref[0, 2] = frame_sum(d_hidden * normed)
    inner = spread(d_hidden, 4, 1.0)
    d_middle = cot + root * (
        inner
        - jnp.mean(inner, axis=-1, keepdims=True)
        - normed * jnp.mean(inner * normed, axis=-1, keepdims=True)
    )
    dmid_ref[...] = d_middle
    sums_ref[0, 0] = frame_sum(d_middle * branch)
    d_branch = spread(d_middle, 2).astype(jnp.bfloat16)
    db1_ref[...] = d_branch
    for slot in range(slots):
        datt_refs[slot][...] = dot_nt(d_branch, part_of(wo_ref, me ^ slot, group)).astype(jnp.bfloat16)


def middle(me, clip, tokens, cotangent, mod, w_out, w_up, w_down, attended):
    slots = len(attended)
    count, length, _ = tokens.shape
    tile = 256
    steps = length // tile
    group = D // slots
    frames = mod.shape[1]
    low = jnp.bfloat16

    def flat(width, kind=low):
        return jax.ShapeDtypeStruct((length, width), kind)

    def flat_spec(width):
        return pl.BlockSpec((tile, width), lambda i: (i, 0))

    outs = pl.pallas_call(
        functools.partial(middle_kernel, slots),
        grid=(steps,),
        in_specs=[
            pl.BlockSpec(memory_space=pltpu.SMEM),
            pl.BlockSpec((1, tile, D), lambda i: (clip, i, 0)),
            pl.BlockSpec((1, tile, D), lambda i: (clip, i, 0)),
            pl.BlockSpec((1, frames, 6 * D), lambda i: (clip * steps + i, 0, 0)),
            *(item[1] for item in (w_out, w_up, w_down)),
        ]
        + [flat_spec(group)] * slots,
        out_specs=[flat_spec(group)] * slots
        + [pl.BlockSpec((1, tile, D), lambda i: (0, i, 0))]
        + [flat_spec(width) for width in (D, D, FF, D, FF, D, D)]
        + [pl.BlockSpec((1, 4, frames, D), lambda i: (i, 0, 0, 0))],
        out_shape=[flat(group)] * slots
        + [jax.ShapeDtypeStruct((1, length, D), low)]
        + [flat(D), flat(D), flat(FF), flat(D), flat(FF), flat(D), flat(D, jnp.float32)]
        + [jax.ShapeDtypeStruct((steps, 4, frames, D), jnp.float32)],
        scratch_shapes=[pltpu.VMEM((tile, FF), jnp.float32)],
        compiler_params=vmem_params(60),
        cost_estimate=pl.CostEstimate(
            flops=2 * length * D * (2 * D + 4 * FF), bytes_accessed=40 * MIB, transcendentals=length * FF
        ),
        name="middle",
    )(me, tokens, cotangent, mod, *(item[0] for item in (w_out, w_up, w_down)), *attended)
    return outs[:slots], outs[slots:]


def last_kernel(slots, me_ref, x_ref, mod_ref, cos_ref, sin_ref, w_ref, dmid_ref, *refs):
    pieces = refs[:-3]
    dproj_ref, grad_ref, sums_ref = refs[-3:]
    frames = mod_ref.shape[1]
    rows = x_ref.shape[1]
    group = D // slots
    pairs = len(pieces) // slots
    narrow = group // pairs
    me = me_ref[0]
    cosine = cos_ref[...]
    sine = -sin_ref[...]
    d_hidden = jnp.zeros((rows, D), jnp.float32)
    for slot in range(slots):
        peer = me ^ slot
        for part in range(3):
            base = pl.multiple_of(part * D + peer * group, group)
            if part == 2:
                value = jnp.concatenate([pieces[pair * slots + slot][part] for pair in range(pairs)], axis=1)
            else:
                value = jnp.concatenate(
                    [
                        turned(
                            pieces[at // narrow * slots + slot][
                                part, :, at % narrow : at % narrow + 128
                            ].astype(jnp.float32),
                            cosine,
                            sine,
                        )
                        for at in range(0, group, 128)
                    ],
                    axis=1,
                ).astype(jnp.bfloat16)
            dproj_ref[:, pl.ds(base, group)] = value
            d_hidden += dot_low(value, w_ref[pl.ds(base, group), :])
    normed, root = norm_parts(x_ref[0].astype(jnp.float32))
    scaling = mod_ref[0, :, D : 2 * D][:, None, :]
    sums_ref[0, 0] = jnp.sum(framed(d_hidden, frames), axis=1)
    sums_ref[0, 1] = jnp.sum(framed(d_hidden * normed, frames), axis=1)
    inner = (framed(d_hidden, frames) * (1.0 + scaling)).reshape(rows, D)
    grad_ref[0] = dmid_ref[...] + root * (
        inner
        - jnp.mean(inner, axis=-1, keepdims=True)
        - normed * jnp.mean(inner * normed, axis=-1, keepdims=True)
    )


def last(me, clip, tokens, mod, cosine, sine, w_qkv, d_middle, pieces, slots):
    count, length, _ = tokens.shape
    tile = 256
    steps = length // tile
    narrow = pieces[0].shape[2]
    frames = mod.shape[1]
    return pl.pallas_call(
        functools.partial(last_kernel, slots),
        grid=(steps,),
        in_specs=[
            pl.BlockSpec(memory_space=pltpu.SMEM),
            pl.BlockSpec((1, tile, D), lambda i: (clip, i, 0)),
            pl.BlockSpec((1, frames, 6 * D), lambda i: (clip * steps + i, 0, 0)),
            pl.BlockSpec((tile, 128), lambda i: (clip * steps + i, 0)),
            pl.BlockSpec((tile, 128), lambda i: (clip * steps + i, 0)),
            whole_spec(w_qkv),
            pl.BlockSpec((tile, D), lambda i: (i, 0)),
        ]
        + [pl.BlockSpec((3, tile, narrow), lambda i: (0, i, 0))] * len(pieces),
        out_specs=[
            pl.BlockSpec((tile, 3 * D), lambda i: (i, 0)),
            pl.BlockSpec((1, tile, D), lambda i: (0, i, 0)),
            pl.BlockSpec((1, 2, frames, D), lambda i: (i, 0, 0, 0)),
        ],
        out_shape=[
            jax.ShapeDtypeStruct((length, 3 * D), jnp.bfloat16),
            jax.ShapeDtypeStruct((1, length, D), jnp.float32),
            jax.ShapeDtypeStruct((steps, 2, frames, D), jnp.float32),
        ],
        compiler_params=vmem_params(60),
        cost_estimate=pl.CostEstimate(
            flops=6 * length * D * D, bytes_accessed=20 * MIB, transcendentals=0
        ),
        name="last",
    )(me, tokens, mod, cosine, sine, w_qkv, d_middle, *pieces)


def member_value(refs, member, doubled, parity):
    left = refs[4 * member : 4 * member + 2]
    right = refs[4 * member + 2 : 4 * member + 4]
    value = dot_tn(left[0][...], right[0][...]) + dot_tn(left[1][...], right[1][...])
    if doubled:
        half = value.shape[0] // 2
        value = jnp.where(parity == 0, value[:half], value[half:])
    return value


def send_kernel(doubled, number_ref, *refs):
    out_ref = refs[-1]
    rows = out_ref.shape[1]
    first = 0
    for member in range(len(doubled)):
        value = member_value(refs, member, doubled[member], 1 - number_ref[0])
        height = value.shape[0] // rows
        out_ref[0, :, first : first + height, :] = value.reshape(rows, height, D).astype(out_ref.dtype)
        first += height


def keep_kernel(doubled, counts, number_ref, *refs):
    members = len(doubled)
    came_refs = refs[4 * members : 4 * members + len(counts)]
    keep_refs, send_refs = refs[-4:-2], refs[-2:]
    half_rows = keep_refs[0].shape[1]
    width = D // 2
    first = 0
    member = 0
    for came_ref, count in zip(came_refs, counts):
        inside = 0
        for _ in range(count):
            value = member_value(refs, member, doubled[member], number_ref[0])
            height = value.shape[0] // (2 * half_rows)
            rows = slice(first, first + height)
            parts = [
                value[row * height : (row + 1) * height]
                + came_ref[0, row, inside : inside + height, :].astype(jnp.float32)
                for row in range(2 * half_rows)
            ]
            for place in range(half_rows):
                for side in range(2):
                    cut = slice(side * width, (side + 1) * width)
                    low = 2 * place if side == 0 else place
                    high = low + (1 if side == 0 else half_rows)
                    upper = number_ref[1 + side] == 1
                    zero, one = parts[low][:, cut], parts[high][:, cut]
                    keep_refs[side][0, place, rows, :] = jnp.where(upper, one, zero)
                    send_refs[side][0, place, rows, :] = jnp.where(upper, zero, one).astype(jnp.bfloat16)
            first += height
            inside += height
            member += 1


def keep_frame_kernel(doubled, counts, number_ref, *refs):
    members = len(doubled)
    came_refs = refs[4 * members : 4 * members + len(counts)]
    keep_ref, send_ref = refs[-2:]
    rows = keep_ref.shape[1]
    kept = lax.rem(pl.program_id(0), 2) == number_ref[3]
    first = 0
    member = 0
    for came_ref, count in zip(came_refs, counts):
        inside = 0
        for _ in range(count):
            value = member_value(refs, member, doubled[member], number_ref[0])
            height = value.shape[0] // rows
            value = value.reshape(rows, height, D)
            value += came_ref[0, :, inside : inside + height, :].astype(jnp.float32)
            at = slice(first, first + height)

            @pl.when(kept)
            def _(value=value, at=at):
                keep_ref[0, :, at, :] = value

            @pl.when(jnp.logical_not(kept))
            def _(value=value, at=at):
                send_ref[0, :, at, :] = value.astype(jnp.bfloat16)

            first += height
            inside += height
            member += 1


def weight_specs(pairs, other):
    frame_devices = lax.axis_size("frame")
    specs, operands, doubled = [], [], []
    height = 0
    for left, right in pairs:
        width = left[0].shape[1] // frame_devices
        height += width // lax.axis_size("row")
        doubled.append(width % 128 != 0)
        if doubled[-1]:
            spec = pl.BlockSpec((left[0].shape[0], 2 * width), lambda i, s: (0, i))
        elif other:
            spec = pl.BlockSpec((left[0].shape[0], width), lambda i, s: (0, 2 * i + 1 - s[0]))
        else:
            spec = pl.BlockSpec((left[0].shape[0], width), lambda i, s: (0, 2 * i + s[0]))
        specs += [spec] * 2
        specs += [pl.BlockSpec(right[0].shape, lambda i, s: (0, 0))] * 2
        operands += [*left, *right]
    flops = sum(4 * left[0].shape[0] * left[0].shape[1] * D // 2 for left, _ in pairs)
    return specs, operands, tuple(doubled), height, flops


def send_sums(numbers, pairs, name):
    specs, operands, doubled, height, flops = weight_specs(pairs, True)
    frames, rows = lax.axis_size("frame") // 2, lax.axis_size("row")
    return pl.pallas_call(
        functools.partial(send_kernel, doubled),
        grid_spec=pltpu.PrefetchScalarGridSpec(
            num_scalar_prefetch=1,
            grid=(frames,),
            in_specs=specs,
            out_specs=pl.BlockSpec((1, rows, height, D), lambda i, s: (i, 0, 0, 0)),
        ),
        out_shape=jax.ShapeDtypeStruct((frames, rows, height, D), jnp.bfloat16),
        compiler_params=vmem_params(60),
        cost_estimate=pl.CostEstimate(flops=flops, bytes_accessed=20 * MIB, transcendentals=0),
        name=name,
    )(numbers, *operands)


def keep_sums(numbers, groups, came, name, by_frame):
    pairs = [pair for group in groups for pair in group]
    specs, operands, doubled, height, flops = weight_specs(pairs, False)
    frames, rows = lax.axis_size("frame") // 2, lax.axis_size("row")
    specs += [pl.BlockSpec((1,) + item.shape[1:], lambda i, s: (i, 0, 0, 0)) for item in came]
    if by_frame:
        kernel = keep_frame_kernel
        shape = (frames // 2, rows, height, D)
        out_spec = pl.BlockSpec((1,) + shape[1:], lambda i, s: (i // 2, 0, 0, 0))
    else:
        kernel = keep_kernel
        shape = (frames, rows // 2, height, D // 2)
        out_spec = pl.BlockSpec((1,) + shape[1:], lambda i, s: (i, 0, 0, 0))
    each = 1 if by_frame else 2
    outs = pl.pallas_call(
        functools.partial(kernel, doubled, tuple(len(group) for group in groups)),
        grid_spec=pltpu.PrefetchScalarGridSpec(
            num_scalar_prefetch=1, grid=(frames,), in_specs=specs, out_specs=[out_spec] * (2 * each)
        ),
        out_shape=[jax.ShapeDtypeStruct(shape, jnp.float32)] * each
        + [jax.ShapeDtypeStruct(shape, jnp.bfloat16)] * each,
        compiler_params=vmem_params(60),
        cost_estimate=pl.CostEstimate(flops=flops, bytes_accessed=40 * MIB, transcendentals=0),
        name=name,
    )(numbers, *operands, *came)
    return list(outs[:each]), list(outs[each:])


def newton_kernel(rows, unroll, pieces, *refs):
    x_refs, out_ref = refs[:pieces], refs[pieces]
    a_ref, t_ref, q_ref, eye_ref, ah, al, nh, th, tl, qh, ql, num_ref = refs[pieces + 1 :]
    width = a_ref.shape[0]
    steps = width // rows
    a_at, m_at, t_at, shift_at, sum_at = 0, 1, 2, 3, 8

    def block(index):
        return pl.ds(pl.multiple_of(index * rows, rows), rows)

    def each(make):
        def one(index, carry):
            make(index)
            return carry

        lax.fori_loop(0, steps, one, 0, unroll=unroll)

    def mean():
        total = num_ref[sum_at]
        for index in range(1, steps):
            total += num_ref[sum_at + index]
        return total * (1.0 / width)

    eye_ref[...] = jnp.where(
        lax.broadcasted_iota(jnp.int32, (rows, rows), 0) == lax.broadcasted_iota(jnp.int32, (rows, rows), 1),
        1.0,
        0.0,
    )
    squares = 0.0
    for index in range(steps):
        columns = slice(index * rows, (index + 1) * rows)
        value = sum(dot_tn(ref[:, columns], ref[:, index * rows :]) for ref in x_refs)
        t_ref[columns, index * rows :] = value
        for other in range(index + 1, steps):
            there = slice(other * rows, (other + 1) * rows)
            t_ref[there, columns] = t_ref[columns, there].T
        squares += jnp.sum(value[:, :rows] * eye_ref[...])
    inverse = 1.0 / (jnp.sqrt(jnp.full((1, 1), squares, jnp.float32)) + 1e-07)
    scale = jnp.sum(inverse)
    scale = scale * scale
    num_ref[a_at] = squares * scale * (1.0 / width)

    def chunks(index):
        for chunk in range(steps):
            yield chunk, slice(chunk * rows, (chunk + 1) * rows), jnp.where(index == chunk, 1.0, 0.0)

    def first_split(index):
        at = block(index)
        total = 0.0
        for _, cut, here in chunks(index):
            value = t_ref[at, cut] * scale - (here * num_ref[a_at]) * eye_ref[...]
            a_ref[at, cut] = value
            ah[at, cut], al[at, cut] = split_two(value)
            total += jnp.sum(value * value)
        num_ref[sum_at + index] = total

    each(first_split)

    for number in range(5):
        two = number < 2
        shift = num_ref[a_at]
        fix = newton_three * mean()
        num_ref[m_at] = newton_one + newton_two * shift + newton_three * shift * shift + fix
        slope = newton_two + 2.0 * newton_three * shift

        def make_n(index):
            at = block(index)
            total = 0.0
            for _, cut, here in chunks(index):
                value = newton_three * dot_low(ah[at, :], ah[:, cut])
                value += slope * a_ref[at, cut] - (here * fix) * eye_ref[...]
                nh[at, cut] = value.astype(jnp.bfloat16)
                total += jnp.sum(value * a_ref[at, cut])
            num_ref[sum_at + index] = total

        each(make_n)
        much = num_ref[m_at]
        keep_low = number < 4 and number >= 2
        if number == 0:

            def first_q(index):
                at = block(index)
                for _, cut, here in chunks(index):
                    value = nh[at, cut].astype(jnp.float32) + (here * much) * eye_ref[...]
                    q_ref[at, cut] = value
                    qh[at, cut] = value.astype(jnp.bfloat16)

            each(first_q)
        else:

            def next_q(index):
                at = block(index)
                high = qh[at, :]
                rest = ql[at, :] if number >= 3 else None
                for _, cut, _ in chunks(index):
                    value = much * q_ref[at, cut] + dot_low(high, nh[:, cut])
                    if number >= 3:
                        value += dot_low(rest, nh[:, cut])
                    t_ref[at, cut] = value
                for _, cut, _ in chunks(index):
                    value = t_ref[at, cut]
                    first, second = split_two(value)
                    qh[at, cut] = first
                    if number >= 2:
                        ql[at, cut] = second
                    if number < 4:
                        q_ref[at, cut] = value

            each(next_q)
        if number == 4:
            break
        fix_t = mean()
        num_ref[t_at] = shift * much + fix_t

        def make_t(index):
            at = block(index)
            total = 0.0
            for _, cut, here in chunks(index):
                value = dot_low(ah[at, :], nh[:, cut])
                if two:
                    value += dot_low(al[at, :], nh[:, cut])
                near = nh[at, cut].astype(jnp.float32)
                value += shift * near + much * a_ref[at, cut] - (here * fix_t) * eye_ref[...]
                t_ref[at, cut] = value
                if two:
                    th[at, cut], tl[at, cut] = split_two(value)
                else:
                    th[at, cut] = value.astype(jnp.bfloat16)
                total += jnp.sum(value * near)
            num_ref[sum_at + index] = total

        each(make_t)
        fix_a = mean()
        t_shift = num_ref[t_at]
        num_ref[a_at] = t_shift * much + fix_a

        def make_a(index):
            at = block(index)
            total = 0.0
            for _, cut, here in chunks(index):
                value = dot_low(nh[at, :], th[:, cut])
                if two:
                    value += dot_low(nh[at, :], tl[:, cut])
                near = nh[at, cut].astype(jnp.float32)
                value += t_shift * near + much * t_ref[at, cut] - (here * fix_a) * eye_ref[...]
                a_ref[at, cut] = value
                if number == 0:
                    ah[at, cut], al[at, cut] = split_two(value)
                else:
                    ah[at, cut] = value.astype(jnp.bfloat16)
                total += jnp.sum(value * value)
            num_ref[sum_at + index] = total

        each(make_a)

    half = out_ref.shape[0] // 2
    for side in range(2):
        mine = x_refs[side][0:half, :]
        out_ref[side * half : (side + 1) * half, :] = (
            (dot_low(mine, qh[...]) + dot_low(mine, ql[...])) * inverse
        ).astype(out_ref.dtype)


def newton(grads, mine_rows, rows=256, unroll=4):
    width = grads[0].shape[1]
    pieces = len(grads)
    low = pltpu.VMEM((width, width), jnp.bfloat16)
    full = pltpu.VMEM((width, width), jnp.float32)
    vmem = pl.BlockSpec(memory_space=pltpu.VMEM)
    return pl.pallas_call(
        functools.partial(newton_kernel, rows, unroll, pieces),
        out_shape=jax.ShapeDtypeStruct((mine_rows, width), jnp.bfloat16),
        in_specs=[vmem] * pieces,
        out_specs=vmem,
        scratch_shapes=[full] * 3
        + [pltpu.VMEM((rows, rows), jnp.float32)]
        + [low] * 7
        + [pltpu.SMEM((16,), jnp.float32)],
        compiler_params=vmem_params(60),
        cost_estimate=pl.CostEstimate(flops=60 * 10**9, bytes_accessed=20 * 10**6, transcendentals=0),
        name="newton",
    )(*grads)


def frame_sums_kernel(count, *refs):
    out_ref = refs[-1]
    ones, twos = refs[:count], refs[count : 2 * count]
    steps, _, frames, _ = ones[0].shape
    at = 0
    for clip in range(count):
        for step in range(steps):
            rows = slice(at, at + frames)
            for index in range(2):
                out_ref[rows, index * D : (index + 1) * D] = ones[clip][step, index]
            for index in range(4):
                out_ref[rows, (index + 2) * D : (index + 3) * D] = twos[clip][step, index]
            at += frames


def frame_sums(ones, twos):
    steps, _, frames, _ = ones[0].shape
    return pl.pallas_call(
        functools.partial(frame_sums_kernel, len(ones)),
        out_shape=jax.ShapeDtypeStruct((len(ones) * steps * frames, 6 * D), jnp.float32),
        in_specs=[pl.BlockSpec(memory_space=pltpu.VMEM)] * (2 * len(ones)),
        out_specs=pl.BlockSpec(memory_space=pltpu.VMEM),
        compiler_params=vmem_params(60),
        cost_estimate=pl.CostEstimate(flops=0, bytes_accessed=MIB, transcendentals=0),
        name="frame_sums",
    )(*ones, *twos)


def swap(slots):
    size = lax.axis_size("row")
    out = [slots[0]]
    for slot in range(1, size):
        out.append(lax.ppermute(slots[slot], "row", [(index, index ^ slot) for index in range(size)]))
    return out


def frame_swap(slots):
    size = lax.axis_size("frame")
    out = [slots[0]]
    for slot in range(1, size // 2):
        pairs = [(index, index ^ (2 * slot)) for index in range(size)]
        out.append(lax.ppermute(slots[slot], "frame", pairs))
    return out


def plane_steps(members):
    size = lax.axis_size("row")
    row_bits = size.bit_length() - 1
    groups = lax.axis_size("frame") // 2
    group_index = lax.axis_index("frame") >> 1
    height = max(item.shape[0] for item in members)
    slab = jnp.stack([jnp.pad(item, ((0, height - item.shape[0]), (0, 0))) for item in members])
    slots = [
        lax.dynamic_index_in_dim(slab, (group_index ^ slot) & 3, 0, keepdims=False) for slot in range(groups)
    ]
    hold = yield slots
    slots = frame_swap(slots)
    slots[0] = held(slots[0], *hold)
    mine = jnp.concatenate(slots, axis=0)
    cut = mine.shape[0] // 2
    grown = [mine[:cut], mine[cut:]]
    for step in range(row_bits):
        hold = yield grown
        for side in range(2):
            bit = step if side == 0 else row_bits - 1 - step
            pairs = [(index, index ^ (1 << bit)) for index in range(size)]
            came = lax.ppermute(grown[side], "row", pairs)
            grown[side] = jnp.concatenate([held(grown[side], *hold), came], axis=0)
    frame_size = lax.axis_size("frame")
    pairs = [(index, index ^ 1) for index in range(frame_size)]
    yield (*grown, *(lax.ppermute(item, "frame", pairs) for item in grown))


def per_device(
    tokens,
    cotangent,
    noise_levels,
    frame_times,
    step_count,
    qkv_master,
    qkv_momentum,
    out_master,
    out_momentum,
    up_master,
    up_momentum,
    down_master,
    down_momentum,
    ada_master,
    ada_first,
    ada_second,
    table_master,
    table_first,
    table_second,
    bias_master,
    bias_first,
    bias_second,
):
    low_type = jnp.bfloat16
    full_type = jnp.float32
    clip_count, frames, rows_dev, columns, model_width = tokens.shape
    seq_local = frames * rows_dev * columns
    row_devices = lax.axis_size("row")
    token_total = clip_count * seq_local
    frame_total = clip_count * frames
    shape_five = (clip_count, frames, rows_dev, columns, model_width)
    both = ("frame", "row")
    frame_devices = lax.axis_size("frame")
    device_total = frame_devices * row_devices
    device_index = lax.axis_index("frame") * row_devices + lax.axis_index("row")
    heights = (qkv_master.shape[1], out_master.shape[0], up_master.shape[1], down_master.shape[0])
    w_qkv = lax.all_gather(qkv_master.T.astype(low_type), both, axis=0, tiled=True)
    shards = jnp.concatenate([down_master, up_master.T, out_master], axis=0).astype(low_type)
    gathered = lax.all_gather(shards, both, axis=0)
    if heights[1] % 16 == 0:

        def from_slab(first, height):
            return gathered, pl.BlockSpec(
                (device_total, height, model_width),
                lambda *_: (0, first // height, 0),
                pipeline_mode=pl.Buffered(1),
            )

    else:

        def from_slab(first, height):
            part = gathered[:, first : first + height].reshape(-1, model_width // row_devices, model_width)
            return part, whole_spec(part)

    w_down = from_slab(0, heights[3])
    w_up = from_slab(heights[3], heights[2])
    w_out = from_slab(heights[3] + heights[2], heights[1])
    level_flat = noise_levels.reshape(frame_total)
    levels_all = lax.all_gather(level_flat, "frame", axis=0, tiled=True)
    frames_all = frame_devices * frame_total
    frames_each = frames_all // device_total
    level_rows = table_master.shape[0]
    my_levels = device_index * level_rows + jnp.arange(level_rows, dtype=jnp.int32)
    level_hot = levels_all[:, None] == my_levels[None, :]
    found = jnp.dot(
        level_hot.astype(low_type),
        lax.optimization_barrier(table_master.astype(low_type)),
        preferred_element_type=full_type,
    )

    def to_all(value):
        return lax.all_to_all(value, both, split_axis=0, concat_axis=0, tiled=True)

    def from_all(value):
        return to_all(jnp.broadcast_to(value[None], (device_total,) + value.shape))

    embedded_mine = jnp.sum(
        to_all(found.reshape(device_total, frames_each, model_width)), axis=0
    )
    embedded_all = from_all(embedded_mine).reshape(frames_all, model_width)
    cond_all = jax.nn.silu(embedded_all).astype(low_type)
    ada_low = lax.optimization_barrier(ada_master.astype(low_type))
    bias_low = lax.optimization_barrier(bias_master.astype(low_type))
    ada_width = ada_master.shape[1]
    mod_columns = jnp.dot(cond_all, ada_low, preferred_element_type=full_type) + bias_low.astype(full_type)
    mod_columns = mod_columns.reshape(frame_devices, 1, frame_total, ada_width)
    mod_columns = jnp.broadcast_to(
        mod_columns, (frame_devices, row_devices, frame_total, ada_width)
    ).reshape(device_total, frame_total, ada_width)
    modulation = jnp.moveaxis(to_all(mod_columns), 0, 1).reshape(frame_total, 6 * model_width)
    grid_shape = (clip_count, frames, rows_dev, columns)
    row_first = lax.axis_index("row") * rows_dev
    time_grid = jnp.broadcast_to(frame_times.astype(full_type)[:, :, None, None], grid_shape)
    row_grid = jnp.broadcast_to(
        (row_first + jnp.arange(rows_dev, dtype=jnp.int32)).astype(full_type)[None, None, :, None],
        grid_shape,
    )
    column_grid = jnp.broadcast_to(
        jnp.arange(columns, dtype=jnp.int32).astype(full_type)[None, None, None, :], grid_shape
    )
    angles = rotary_angles(time_grid, row_grid, column_grid).reshape(clip_count, seq_local, HD // 2)
    flat_angles = angles.reshape(token_total, HD // 2)
    pair_sign = jnp.tile(jnp.array([-1.0, 1.0], full_type), HD)
    cosine = jnp.tile(jnp.repeat(jnp.cos(flat_angles), 2, axis=1), (1, 2))
    sine = jnp.tile(jnp.repeat(jnp.sin(flat_angles), 2, axis=1), (1, 2)) * pair_sign
    tile_count = token_total // 256
    mod = modulation.reshape(tile_count, frame_total // tile_count, 6 * model_width)
    me = lax.axis_index("row").astype(jnp.int32).reshape(1)
    tokens_flat = tokens.reshape(clip_count, seq_local, model_width)
    cotangent_flat = cotangent.reshape(clip_count, seq_local, model_width)
    clips = range(clip_count)
    hidden_one, pieces = [], []
    for clip in clips:
        hidden, *slots = project(me, clip, tokens_flat, mod, cosine, sine, w_qkv, row_devices)
        hidden_one.append(hidden[0])
        pieces.append(swap(slots))
    attended, full, logs = [], [], []
    for clip in clips:
        slots, full_clip, log_clip = attend(pieces[clip])
        attended.append(swap(slots))
        full.append(full_clip)
        logs.append(log_clip)
    d_attended, middles = [], []
    for clip in clips:
        slots, others = middle(
            me, clip, tokens_flat, cotangent_flat, mod, w_out, w_up, w_down, attended[clip]
        )
        d_attended.append(swap(slots))
        middles.append(others)
    block_out = jnp.concatenate([item[0] for item in middles], axis=0).reshape(shape_five)
    att_low, hidden_two, activated, d_branch_two, d_up, d_branch_one, d_middle, two_sums = (
        [item[index] for item in middles] for index in range(1, 9)
    )
    early = scatter_steps(
        [[(activated, d_branch_two)], [(d_up, hidden_two), (att_low, d_branch_one)]], "early", True, []
    )

    def after(value, state):
        return [held(value[0], *state), *value[1:]]

    ready = next(early)
    d_pieces = []
    for clip in clips:
        if clip < clip_count - 1:
            slots = attend_back(pieces[clip], after(d_attended[clip], ready), full[clip], logs[clip])
            before = swap(slots)
            d_pieces.append(before)
            ready = [slots[0]]
            continue
        parts = []
        for pair in range(D // 128 // row_devices):
            slots = attend_back(pieces[clip], after(d_attended[clip], ready), full[clip], logs[clip], pair)
            parts += swap(slots)
            ready = [slots[0], *before[1:]]
        d_pieces.append(parts)
    state = []
    lasts = []
    for clip in clips:
        lasts.append(
            last(
                me, clip, tokens_flat, mod, cosine, sine, w_qkv, d_middle[clip],
                after(d_pieces[clip], state), row_devices,
            )
        )
        if clip < clip_count - 1:
            state = early.send([lasts[clip][2]])
    input_grad = jnp.concatenate([item[1] for item in lasts], axis=0).reshape(shape_five)
    one_sums = [item[2] for item in lasts]
    d_modulation = frame_sums(one_sums, two_sums)
    state = early.send([lasts[-1][2]])
    late = scatter_steps(
        [[([item[0] for item in lasts], hidden_one)]],
        "late",
        False,
        [d_modulation],
        state if isinstance(state, list) else (),
    )
    late_state = next(late)
    late_row = late.send([])
    early_sum = finished(early, early.send(late_row))
    state = late.send([])

    mod_parts = to_all(jnp.moveaxis(d_modulation.reshape(frame_total, device_total, ada_width), 1, 0))
    mod_parts = held(mod_parts, *late_row)
    mod_mine = (
        jnp.sum(mod_parts.reshape(frame_devices, row_devices, frame_total, ada_width), axis=1)
        .reshape(frames_all, ada_width)
        .astype(low_type)
    )
    g_ada = jnp.einsum("fd,fe->de", cond_all, mod_mine, preferred_element_type=full_type)
    g_bias = jnp.sum(mod_mine.astype(full_type), axis=0)
    d_cond_parts = jnp.einsum("fe,de->fd", mod_mine, ada_low, preferred_element_type=full_type)
    d_cond = to_all(d_cond_parts.reshape(device_total, frames_each, model_width))
    d_cond = jnp.sum(held(d_cond, *state) if isinstance(state, list) else d_cond, axis=0)
    g_qkv = finished(late, state)
    d_embedded_mine = jax.vjp(jax.nn.silu, embedded_mine)[1](d_cond)[0]
    d_embedded = from_all(d_embedded_mine).reshape(frames_all, model_width)
    g_table = jnp.dot(level_hot.astype(full_type).T, d_embedded, precision=highest)
    g_down = early_sum[: heights[3]]
    g_up = early_sum[heights[3] : heights[3] + heights[2]]
    g_out = early_sum[heights[3] + heights[2] :]
    muon_grads = (g_qkv, g_out, g_up, g_down)
    flipped = (True, False, True, False)

    def tall(value, member):
        return value.T if flipped[member] else value

    muon_moments = (qkv_momentum, out_momentum, up_momentum, down_momentum)
    muon_masters = (qkv_master, out_master, up_master, down_master)
    factors = (math.sqrt(3.0), 1.0, math.sqrt(FF / D), math.sqrt(FF / D))
    adam_local = jnp.sum(g_ada * g_ada) + jnp.sum(g_table * g_table) + jnp.sum(g_bias * g_bias)
    local_total = adam_local + sum((jnp.sum(item * item) for item in muon_grads))
    norm_value = jnp.sqrt(jnp.sum(from_all(jnp.full((1, 128), local_total))[:, 0, 0]))
    clip_factor = jnp.minimum(1.0, clip_limit / (norm_value + 1e-06))
    moments_new = []
    updates = []
    slot_rows = max(heights)
    for member in range(4):
        clipped = clip_factor * muon_grads[member]
        moment = momentum_decay * tall(muon_moments[member], member) + clipped
        update = (clipped + momentum_decay * moment).astype(low_type)
        moments_new.append(tall(moment, member))
        updates.append(update)
    row_steps = plane_steps(updates)
    update_rows = next(row_steps)
    while not isinstance(update_rows, tuple):
        update_rows = row_steps.send([])
    groups = frame_devices // 2
    group_index = lax.axis_index("frame") >> 1
    ortho_rows = newton(update_rows, groups * slot_rows).reshape(groups, slot_rows, model_width)
    ortho_slots = jnp.stack(frame_swap([ortho_rows[slot] for slot in range(groups)]))
    ortho_mine = [
        lax.dynamic_index_in_dim(ortho_slots, (group_index & 3) ^ member, 0, keepdims=False)
        for member in range(4)
    ]
    blocks = [tall(ortho_mine[member][: heights[member]].astype(full_type), member) for member in range(4)]
    masters_new = []
    for member in range(4):
        ortho = blocks[member]
        masters_new.append(
            muon_masters[member] * (1.0 - muon_rate * weight_decay)
            - muon_rate * factors[member] * ortho
        )
    step_value = step_count.astype(full_type)[0]
    ada_first_new, ada_second_new, ada_master_new = adam_update(
        g_ada, ada_first, ada_second, ada_master, 0.03, clip_factor, step_value
    )
    table_clipped = clip_factor * g_table
    table_first_new, table_second_new, table_master_new = adam_update(
        g_table, table_first, table_second, table_master, 0.5, clip_factor, step_value
    )
    bias_first_new, bias_second_new, bias_master_new = adam_update(
        g_bias, bias_first, bias_second, bias_master, 0.5, clip_factor, step_value
    )
    return (
        block_out,
        input_grad,
        norm_value.reshape(1),
        moments_new[0],
        masters_new[0],
        moments_new[1],
        masters_new[1],
        moments_new[2],
        masters_new[2],
        moments_new[3],
        masters_new[3],
        ada_first_new,
        ada_second_new,
        ada_master_new,
        table_first_new,
        table_clipped,
        table_master_new,
        bias_first_new,
        bias_second_new,
        bias_master_new,
    )


def solution(mesh):
    return jax.shard_map(
        per_device,
        mesh=mesh,
        in_specs=(
            P("frame", None, "row", None, None),
            P("frame", None, "row", None, None),
            P("frame", None),
            P("frame", None),
            P(),
            P(None, ("frame", "row")),
            P(None, ("frame", "row")),
            P(("frame", "row"), None),
            P(("frame", "row"), None),
            P(None, ("frame", "row")),
            P(None, ("frame", "row")),
            P(("frame", "row"), None),
            P(("frame", "row"), None),
            P(None, ("frame", "row")),
            P(None, ("frame", "row")),
            P(None, ("frame", "row")),
            P(("frame", "row"), None),
            P(("frame", "row"), None),
            P(("frame", "row"), None),
            P(("frame", "row")),
            P(("frame", "row")),
            P(("frame", "row")),
        ),
        out_specs=(
            P("frame", None, "row", None, None),
            P("frame", None, "row", None, None),
            P(),
            P(None, ("frame", "row")),
            P(None, ("frame", "row")),
            P(("frame", "row"), None),
            P(("frame", "row"), None),
            P(None, ("frame", "row")),
            P(None, ("frame", "row")),
            P(("frame", "row"), None),
            P(("frame", "row"), None),
            P(None, ("frame", "row")),
            P(None, ("frame", "row")),
            P(None, ("frame", "row")),
            P(("frame", "row"), None),
            P(("frame", "row"), None),
            P(("frame", "row"), None),
            P(("frame", "row")),
            P(("frame", "row")),
            P(("frame", "row")),
        ),
        check_vma=False,
    )
```

```python
import functools
import math

import jax
import jax.numpy as jnp
from jax import lax
from jax.experimental import pallas as pl
from jax.experimental.pallas import tpu as pltpu
from jax.sharding import PartitionSpec as P

D = 1024
HEADS = 16
HD = 64
FF = 4096


highest = lax.Precision.HIGHEST
newton_one = 3.4445
newton_two = -4.775
newton_three = 2.0315
momentum_decay = 0.95
muon_rate = 1.5
weight_decay = 0.01
beta_first = 0.9
beta_second = 0.95
adam_floor = 1e-08
norm_floor = 1e-06
clip_limit = 1.0
rotary_base = 10000.0


def rotary_angles(time_grid, row_grid, column_grid):
    quarter_pairs = HD // 4
    eighth_pairs = HD // 8
    time_rates = rotary_base ** (-jnp.arange(quarter_pairs, dtype=jnp.float32) / quarter_pairs)
    space_rates = rotary_base ** (-jnp.arange(eighth_pairs, dtype=jnp.float32) / eighth_pairs)
    return jnp.concatenate(
        [
            time_grid[..., None] * time_rates,
            row_grid[..., None] * space_rates,
            column_grid[..., None] * space_rates,
        ],
        axis=-1,
    )


def adam_update(grad_item, first, second, master, rate, clip_factor, step_value):
    clipped = clip_factor * grad_item
    first_new = beta_first * first + (1.0 - beta_first) * clipped
    second_new = beta_second * second + (1.0 - beta_second) * clipped * clipped
    first_fix = 1.0 - beta_first**step_value
    second_fix = 1.0 - beta_second**step_value
    master_new = master * (1.0 - rate * weight_decay) - rate * (first_new / first_fix) / (
        jnp.sqrt(second_new / second_fix) + adam_floor
    )
    return (first_new, second_new, master_new)


def halves(value, dim, axis, bit):
    mine = (lax.axis_index(axis) >> bit) & 1
    keep = lax.dynamic_index_in_dim(value, mine, dim, keepdims=False)
    send = lax.dynamic_index_in_dim(value, 1 - mine, dim, keepdims=False)
    return keep, send.astype(jnp.bfloat16)


def joined(keep, send, axis, bit):
    size = lax.axis_size(axis)
    came = lax.ppermute(send, axis, [(index, index ^ (1 << bit)) for index in range(size)])
    return keep + came.astype(jnp.float32)


def held(value, *others):
    if not others:
        return value
    return lax.optimization_barrier((value, *others))[0]


def scatter_steps(groups, name, by_frame, ready, keep_ready=()):
    frame_bits = lax.axis_size("frame").bit_length() - 1
    row_bits = lax.axis_size("row").bit_length() - 1
    row, frame = lax.axis_index("row"), lax.axis_index("frame")
    numbers = jnp.stack([frame & 1, row & 1, row >> (row_bits - 1), (frame >> 1) & 1]).astype(jnp.int32)
    numbers = held(numbers, *ready)
    size = lax.axis_size("frame")
    came = []
    for at, group in enumerate(groups):
        send = send_sums(numbers, group, f"{name}_send_{at}")
        came.append(lax.ppermute(send, "frame", [(index, index ^ 1) for index in range(size)]))
        numbers = held(numbers, send)
    numbers = held(numbers, *keep_ready)
    keep, send = keep_sums(numbers, groups, came, name + "_keep", by_frame)
    hold = yield send
    names = [("frame", bit) for bit in reversed(range(1, frame_bits))]
    names += [("row", bit) for bit in reversed(range(row_bits))]
    rest = [("frame", bit) for bit in range(1, frame_bits)]
    side_names = []
    if by_frame:
        names.remove(("frame", 1))
        rest.remove(("frame", 1))
        value = joined(held(keep[0], *hold), send[0], "frame", 1)
        value = value.reshape((2,) * len(names) + value.shape[2:])
        width = value.shape[-1] // 2
        keep, send = [], []
        for side in range(2):
            bit = 0 if side == 0 else row_bits - 1
            side_names.append([item for item in names if item != ("row", bit)])
            part = value[..., side * width : (side + 1) * width]
            kept, sent = halves(part, names.index(("row", bit)), "row", bit)
            keep.append(kept)
            send.append(sent)
        hold = yield send
    else:
        for side in range(2):
            bit = 0 if side == 0 else row_bits - 1
            side_names.append([item for item in names if item != ("row", bit)])
            shape = (2,) * (len(names) - 1) + keep[side].shape[2:]
            keep[side] = keep[side].reshape(shape)
            send[side] = send[side].reshape(shape)
    for step in range(row_bits):
        parts = []
        for side in range(2):
            bit = step if side == 0 else row_bits - 1 - step
            parts.append(joined(held(keep[side], *hold), send[side], "row", bit))
        if step == row_bits - 1:
            break
        for side in range(2):
            bit = step + 1 if side == 0 else row_bits - 2 - step
            dim = side_names[side].index(("row", bit))
            side_names[side].pop(dim)
            keep[side], send[side] = halves(parts[side], dim, "row", bit)
        hold = yield send
    value = jnp.concatenate(parts, axis=-1)
    value = value.reshape((-1,) + value.shape[-2:])
    count = value.shape[0]
    low = rest[0][1] if rest else 0
    mine = frame >> low
    keep = lax.dynamic_index_in_dim(value, mine & (count - 1), 0, keepdims=False)
    sends = [
        lax.dynamic_index_in_dim(value, (mine ^ slot) & (count - 1), 0, keepdims=False).astype(jnp.bfloat16)
        for slot in range(1, count)
    ]
    hold = yield sends
    keep = held(keep, *hold)
    for slot, send in enumerate(sends, 1):
        pairs = [(index, index ^ (slot << low)) for index in range(size)]
        keep = keep + lax.ppermute(send, "frame", pairs).astype(jnp.float32)
    yield keep


def finished(steps, state):
    while isinstance(state, list):
        state = steps.send([])
    return state


def split_two(value):
    high = value.astype(jnp.bfloat16)
    return high, (value - high.astype(jnp.float32)).astype(jnp.bfloat16)


def dot_low(left, right):
    return lax.dot_general(left, right, (((1,), (0,)), ((), ())), preferred_element_type=jnp.float32)


def dot_nt(left, right):
    return lax.dot_general(left, right, (((1,), (1,)), ((), ())), preferred_element_type=jnp.float32)


def dot_tn(left, right):
    return lax.dot_general(left, right, (((0,), (0,)), ((), ())), preferred_element_type=jnp.float32)


MIB = 1024 * 1024


def vmem_params(mib, semantics=None):
    return pltpu.CompilerParams(vmem_limit_bytes=mib * MIB, dimension_semantics=semantics)


def whole_spec(array):
    zeros = (0,) * array.ndim
    return pl.BlockSpec(array.shape, lambda *_: zeros, pipeline_mode=pl.Buffered(1))


def turned(value, cosine, sine):
    even = lax.broadcasted_iota(jnp.int32, value.shape, 1) % 2 == 0
    width = value.shape[1]
    swapped = jnp.where(even, pltpu.roll(value, width - 1, 1), pltpu.roll(value, 1, 1))
    return value * cosine + swapped * sine


def framed(value, frames):
    rows, width = value.shape
    return value.reshape(frames, rows // frames, width)


def norm_parts(value):
    mean = jnp.mean(value, axis=-1, keepdims=True)
    centered = value - mean
    root = lax.rsqrt(jnp.mean(centered * centered, axis=-1, keepdims=True) + norm_floor)
    return centered * root, root


def project_kernel(slots, me_ref, x_ref, mod_ref, cos_ref, sin_ref, w_ref, hid_ref, *out_refs):
    frames = mod_ref.shape[1]
    group = D // slots
    normed, _ = norm_parts(x_ref[0].astype(jnp.float32))
    normed = framed(normed, frames)
    shift = mod_ref[0, :, 0:D][:, None, :]
    scaling = mod_ref[0, :, D : 2 * D][:, None, :]
    hidden = (normed * (1.0 + scaling) + shift).reshape(x_ref.shape[1], D).astype(jnp.bfloat16)
    hid_ref[0] = hidden
    cosine = cos_ref[...]
    sine = sin_ref[...]
    me = me_ref[0]
    for slot in range(slots):
        peer = me ^ slot
        for part in range(3):
            rows = pl.ds(pl.multiple_of(part * D + peer * group, group), group)
            value = dot_nt(hidden, w_ref[rows, :])
            if part == 2:
                out_refs[slot][part] = value.astype(jnp.bfloat16)
                continue
            for first in range(0, group, 128):
                piece = turned(value[:, first : first + 128], cosine, sine)
                if part == 0:
                    piece = piece * (1.0 / math.sqrt(HD))
                out_refs[slot][part, :, first : first + 128] = piece.astype(jnp.bfloat16)


def project(me, clip, tokens, mod, cosine, sine, w_qkv, slots):
    count, tall_rows, _ = tokens.shape
    tile = 256
    steps = tall_rows // tile
    group = D // slots
    out_shape = [jax.ShapeDtypeStruct((1, tall_rows, D), jnp.bfloat16)]
    out_shape += [jax.ShapeDtypeStruct((3, tall_rows, group), jnp.bfloat16)] * slots
    return pl.pallas_call(
        functools.partial(project_kernel, slots),
        grid=(steps,),
        in_specs=[
            pl.BlockSpec(memory_space=pltpu.SMEM),
            pl.BlockSpec((1, tile, D), lambda i: (clip, i, 0)),
            pl.BlockSpec((1, mod.shape[1], 6 * D), lambda i: (clip * steps + i, 0, 0)),
            pl.BlockSpec((tile, 128), lambda i: (clip * steps + i, 0)),
            pl.BlockSpec((tile, 128), lambda i: (clip * steps + i, 0)),
            whole_spec(w_qkv),
        ],
        out_specs=[pl.BlockSpec((1, tile, D), lambda i: (0, i, 0))]
        + [pl.BlockSpec((3, tile, group), lambda i: (0, i, 0))] * slots,
        out_shape=out_shape,
        compiler_params=vmem_params(60),
        cost_estimate=pl.CostEstimate(
            flops=6 * tall_rows * D * D, bytes_accessed=10 * MIB, transcendentals=0
        ),
        name="project",
    )(me, tokens, mod, cosine, sine, w_qkv)


def head_mask(shape, head, axis):
    return lax.broadcasted_iota(jnp.int32, shape, axis) // HD == head


def attend_kernel(slots, tile, *refs):
    ins, outs = refs[:slots], refs[slots : 2 * slots]
    full_ref, log_ref, qs, ks, vs = refs[2 * slots :]
    length = ins[0].shape[1]
    for slot in range(slots):
        rows = slice(slot * length, (slot + 1) * length)
        qs[rows, :] = ins[slot][0]
        ks[rows, :] = ins[slot][1]
        vs[rows, :] = ins[slot][2]

    def one(index, carry):
        rows = pl.ds(pl.multiple_of(index * tile, tile), tile)
        query = qs[rows, :]
        first = head_mask((tile, 128), 0, 1)
        parts = []
        logs = []
        for head in range(2):
            masked = jnp.where(first if head == 0 else ~first, query, jnp.zeros_like(query))
            scores = dot_nt(masked, ks[...])
            top = jnp.max(scores, axis=-1, keepdims=True)
            raised = jnp.exp(scores - top)
            total = jnp.sum(raised, axis=-1, keepdims=True)
            parts.append(dot_low(raised.astype(jnp.bfloat16), vs[...]) * (1.0 / total))
            logs.append(top + jnp.log(total))
        full_ref[rows, :] = jnp.where(first, parts[0], parts[1])
        log_ref[rows, :] = jnp.where(first, logs[0], logs[1])
        return carry

    lax.fori_loop(0, slots * length // tile, one, 0)
    for slot in range(slots):
        rows = slice(slot * length, (slot + 1) * length)
        outs[slot][...] = full_ref[rows, :].astype(jnp.bfloat16)


def attend(pieces):
    slots = len(pieces)
    _, length, group = pieces[0].shape
    total = slots * length
    scratch = pltpu.VMEM((total, 128), jnp.bfloat16)
    outs = pl.pallas_call(
        functools.partial(attend_kernel, slots, 256),
        grid=(group // 128,),
        in_specs=[pl.BlockSpec((3, length, 128), lambda i: (0, 0, i))] * slots,
        out_specs=[pl.BlockSpec((length, 128), lambda i: (0, i))] * slots
        + [pl.BlockSpec((total, 128), lambda i: (0, i))] * 2,
        out_shape=[jax.ShapeDtypeStruct((length, group), jnp.bfloat16)] * slots
        + [jax.ShapeDtypeStruct((total, group), jnp.float32)] * 2,
        scratch_shapes=[scratch] * 3,
        compiler_params=vmem_params(60),
        cost_estimate=pl.CostEstimate(
            flops=16 * total * total * group, bytes_accessed=8 * MIB, transcendentals=total * total * 4
        ),
        name="attend",
    )(*pieces)
    return outs[:slots], outs[slots], outs[slots + 1]


def attend_back_kernel(slots, tile, *refs):
    ins, grads = refs[:slots], refs[slots : 2 * slots]
    full_ref, log_ref = refs[2 * slots : 2 * slots + 2]
    outs = refs[2 * slots + 2 : 3 * slots + 2]
    qs, ks, vs, gs, q_turned, g_turned, dq, dk, dv = refs[3 * slots + 2 :]
    length = ins[0].shape[1]
    total = slots * length
    for slot in range(slots):
        rows = slice(slot * length, (slot + 1) * length)
        qs[rows, :] = ins[slot][0]
        ks[rows, :] = ins[slot][1]
        vs[rows, :] = ins[slot][2]
        gs[rows, :] = grads[slot][...]
        q_turned[:, rows] = ins[slot][0].T
        g_turned[:, rows] = grads[slot][...].T
    dk[...] = jnp.zeros_like(dk)
    dv[...] = jnp.zeros_like(dv)

    def one(index, carry):
        rows = pl.ds(pl.multiple_of(index * tile, tile), tile)
        first = head_mask((tile, 128), 0, 1)
        upper = head_mask((128, tile), 0, 0)
        query, grad = qs[rows, :], gs[rows, :]
        query_t, grad_t = q_turned[:, rows], g_turned[:, rows]
        product = grad.astype(jnp.float32) * full_ref[rows, :]
        masks = (first, ~first)
        masks_t = (upper, ~upper)
        zero = jnp.zeros_like(query)
        zero_t = jnp.zeros_like(query_t)
        q_low = [jnp.where(mask, query, zero) for mask in masks]
        g_low = [jnp.where(mask, grad, zero) for mask in masks]
        qt_low = [jnp.where(mask, query_t, zero_t) for mask in masks_t]
        gt_low = [jnp.where(mask, grad_t, zero_t) for mask in masks_t]
        inner = [jnp.sum(jnp.where(mask, product, 0.0), axis=-1, keepdims=True) for mask in masks]
        logs = [log_ref[rows, 0:1], log_ref[rows, HD : HD + 1]]

        def inside(k_index, sums):
            at = pl.ds(pl.multiple_of(k_index * tile, tile), tile)
            key, value = ks[at, :], vs[at, :]
            out = []
            for head in range(2):
                probs = jnp.exp(dot_nt(q_low[head], key) - logs[head])
                d_probs = dot_nt(g_low[head], value)
                d_scores = (probs * (d_probs - inner[head])).astype(jnp.bfloat16)
                dv[:, at] += dot_low(gt_low[head], probs.astype(jnp.bfloat16))
                dk[:, at] += dot_low(qt_low[head], d_scores)
                out.append(sums[head] + dot_low(d_scores, key))
            return tuple(out)

        start = jnp.zeros((tile, 128), jnp.float32)
        sums = lax.fori_loop(0, total // tile, inside, (start, start))
        dq[rows, :] = (jnp.where(first, sums[0], sums[1]) * (1.0 / math.sqrt(HD))).astype(jnp.bfloat16)
        return carry

    lax.fori_loop(0, total // tile, one, 0)
    for slot in range(slots):
        rows = slice(slot * length, (slot + 1) * length)
        outs[slot][0] = dq[rows, :]
        outs[slot][1] = dk[:, rows].T.astype(jnp.bfloat16)
        outs[slot][2] = dv[:, rows].T.astype(jnp.bfloat16)


def attend_back(pieces, grads, full, logs, pair=None):
    slots = len(pieces)
    _, length, group = pieces[0].shape
    first = 0 if pair is None else pair
    count = group // 128 if pair is None else 1
    group = 128 * count
    total = slots * length
    low = pltpu.VMEM((total, 128), jnp.bfloat16)
    low_t = pltpu.VMEM((128, total), jnp.bfloat16)
    full_t = pltpu.VMEM((128, total), jnp.float32)
    return pl.pallas_call(
        functools.partial(attend_back_kernel, slots, 512),
        grid=(count,),
        in_specs=[pl.BlockSpec((3, length, 128), lambda i: (0, 0, i + first))] * slots
        + [pl.BlockSpec((length, 128), lambda i: (0, i + first))] * slots
        + [pl.BlockSpec((total, 128), lambda i: (0, i + first))] * 2,
        out_specs=[pl.BlockSpec((3, length, 128), lambda i: (0, 0, i))] * slots,
        out_shape=[jax.ShapeDtypeStruct((3, length, group), jnp.bfloat16)] * slots,
        scratch_shapes=[low] * 4 + [low_t] * 2 + [low] + [full_t] * 2,
        compiler_params=vmem_params(60),
        cost_estimate=pl.CostEstimate(
            flops=40 * total * total * group, bytes_accessed=12 * MIB, transcendentals=total * total * 4
        ),
        name="attend_back",
    )(*pieces, *grads, full, logs)


def part_of(ref, index, size):
    count = size // ref.shape[1]
    return ref[pl.ds(index * count, count)].reshape(size, ref.shape[2])


def middle_kernel(slots, me_ref, x_ref, cot_ref, mod_ref, wo_ref, wu_ref, wd_ref, *refs):
    att_refs = refs[:slots]
    datt_refs = refs[slots : 2 * slots]
    (
        out_ref,
        att_ref,
        h2_ref,
        act_ref,
        db2_ref,
        dup_ref,
        db1_ref,
        dmid_ref,
        sums_ref,
        slope,
    ) = refs[2 * slots :]
    frames = mod_ref.shape[1]
    rows = x_ref.shape[1]
    group = D // slots
    me = me_ref[0]

    def mod(index):
        return mod_ref[0, :, index * D : (index + 1) * D][:, None, :]

    def spread(value, index, plus=0.0):
        return (framed(value, frames) * (mod(index) + plus)).reshape(rows, D)

    def frame_sum(value):
        return jnp.sum(framed(value, frames), axis=1)

    branch = jnp.zeros((rows, D), jnp.float32)
    for slot in range(slots):
        at = pl.ds(pl.multiple_of((me ^ slot) * group, group), group)
        piece = att_refs[slot][...]
        att_ref[:, at] = piece
        branch += dot_low(piece, part_of(wo_ref, me ^ slot, group))
    middle = x_ref[0].astype(jnp.float32) + spread(branch, 2)
    normed, root = norm_parts(middle)
    hidden = (framed(spread(normed, 4, 1.0), frames) + mod(3)).reshape(rows, D).astype(jnp.bfloat16)
    h2_ref[...] = hidden
    wide = 1024
    curve = math.sqrt(2.0 / math.pi)
    branch_two = jnp.zeros((rows, D), jnp.float32)
    for first in range(0, FF, wide):
        cut = slice(first, first + wide)
        up = dot_nt(hidden, part_of(wu_ref, first // wide, wide))
        square = up * up
        bent = jnp.tanh(curve * up * (1.0 + 0.044715 * square))
        half = 0.5 * (1.0 + bent)
        active = (up * half).astype(jnp.bfloat16)
        slope[:, cut] = half + 0.5 * up * (1.0 - bent * bent) * (curve * (1.0 + 3 * 0.044715 * square))
        act_ref[:, cut] = active
        branch_two += dot_low(active, part_of(wd_ref, first // wide, wide))
    cot = cot_ref[0].astype(jnp.float32)
    out_ref[0] = (middle + spread(branch_two, 5)).astype(jnp.bfloat16)
    sums_ref[0, 3] = frame_sum(cot * branch_two)
    d_branch_two = spread(cot, 5).astype(jnp.bfloat16)
    db2_ref[...] = d_branch_two
    d_hidden = jnp.zeros((rows, D), jnp.float32)
    for first in range(0, FF, wide):
        cut = slice(first, first + wide)
        d_up = (dot_nt(d_branch_two, part_of(wd_ref, first // wide, wide)) * slope[:, cut]).astype(jnp.bfloat16)
        dup_ref[:, cut] = d_up
        d_hidden += dot_low(d_up, part_of(wu_ref, first // wide, wide))
    sums_ref[0, 1] = frame_sum(d_hidden)
    sums_ref[0, 2] = frame_sum(d_hidden * normed)
    inner = spread(d_hidden, 4, 1.0)
    d_middle = cot + root * (
        inner
        - jnp.mean(inner, axis=-1, keepdims=True)
        - normed * jnp.mean(inner * normed, axis=-1, keepdims=True)
    )
    dmid_ref[...] = d_middle
    sums_ref[0, 0] = frame_sum(d_middle * branch)
    d_branch = spread(d_middle, 2).astype(jnp.bfloat16)
    db1_ref[...] = d_branch
    for slot in range(slots):
        datt_refs[slot][...] = dot_nt(d_branch, part_of(wo_ref, me ^ slot, group)).astype(jnp.bfloat16)


def middle(me, clip, tokens, cotangent, mod, w_out, w_up, w_down, attended):
    slots = len(attended)
    count, length, _ = tokens.shape
    tile = 256
    steps = length // tile
    group = D // slots
    frames = mod.shape[1]
    low = jnp.bfloat16

    def flat(width, kind=low):
        return jax.ShapeDtypeStruct((length, width), kind)

    def flat_spec(width):
        return pl.BlockSpec((tile, width), lambda i: (i, 0))

    outs = pl.pallas_call(
        functools.partial(middle_kernel, slots),
        grid=(steps,),
        in_specs=[
            pl.BlockSpec(memory_space=pltpu.SMEM),
            pl.BlockSpec((1, tile, D), lambda i: (clip, i, 0)),
            pl.BlockSpec((1, tile, D), lambda i: (clip, i, 0)),
            pl.BlockSpec((1, frames, 6 * D), lambda i: (clip * steps + i, 0, 0)),
            *(item[1] for item in (w_out, w_up, w_down)),
        ]
        + [flat_spec(group)] * slots,
        out_specs=[flat_spec(group)] * slots
        + [pl.BlockSpec((1, tile, D), lambda i: (0, i, 0))]
        + [flat_spec(width) for width in (D, D, FF, D, FF, D, D)]
        + [pl.BlockSpec((1, 4, frames, D), lambda i: (i, 0, 0, 0))],
        out_shape=[flat(group)] * slots
        + [jax.ShapeDtypeStruct((1, length, D), low)]
        + [flat(D), flat(D), flat(FF), flat(D), flat(FF), flat(D), flat(D, jnp.float32)]
        + [jax.ShapeDtypeStruct((steps, 4, frames, D), jnp.float32)],
        scratch_shapes=[pltpu.VMEM((tile, FF), jnp.float32)],
        compiler_params=vmem_params(60),
        cost_estimate=pl.CostEstimate(
            flops=2 * length * D * (2 * D + 4 * FF), bytes_accessed=40 * MIB, transcendentals=length * FF
        ),
        name="middle",
    )(me, tokens, cotangent, mod, *(item[0] for item in (w_out, w_up, w_down)), *attended)
    return outs[:slots], outs[slots:]


def last_kernel(slots, me_ref, x_ref, mod_ref, cos_ref, sin_ref, w_ref, dmid_ref, *refs):
    pieces = refs[:-3]
    dproj_ref, grad_ref, sums_ref = refs[-3:]
    frames = mod_ref.shape[1]
    rows = x_ref.shape[1]
    group = D // slots
    pairs = len(pieces) // slots
    narrow = group // pairs
    me = me_ref[0]
    cosine = cos_ref[...]
    sine = -sin_ref[...]
    d_hidden = jnp.zeros((rows, D), jnp.float32)
    for slot in range(slots):
        peer = me ^ slot
        for part in range(3):
            base = pl.multiple_of(part * D + peer * group, group)
            if part == 2:
                value = jnp.concatenate([pieces[pair * slots + slot][part] for pair in range(pairs)], axis=1)
            else:
                value = jnp.concatenate(
                    [
                        turned(
                            pieces[at // narrow * slots + slot][
                                part, :, at % narrow : at % narrow + 128
                            ].astype(jnp.float32),
                            cosine,
                            sine,
                        )
                        for at in range(0, group, 128)
                    ],
                    axis=1,
                ).astype(jnp.bfloat16)
            dproj_ref[:, pl.ds(base, group)] = value
            d_hidden += dot_low(value, w_ref[pl.ds(base, group), :])
    normed, root = norm_parts(x_ref[0].astype(jnp.float32))
    scaling = mod_ref[0, :, D : 2 * D][:, None, :]
    sums_ref[0, 0] = jnp.sum(framed(d_hidden, frames), axis=1)
    sums_ref[0, 1] = jnp.sum(framed(d_hidden * normed, frames), axis=1)
    inner = (framed(d_hidden, frames) * (1.0 + scaling)).reshape(rows, D)
    grad_ref[0] = dmid_ref[...] + root * (
        inner
        - jnp.mean(inner, axis=-1, keepdims=True)
        - normed * jnp.mean(inner * normed, axis=-1, keepdims=True)
    )


def last(me, clip, tokens, mod, cosine, sine, w_qkv, d_middle, pieces, slots):
    count, length, _ = tokens.shape
    tile = 256
    steps = length // tile
    narrow = pieces[0].shape[2]
    frames = mod.shape[1]
    return pl.pallas_call(
        functools.partial(last_kernel, slots),
        grid=(steps,),
        in_specs=[
            pl.BlockSpec(memory_space=pltpu.SMEM),
            pl.BlockSpec((1, tile, D), lambda i: (clip, i, 0)),
            pl.BlockSpec((1, frames, 6 * D), lambda i: (clip * steps + i, 0, 0)),
            pl.BlockSpec((tile, 128), lambda i: (clip * steps + i, 0)),
            pl.BlockSpec((tile, 128), lambda i: (clip * steps + i, 0)),
            whole_spec(w_qkv),
            pl.BlockSpec((tile, D), lambda i: (i, 0)),
        ]
        + [pl.BlockSpec((3, tile, narrow), lambda i: (0, i, 0))] * len(pieces),
        out_specs=[
            pl.BlockSpec((tile, 3 * D), lambda i: (i, 0)),
            pl.BlockSpec((1, tile, D), lambda i: (0, i, 0)),
            pl.BlockSpec((1, 2, frames, D), lambda i: (i, 0, 0, 0)),
        ],
        out_shape=[
            jax.ShapeDtypeStruct((length, 3 * D), jnp.bfloat16),
            jax.ShapeDtypeStruct((1, length, D), jnp.float32),
            jax.ShapeDtypeStruct((steps, 2, frames, D), jnp.float32),
        ],
        compiler_params=vmem_params(60),
        cost_estimate=pl.CostEstimate(
            flops=6 * length * D * D, bytes_accessed=20 * MIB, transcendentals=0
        ),
        name="last",
    )(me, tokens, mod, cosine, sine, w_qkv, d_middle, *pieces)


def member_value(refs, member, doubled, parity):
    left = refs[4 * member : 4 * member + 2]
    right = refs[4 * member + 2 : 4 * member + 4]
    value = dot_tn(left[0][...], right[0][...]) + dot_tn(left[1][...], right[1][...])
    if doubled:
        half = value.shape[0] // 2
        value = jnp.where(parity == 0, value[:half], value[half:])
    return value


def send_kernel(doubled, number_ref, *refs):
    out_ref = refs[-1]
    rows = out_ref.shape[1]
    first = 0
    for member in range(len(doubled)):
        value = member_value(refs, member, doubled[member], 1 - number_ref[0])
        height = value.shape[0] // rows
        out_ref[0, :, first : first + height, :] = value.reshape(rows, height, D).astype(out_ref.dtype)
        first += height


def keep_kernel(doubled, counts, number_ref, *refs):
    members = len(doubled)
    came_refs = refs[4 * members : 4 * members + len(counts)]
    keep_refs, send_refs = refs[-4:-2], refs[-2:]
    half_rows = keep_refs[0].shape[1]
    width = D // 2
    first = 0
    member = 0
    for came_ref, count in zip(came_refs, counts):
        inside = 0
        for _ in range(count):
            value = member_value(refs, member, doubled[member], number_ref[0])
            height = value.shape[0] // (2 * half_rows)
            rows = slice(first, first + height)
            parts = [
                value[row * height : (row + 1) * height]
                + came_ref[0, row, inside : inside + height, :].astype(jnp.float32)
                for row in range(2 * half_rows)
            ]
            for place in range(half_rows):
                for side in range(2):
                    cut = slice(side * width, (side + 1) * width)
                    low = 2 * place if side == 0 else place
                    high = low + (1 if side == 0 else half_rows)
                    upper = number_ref[1 + side] == 1
                    zero, one = parts[low][:, cut], parts[high][:, cut]
                    keep_refs[side][0, place, rows, :] = jnp.where(upper, one, zero)
                    send_refs[side][0, place, rows, :] = jnp.where(upper, zero, one).astype(jnp.bfloat16)
            first += height
            inside += height
            member += 1


def keep_frame_kernel(doubled, counts, number_ref, *refs):
    members = len(doubled)
    came_refs = refs[4 * members : 4 * members + len(counts)]
    keep_ref, send_ref = refs[-2:]
    rows = keep_ref.shape[1]
    kept = lax.rem(pl.program_id(0), 2) == number_ref[3]
    first = 0
    member = 0
    for came_ref, count in zip(came_refs, counts):
        inside = 0
        for _ in range(count):
            value = member_value(refs, member, doubled[member], number_ref[0])
            height = value.shape[0] // rows
            value = value.reshape(rows, height, D)
            value += came_ref[0, :, inside : inside + height, :].astype(jnp.float32)
            at = slice(first, first + height)

            @pl.when(kept)
            def _(value=value, at=at):
                keep_ref[0, :, at, :] = value

            @pl.when(jnp.logical_not(kept))
            def _(value=value, at=at):
                send_ref[0, :, at, :] = value.astype(jnp.bfloat16)

            first += height
            inside += height
            member += 1


def weight_specs(pairs, other):
    frame_devices = lax.axis_size("frame")
    specs, operands, doubled = [], [], []
    height = 0
    for left, right in pairs:
        width = left[0].shape[1] // frame_devices
        height += width // lax.axis_size("row")
        doubled.append(width % 128 != 0)
        if doubled[-1]:
            spec = pl.BlockSpec((left[0].shape[0], 2 * width), lambda i, s: (0, i))
        elif other:
            spec = pl.BlockSpec((left[0].shape[0], width), lambda i, s: (0, 2 * i + 1 - s[0]))
        else:
            spec = pl.BlockSpec((left[0].shape[0], width), lambda i, s: (0, 2 * i + s[0]))
        specs += [spec] * 2
        specs += [pl.BlockSpec(right[0].shape, lambda i, s: (0, 0))] * 2
        operands += [*left, *right]
    flops = sum(4 * left[0].shape[0] * left[0].shape[1] * D // 2 for left, _ in pairs)
    return specs, operands, tuple(doubled), height, flops


def send_sums(numbers, pairs, name):
    specs, operands, doubled, height, flops = weight_specs(pairs, True)
    frames, rows = lax.axis_size("frame") // 2, lax.axis_size("row")
    return pl.pallas_call(
        functools.partial(send_kernel, doubled),
        grid_spec=pltpu.PrefetchScalarGridSpec(
            num_scalar_prefetch=1,
            grid=(frames,),
            in_specs=specs,
            out_specs=pl.BlockSpec((1, rows, height, D), lambda i, s: (i, 0, 0, 0)),
        ),
        out_shape=jax.ShapeDtypeStruct((frames, rows, height, D), jnp.bfloat16),
        compiler_params=vmem_params(60),
        cost_estimate=pl.CostEstimate(flops=flops, bytes_accessed=20 * MIB, transcendentals=0),
        name=name,
    )(numbers, *operands)


def keep_sums(numbers, groups, came, name, by_frame):
    pairs = [pair for group in groups for pair in group]
    specs, operands, doubled, height, flops = weight_specs(pairs, False)
    frames, rows = lax.axis_size("frame") // 2, lax.axis_size("row")
    specs += [pl.BlockSpec((1,) + item.shape[1:], lambda i, s: (i, 0, 0, 0)) for item in came]
    if by_frame:
        kernel = keep_frame_kernel
        shape = (frames // 2, rows, height, D)
        out_spec = pl.BlockSpec((1,) + shape[1:], lambda i, s: (i // 2, 0, 0, 0))
    else:
        kernel = keep_kernel
        shape = (frames, rows // 2, height, D // 2)
        out_spec = pl.BlockSpec((1,) + shape[1:], lambda i, s: (i, 0, 0, 0))
    each = 1 if by_frame else 2
    outs = pl.pallas_call(
        functools.partial(kernel, doubled, tuple(len(group) for group in groups)),
        grid_spec=pltpu.PrefetchScalarGridSpec(
            num_scalar_prefetch=1, grid=(frames,), in_specs=specs, out_specs=[out_spec] * (2 * each)
        ),
        out_shape=[jax.ShapeDtypeStruct(shape, jnp.float32)] * each
        + [jax.ShapeDtypeStruct(shape, jnp.bfloat16)] * each,
        compiler_params=vmem_params(60),
        cost_estimate=pl.CostEstimate(flops=flops, bytes_accessed=40 * MIB, transcendentals=0),
        name=name,
    )(numbers, *operands, *came)
    return list(outs[:each]), list(outs[each:])


def newton_kernel(rows, unroll, pieces, *refs):
    x_refs, out_ref = refs[:pieces], refs[pieces]
    a_ref, t_ref, q_ref, eye_ref, ah, al, nh, th, tl, qh, ql, num_ref = refs[pieces + 1 :]
    width = a_ref.shape[0]
    steps = width // rows
    a_at, m_at, t_at, shift_at, sum_at = 0, 1, 2, 3, 8

    def block(index):
        return pl.ds(pl.multiple_of(index * rows, rows), rows)

    def each(make):
        def one(index, carry):
            make(index)
            return carry

        lax.fori_loop(0, steps, one, 0, unroll=unroll)

    def mean():
        total = num_ref[sum_at]
        for index in range(1, steps):
            total += num_ref[sum_at + index]
        return total * (1.0 / width)

    eye_ref[...] = jnp.where(
        lax.broadcasted_iota(jnp.int32, (rows, rows), 0) == lax.broadcasted_iota(jnp.int32, (rows, rows), 1),
        1.0,
        0.0,
    )
    squares = 0.0
    for index in range(steps):
        columns = slice(index * rows, (index + 1) * rows)
        value = sum(dot_tn(ref[:, columns], ref[:, index * rows :]) for ref in x_refs)
        t_ref[columns, index * rows :] = value
        for other in range(index + 1, steps):
            there = slice(other * rows, (other + 1) * rows)
            t_ref[there, columns] = t_ref[columns, there].T
        squares += jnp.sum(value[:, :rows] * eye_ref[...])
    inverse = 1.0 / (jnp.sqrt(jnp.full((1, 1), squares, jnp.float32)) + 1e-07)
    scale = jnp.sum(inverse)
    scale = scale * scale
    num_ref[a_at] = squares * scale * (1.0 / width)

    def chunks(index):
        for chunk in range(steps):
            yield chunk, slice(chunk * rows, (chunk + 1) * rows), jnp.where(index == chunk, 1.0, 0.0)

    def first_split(index):
        at = block(index)
        total = 0.0
        for _, cut, here in chunks(index):
            value = t_ref[at, cut] * scale - (here * num_ref[a_at]) * eye_ref[...]
            a_ref[at, cut] = value
            ah[at, cut], al[at, cut] = split_two(value)
            total += jnp.sum(value * value)
        num_ref[sum_at + index] = total

    each(first_split)

    for number in range(5):
        two = number < 2
        shift = num_ref[a_at]
        fix = newton_three * mean()
        num_ref[m_at] = newton_one + newton_two * shift + newton_three * shift * shift + fix
        slope = newton_two + 2.0 * newton_three * shift

        def make_n(index):
            at = block(index)
            total = 0.0
            for _, cut, here in chunks(index):
                value = newton_three * dot_low(ah[at, :], ah[:, cut])
                value += slope * a_ref[at, cut] - (here * fix) * eye_ref[...]
                nh[at, cut] = value.astype(jnp.bfloat16)
                total += jnp.sum(value * a_ref[at, cut])
            num_ref[sum_at + index] = total

        each(make_n)
        much = num_ref[m_at]
        keep_low = number < 4 and number >= 2
        if number == 0:

            def first_q(index):
                at = block(index)
                for _, cut, here in chunks(index):
                    value = nh[at, cut].astype(jnp.float32) + (here * much) * eye_ref[...]
                    q_ref[at, cut] = value
                    qh[at, cut] = value.astype(jnp.bfloat16)

            each(first_q)
        else:

            def next_q(index):
                at = block(index)
                high = qh[at, :]
                rest = ql[at, :] if number >= 3 else None
                for _, cut, _ in chunks(index):
                    value = much * q_ref[at, cut] + dot_low(high, nh[:, cut])
                    if number >= 3:
                        value += dot_low(rest, nh[:, cut])
                    t_ref[at, cut] = value
                for _, cut, _ in chunks(index):
                    value = t_ref[at, cut]
                    first, second = split_two(value)
                    qh[at, cut] = first
                    if number >= 2:
                        ql[at, cut] = second
                    if number < 4:
                        q_ref[at, cut] = value

            each(next_q)
        if number == 4:
            break
        fix_t = mean()
        num_ref[t_at] = shift * much + fix_t

        def make_t(index):
            at = block(index)
            total = 0.0
            for _, cut, here in chunks(index):
                value = dot_low(ah[at, :], nh[:, cut])
                if two:
                    value += dot_low(al[at, :], nh[:, cut])
                near = nh[at, cut].astype(jnp.float32)
                value += shift * near + much * a_ref[at, cut] - (here * fix_t) * eye_ref[...]
                t_ref[at, cut] = value
                if two:
                    th[at, cut], tl[at, cut] = split_two(value)
                else:
                    th[at, cut] = value.astype(jnp.bfloat16)
                total += jnp.sum(value * near)
            num_ref[sum_at + index] = total

        each(make_t)
        fix_a = mean()
        t_shift = num_ref[t_at]
        num_ref[a_at] = t_shift * much + fix_a

        def make_a(index):
            at = block(index)
            total = 0.0
            for _, cut, here in chunks(index):
                value = dot_low(nh[at, :], th[:, cut])
                if two:
                    value += dot_low(nh[at, :], tl[:, cut])
                near = nh[at, cut].astype(jnp.float32)
                value += t_shift * near + much * t_ref[at, cut] - (here * fix_a) * eye_ref[...]
                a_ref[at, cut] = value
                if number == 0:
                    ah[at, cut], al[at, cut] = split_two(value)
                else:
                    ah[at, cut] = value.astype(jnp.bfloat16)
                total += jnp.sum(value * value)
            num_ref[sum_at + index] = total

        each(make_a)

    half = out_ref.shape[0] // 2
    for side in range(2):
        mine = x_refs[side][0:half, :]
        out_ref[side * half : (side + 1) * half, :] = (
            (dot_low(mine, qh[...]) + dot_low(mine, ql[...])) * inverse
        ).astype(out_ref.dtype)


def newton(grads, mine_rows, rows=256, unroll=4):
    width = grads[0].shape[1]
    pieces = len(grads)
    low = pltpu.VMEM((width, width), jnp.bfloat16)
    full = pltpu.VMEM((width, width), jnp.float32)
    vmem = pl.BlockSpec(memory_space=pltpu.VMEM)
    return pl.pallas_call(
        functools.partial(newton_kernel, rows, unroll, pieces),
        out_shape=jax.ShapeDtypeStruct((mine_rows, width), jnp.bfloat16),
        in_specs=[vmem] * pieces,
        out_specs=vmem,
        scratch_shapes=[full] * 3
        + [pltpu.VMEM((rows, rows), jnp.float32)]
        + [low] * 7
        + [pltpu.SMEM((16,), jnp.float32)],
        compiler_params=vmem_params(60),
        cost_estimate=pl.CostEstimate(flops=60 * 10**9, bytes_accessed=20 * 10**6, transcendentals=0),
        name="newton",
    )(*grads)


def frame_sums_kernel(count, *refs):
    out_ref = refs[-1]
    ones, twos = refs[:count], refs[count : 2 * count]
    steps, _, frames, _ = ones[0].shape
    at = 0
    for clip in range(count):
        for step in range(steps):
            rows = slice(at, at + frames)
            for index in range(2):
                out_ref[rows, index * D : (index + 1) * D] = ones[clip][step, index]
            for index in range(4):
                out_ref[rows, (index + 2) * D : (index + 3) * D] = twos[clip][step, index]
            at += frames


def frame_sums(ones, twos):
    steps, _, frames, _ = ones[0].shape
    return pl.pallas_call(
        functools.partial(frame_sums_kernel, len(ones)),
        out_shape=jax.ShapeDtypeStruct((len(ones) * steps * frames, 6 * D), jnp.float32),
        in_specs=[pl.BlockSpec(memory_space=pltpu.VMEM)] * (2 * len(ones)),
        out_specs=pl.BlockSpec(memory_space=pltpu.VMEM),
        compiler_params=vmem_params(60),
        cost_estimate=pl.CostEstimate(flops=0, bytes_accessed=MIB, transcendentals=0),
        name="frame_sums",
    )(*ones, *twos)


def swap(slots):
    size = lax.axis_size("row")
    out = [slots[0]]
    for slot in range(1, size):
        out.append(lax.ppermute(slots[slot], "row", [(index, index ^ slot) for index in range(size)]))
    return out


def frame_swap(slots):
    size = lax.axis_size("frame")
    out = [slots[0]]
    for slot in range(1, size // 2):
        pairs = [(index, index ^ (2 * slot)) for index in range(size)]
        out.append(lax.ppermute(slots[slot], "frame", pairs))
    return out


def plane_steps(members):
    size = lax.axis_size("row")
    row_bits = size.bit_length() - 1
    groups = lax.axis_size("frame") // 2
    group_index = lax.axis_index("frame") >> 1
    height = max(item.shape[0] for item in members)
    slab = jnp.stack([jnp.pad(item, ((0, height - item.shape[0]), (0, 0))) for item in members])
    slots = [
        lax.dynamic_index_in_dim(slab, (group_index ^ slot) & 3, 0, keepdims=False) for slot in range(groups)
    ]
    hold = yield slots
    slots = frame_swap(slots)
    slots[0] = held(slots[0], *hold)
    mine = jnp.concatenate(slots, axis=0)
    cut = mine.shape[0] // 2
    grown = [mine[:cut], mine[cut:]]
    for step in range(row_bits):
        hold = yield grown
        for side in range(2):
            bit = step if side == 0 else row_bits - 1 - step
            pairs = [(index, index ^ (1 << bit)) for index in range(size)]
            came = lax.ppermute(grown[side], "row", pairs)
            grown[side] = jnp.concatenate([held(grown[side], *hold), came], axis=0)
    frame_size = lax.axis_size("frame")
    pairs = [(index, index ^ 1) for index in range(frame_size)]
    yield (*grown, *(lax.ppermute(item, "frame", pairs) for item in grown))


def per_device(
    tokens,
    cotangent,
    noise_levels,
    frame_times,
    step_count,
    qkv_master,
    qkv_momentum,
    out_master,
    out_momentum,
    up_master,
    up_momentum,
    down_master,
    down_momentum,
    ada_master,
    ada_first,
    ada_second,
    table_master,
    table_first,
    table_second,
    bias_master,
    bias_first,
    bias_second,
):
    low_type = jnp.bfloat16
    full_type = jnp.float32
    clip_count, frames, rows_dev, columns, model_width = tokens.shape
    seq_local = frames * rows_dev * columns
    row_devices = lax.axis_size("row")
    token_total = clip_count * seq_local
    frame_total = clip_count * frames
    shape_five = (clip_count, frames, rows_dev, columns, model_width)
    both = ("frame", "row")
    frame_devices = lax.axis_size("frame")
    device_total = frame_devices * row_devices
    device_index = lax.axis_index("frame") * row_devices + lax.axis_index("row")
    heights = (qkv_master.shape[1], out_master.shape[0], up_master.shape[1], down_master.shape[0])
    w_qkv = lax.all_gather(qkv_master.T.astype(low_type), both, axis=0, tiled=True)
    shards = jnp.concatenate([down_master, up_master.T, out_master], axis=0).astype(low_type)
    gathered = lax.all_gather(shards, both, axis=0)
    if heights[1] % 16 == 0:

        def from_slab(first, height):
            return gathered, pl.BlockSpec(
                (device_total, height, model_width),
                lambda *_: (0, first // height, 0),
                pipeline_mode=pl.Buffered(1),
            )

    else:

        def from_slab(first, height):
            part = gathered[:, first : first + height].reshape(-1, model_width // row_devices, model_width)
            return part, whole_spec(part)

    w_down = from_slab(0, heights[3])
    w_up = from_slab(heights[3], heights[2])
    w_out = from_slab(heights[3] + heights[2], heights[1])
    level_flat = noise_levels.reshape(frame_total)
    levels_all = lax.all_gather(level_flat, "frame", axis=0, tiled=True)
    frames_all = frame_devices * frame_total
    frames_each = frames_all // device_total
    level_rows = table_master.shape[0]
    my_levels = device_index * level_rows + jnp.arange(level_rows, dtype=jnp.int32)
    level_hot = levels_all[:, None] == my_levels[None, :]
    found = jnp.dot(
        level_hot.astype(low_type),
        lax.optimization_barrier(table_master.astype(low_type)),
        preferred_element_type=full_type,
    )

    def to_all(value):
        return lax.all_to_all(value, both, split_axis=0, concat_axis=0, tiled=True)

    def from_all(value):
        return to_all(jnp.broadcast_to(value[None], (device_total,) + value.shape))

    embedded_mine = jnp.sum(
        to_all(found.reshape(device_total, frames_each, model_width)), axis=0
    )
    embedded_all = from_all(embedded_mine).reshape(frames_all, model_width)
    cond_all = jax.nn.silu(embedded_all).astype(low_type)
    ada_low = lax.optimization_barrier(ada_master.astype(low_type))
    bias_low = lax.optimization_barrier(bias_master.astype(low_type))
    ada_width = ada_master.shape[1]
    mod_columns = jnp.dot(cond_all, ada_low, preferred_element_type=full_type) + bias_low.astype(full_type)
    mod_columns = mod_columns.reshape(frame_devices, 1, frame_total, ada_width)
    mod_columns = jnp.broadcast_to(
        mod_columns, (frame_devices, row_devices, frame_total, ada_width)
    ).reshape(device_total, frame_total, ada_width)
    modulation = jnp.moveaxis(to_all(mod_columns), 0, 1).reshape(frame_total, 6 * model_width)
    grid_shape = (clip_count, frames, rows_dev, columns)
    row_first = lax.axis_index("row") * rows_dev
    time_grid = jnp.broadcast_to(frame_times.astype(full_type)[:, :, None, None], grid_shape)
    row_grid = jnp.broadcast_to(
        (row_first + jnp.arange(rows_dev, dtype=jnp.int32)).astype(full_type)[None, None, :, None],
        grid_shape,
    )
    column_grid = jnp.broadcast_to(
        jnp.arange(columns, dtype=jnp.int32).astype(full_type)[None, None, None, :], grid_shape
    )
    angles = rotary_angles(time_grid, row_grid, column_grid).reshape(clip_count, seq_local, HD // 2)
    flat_angles = angles.reshape(token_total, HD // 2)
    pair_sign = jnp.tile(jnp.array([-1.0, 1.0], full_type), HD)
    cosine = jnp.tile(jnp.repeat(jnp.cos(flat_angles), 2, axis=1), (1, 2))
    sine = jnp.tile(jnp.repeat(jnp.sin(flat_angles), 2, axis=1), (1, 2)) * pair_sign
    tile_count = token_total // 256
    mod = modulation.reshape(tile_count, frame_total // tile_count, 6 * model_width)
    me = lax.axis_index("row").astype(jnp.int32).reshape(1)
    tokens_flat = tokens.reshape(clip_count, seq_local, model_width)
    cotangent_flat = cotangent.reshape(clip_count, seq_local, model_width)
    clips = range(clip_count)
    hidden_one, pieces = [], []
    for clip in clips:
        hidden, *slots = project(me, clip, tokens_flat, mod, cosine, sine, w_qkv, row_devices)
        hidden_one.append(hidden[0])
        pieces.append(swap(slots))
    attended, full, logs = [], [], []
    for clip in clips:
        slots, full_clip, log_clip = attend(pieces[clip])
        attended.append(swap(slots))
        full.append(full_clip)
        logs.append(log_clip)
    d_attended, middles = [], []
    for clip in clips:
        slots, others = middle(
            me, clip, tokens_flat, cotangent_flat, mod, w_out, w_up, w_down, attended[clip]
        )
        d_attended.append(swap(slots))
        middles.append(others)
    block_out = jnp.concatenate([item[0] for item in middles], axis=0).reshape(shape_five)
    att_low, hidden_two, activated, d_branch_two, d_up, d_branch_one, d_middle, two_sums = (
        [item[index] for item in middles] for index in range(1, 9)
    )
    early = scatter_steps(
        [[(activated, d_branch_two)], [(d_up, hidden_two), (att_low, d_branch_one)]], "early", True, []
    )

    def after(value, state):
        return [held(value[0], *state), *value[1:]]

    ready = next(early)
    d_pieces = []
    for clip in clips:
        if clip < clip_count - 1:
            slots = attend_back(pieces[clip], after(d_attended[clip], ready), full[clip], logs[clip])
            before = swap(slots)
            d_pieces.append(before)
            ready = [slots[0]]
            continue
        parts = []
        for pair in range(D // 128 // row_devices):
            slots = attend_back(pieces[clip], after(d_attended[clip], ready), full[clip], logs[clip], pair)
            parts += swap(slots)
            ready = [slots[0], *before[1:]]
        d_pieces.append(parts)
    state = []
    lasts = []
    for clip in clips:
        lasts.append(
            last(
                me, clip, tokens_flat, mod, cosine, sine, w_qkv, d_middle[clip],
                after(d_pieces[clip], state), row_devices,
            )
        )
        if clip < clip_count - 1:
            state = early.send([lasts[clip][2]])
    input_grad = jnp.concatenate([item[1] for item in lasts], axis=0).reshape(shape_five)
    one_sums = [item[2] for item in lasts]
    d_modulation = frame_sums(one_sums, two_sums)
    ada_width = ada_master.shape[1]
    mod_parts = to_all(jnp.moveaxis(d_modulation.reshape(frame_total, device_total, ada_width), 1, 0))
    late = scatter_steps(
        [[([item[0] for item in lasts], hidden_one)]],
        "late",
        False,
        [d_modulation],
        [mod_parts],
    )
    late_state = next(late)
    late_row = late.send([])
    early_sum = finished(early, early.send(late_row))
    state = late.send([])

    mod_parts = held(mod_parts, *late_state)
    mod_mine = (
        jnp.sum(mod_parts.reshape(frame_devices, row_devices, frame_total, ada_width), axis=1)
        .reshape(frames_all, ada_width)
        .astype(low_type)
    )
    g_ada = jnp.einsum("fd,fe->de", cond_all, mod_mine, preferred_element_type=full_type)
    g_bias = jnp.sum(mod_mine.astype(full_type), axis=0)
    d_cond_parts = jnp.einsum("fe,de->fd", mod_mine, ada_low, preferred_element_type=full_type)
    d_cond = to_all(d_cond_parts.reshape(device_total, frames_each, model_width))
    d_cond = jnp.sum(held(d_cond, *state) if isinstance(state, list) else d_cond, axis=0)
    g_qkv = finished(late, state)
    d_embedded_mine = jax.vjp(jax.nn.silu, embedded_mine)[1](d_cond)[0]
    d_embedded = from_all(d_embedded_mine).reshape(frames_all, model_width)
    g_table = jnp.dot(level_hot.astype(full_type).T, d_embedded, precision=highest)
    g_down = early_sum[: heights[3]]
    g_up = early_sum[heights[3] : heights[3] + heights[2]]
    g_out = early_sum[heights[3] + heights[2] :]
    muon_grads = (g_qkv, g_out, g_up, g_down)
    flipped = (True, False, True, False)

    def tall(value, member):
        return value.T if flipped[member] else value

    muon_moments = (qkv_momentum, out_momentum, up_momentum, down_momentum)
    muon_masters = (qkv_master, out_master, up_master, down_master)
    factors = (math.sqrt(3.0), 1.0, math.sqrt(FF / D), math.sqrt(FF / D))
    adam_local = jnp.sum(g_ada * g_ada) + jnp.sum(g_table * g_table) + jnp.sum(g_bias * g_bias)
    local_total = adam_local + sum((jnp.sum(item * item) for item in muon_grads))
    norm_value = jnp.sqrt(jnp.sum(from_all(jnp.full((1, 128), local_total))[:, 0, 0]))
    clip_factor = jnp.minimum(1.0, clip_limit / (norm_value + 1e-06))
    moments_new = []
    updates = []
    slot_rows = max(heights)
    for member in range(4):
        clipped = clip_factor * muon_grads[member]
        moment = momentum_decay * tall(muon_moments[member], member) + clipped
        update = (clipped + momentum_decay * moment).astype(low_type)
        moments_new.append(tall(moment, member))
        updates.append(update)
    row_steps = plane_steps(updates)
    update_rows = next(row_steps)
    while not isinstance(update_rows, tuple):
        update_rows = row_steps.send([])
    groups = frame_devices // 2
    group_index = lax.axis_index("frame") >> 1
    ortho_rows = newton(update_rows, groups * slot_rows).reshape(groups, slot_rows, model_width)
    ortho_slots = jnp.stack(frame_swap([ortho_rows[slot] for slot in range(groups)]))
    ortho_mine = [
        lax.dynamic_index_in_dim(ortho_slots, (group_index & 3) ^ member, 0, keepdims=False)
        for member in range(4)
    ]
    blocks = [tall(ortho_mine[member][: heights[member]].astype(full_type), member) for member in range(4)]
    masters_new = []
    for member in range(4):
        ortho = blocks[member]
        masters_new.append(
            muon_masters[member] * (1.0 - muon_rate * weight_decay)
            - muon_rate * factors[member] * ortho
        )
    step_value = step_count.astype(full_type)[0]
    ada_first_new, ada_second_new, ada_master_new = adam_update(
        g_ada, ada_first, ada_second, ada_master, 0.03, clip_factor, step_value
    )
    table_clipped = clip_factor * g_table
    table_first_new, table_second_new, table_master_new = adam_update(
        g_table, table_first, table_second, table_master, 0.5, clip_factor, step_value
    )
    bias_first_new, bias_second_new, bias_master_new = adam_update(
        g_bias, bias_first, bias_second, bias_master, 0.5, clip_factor, step_value
    )
    return (
        block_out,
        input_grad,
        norm_value.reshape(1),
        moments_new[0],
        masters_new[0],
        moments_new[1],
        masters_new[1],
        moments_new[2],
        masters_new[2],
        moments_new[3],
        masters_new[3],
        ada_first_new,
        ada_second_new,
        ada_master_new,
        table_first_new,
        table_clipped,
        table_master_new,
        bias_first_new,
        bias_second_new,
        bias_master_new,
    )


def solution(mesh):
    return jax.shard_map(
        per_device,
        mesh=mesh,
        in_specs=(
            P("frame", None, "row", None, None),
            P("frame", None, "row", None, None),
            P("frame", None),
            P("frame", None),
            P(),
            P(None, ("frame", "row")),
            P(None, ("frame", "row")),
            P(("frame", "row"), None),
            P(("frame", "row"), None),
            P(None, ("frame", "row")),
            P(None, ("frame", "row")),
            P(("frame", "row"), None),
            P(("frame", "row"), None),
            P(None, ("frame", "row")),
            P(None, ("frame", "row")),
            P(None, ("frame", "row")),
            P(("frame", "row"), None),
            P(("frame", "row"), None),
            P(("frame", "row"), None),
            P(("frame", "row")),
            P(("frame", "row")),
            P(("frame", "row")),
        ),
        out_specs=(
            P("frame", None, "row", None, None),
            P("frame", None, "row", None, None),
            P(),
            P(None, ("frame", "row")),
            P(None, ("frame", "row")),
            P(("frame", "row"), None),
            P(("frame", "row"), None),
            P(None, ("frame", "row")),
            P(None, ("frame", "row")),
            P(("frame", "row"), None),
            P(("frame", "row"), None),
            P(None, ("frame", "row")),
            P(None, ("frame", "row")),
            P(None, ("frame", "row")),
            P(("frame", "row"), None),
            P(("frame", "row"), None),
            P(("frame", "row"), None),
            P(("frame", "row")),
            P(("frame", "row")),
            P(("frame", "row")),
        ),
        check_vma=False,
    )
```
